32 devices in a mesh: dp: 4 (over x, core), ctx: 2 (over y), tensor: 4 (over z).
Axes of the slice: x: 2, y: 2, z: 4, core: 2. Of those that a mesh axis runs over, the one named last changes fastest.
Arguments:
- block_input: bfloat16 [4, 4096, 768], P('dp', 'ctx'), may hold values from -6 to 6
- cotangent: bfloat16 [4, 4096, 768], P('dp', 'ctx'), may hold values from -6 to 6
- norm1_gain: bfloat16 [768], P('dp'), may hold values from 0.25 to 1.75
- norm1_bias: bfloat16 [768], P('dp'), may hold values from -1.5 to 1.5
- qkv_weight: bfloat16 [768, 3, 768], P('dp', None, 'tensor'), may hold values from -0.21875 to 0.21875
- qkv_bias: bfloat16 [2, 12, 64], P(None, 'tensor', 'dp'), may hold values from -1.5 to 1.5
- rel_pos_h: bfloat16 [127, 64], P(None, 'dp'), may hold values from -0.75 to 0.75
- rel_pos_w: bfloat16 [127, 64], P(None, 'dp'), may hold values from -0.75 to 0.75
- proj_weight: bfloat16 [768, 768], P('tensor', 'dp'), may hold values from -3 to 3
- proj_bias: bfloat16 [768], P('dp'), may hold values from -1.5 to 1.5
- norm2_gain: bfloat16 [768], P('dp'), may hold values from 0.25 to 1.75
- norm2_bias: bfloat16 [768], P('dp'), may hold values from -1.5 to 1.5
- mlp_in_weight: bfloat16 [768, 3072], P('dp', 'tensor'), may hold values from -0.21875 to 0.21875
- mlp_in_bias: bfloat16 [48, 64], P('tensor', 'dp'), may hold values from -2 to 2
- mlp_out_weight: bfloat16 [3072, 768], P('tensor', 'dp'), may hold values from -0.15625 to 0.15625
- mlp_out_bias: bfloat16 [768], P('dp'), may hold values from -1.5 to 1.5
Outputs:
- block_out: bfloat16 [4, 4096, 768], P('dp', 'ctx')
- grad_input: float32 [4, 4096, 768], P('dp', 'ctx')
- grad_norm1_gain: float32 [768], P('dp')
- grad_norm1_bias: float32 [768], P('dp')
- grad_qkv_weight: float32 [768, 3, 768], P('dp', None, 'tensor')
- grad_qkv_bias: float32 [2, 12, 64], P(None, 'tensor', 'dp')
- grad_rel_pos_h: float32 [127, 64], P(None, 'dp')
- grad_rel_pos_w: float32 [127, 64], P(None, 'dp')
- grad_proj_weight: float32 [768, 768], P('tensor', 'dp')
- grad_proj_bias: float32 [768], P('dp')
- grad_norm2_gain: float32 [768], P('dp')
- grad_norm2_bias: float32 [768], P('dp')
- grad_mlp_in_weight: float32 [768, 3072], P('dp', 'tensor')
- grad_mlp_in_bias: float32 [48, 64], P('tensor', 'dp')
- grad_mlp_out_weight: float32 [3072, 768], P('tensor', 'dp')
- grad_mlp_out_bias: float32 [768], P('dp')
The draws below stay inside these ranges and needn't reach their ends.
All inputs are finite; a program needn't handle non-finite values.
Results may differ from the reference program's by a relative error of at most 0.023.
Values may be sent and summed in bfloat16 or wider, within the bound.
No kernel may reach another device: no remote copies, remote signals or barrier semaphores. Data moves between devices by JAX's collectives and lax.ppermute only.
A program may use at most 384 MiB of HBM per device.

```python
from functools import partial
import jax
import jax.numpy as jnp
from jax import lax

D = 768
HEADS = 12
HD = 64
FF = 3072
GH = 64
GW = 64
IMGS = 4
TOKENS = 4096


def block_scale(own_key, shape, split, smallest, largest):
    factor_of = 1.0
    for position, parts in split:
        steps = jax.random.uniform(jax.random.fold_in(jax.random.fold_in(own_key, 6), position), (parts,), jnp.float32, smallest / len(split), largest / len(split))
        factor_of = factor_of * jnp.repeat(jnp.exp(steps), shape[position] // parts).reshape((-1,) + (1,) * (len(shape) - 1 - position))
    return factor_of


def normal_values(rng, dims, scale, reach, split=(), kind=jnp.bfloat16):
    loudness = block_scale(rng, dims, split, -0.22, 0.18) if split else 1.0
    values = jax.random.normal(rng, dims, jnp.float32) * scale * loudness
    return jnp.minimum(jnp.maximum(values, -reach), reach).astype(kind)


def setup_inputs(seed: int = 0) -> dict:
    key_list = jax.random.split(jax.random.key(seed), 17)
    block_input = normal_values(key_list[0], (IMGS, TOKENS, D), 1.0, 6.0, ((0, 4), (1, 2)))
    cotangent = normal_values(key_list[1], (IMGS, TOKENS, D), 1.0, 6.0, ((0, 4), (1, 2)))
    norm1_gain = jnp.clip(1.0 + 0.15 * jax.random.normal(key_list[2], (D,), jnp.float32), 0.25, 1.75).astype(jnp.bfloat16)
    norm1_bias = normal_values(key_list[3], (D,), 0.3, 1.5, ((0, 4),))
    qkv_weight = normal_values(key_list[4], (D, 3, D), D ** -0.5, 0.21875, ((0, 4), (2, 4)))
    qkv_bias = normal_values(key_list[5], (2, HEADS, HD), 0.3, 1.5, ((1, 4), (2, 4)))
    rel_pos_h = normal_values(key_list[6], (2 * GH - 1, HD), 0.125, 0.75, ((1, 4),))
    rel_pos_w = normal_values(key_list[7], (2 * GW - 1, HD), 0.125, 0.75, ((1, 4),))
    proj_weight = normal_values(key_list[8], (D, D), (max(D // 192, 1)) ** -0.5, 3.0, ((0, 4), (1, 4)))
    proj_bias = normal_values(key_list[9], (D,), 0.3, 1.5, ((0, 4),))
    norm2_gain = jnp.clip(1.0 + 0.15 * jax.random.normal(key_list[10], (D,), jnp.float32), 0.25, 1.75).astype(jnp.bfloat16)
    norm2_bias = normal_values(key_list[11], (D,), 0.3, 1.5, ((0, 4),))
    mlp_in_weight = normal_values(key_list[12], (D, FF), D ** -0.5, 0.21875, ((0, 4), (1, 4)))
    mlp_in_bias = normal_values(key_list[13], (FF // 64, 64), 0.4, 2.0, ((0, 4), (1, 4)))
    mlp_out_weight = normal_values(key_list[14], (FF, D), (FF // 2) ** -0.5, 0.15625, ((0, 4), (1, 4)))
    mlp_out_bias = normal_values(key_list[15], (D,), 0.3, 1.5, ((0, 4),))
    return {"block_input": block_input, "cotangent": cotangent, "norm1_gain": norm1_gain, "norm1_bias": norm1_bias, "qkv_weight": qkv_weight, "qkv_bias": qkv_bias, "rel_pos_h": rel_pos_h, "rel_pos_w": rel_pos_w, "proj_weight": proj_weight, "proj_bias": proj_bias, "norm2_gain": norm2_gain, "norm2_bias": norm2_bias, "mlp_in_weight": mlp_in_weight, "mlp_in_bias": mlp_in_bias, "mlp_out_weight": mlp_out_weight, "mlp_out_bias": mlp_out_bias}


@jax.custom_vjp
def low(v):
    return lax.optimization_barrier(v.astype(jnp.bfloat16)).astype(jnp.float32)

@jax.custom_vjp
def low_back(v):
    return v

def low_keep(v):
    return (low(v), None)

def low_pass(kept, grad):
    return (grad,)

def back_keep(v):
    return (v, None)

def back_low(kept, grad):
    return (low(grad),)
low.defvjp(low_keep, low_pass)
low_back.defvjp(back_keep, back_low)
norm_epsilon = 1e-06

def layer_norm(values, norm_gain, norm_shift):
    center = lax.optimization_barrier(jnp.mean(values, axis=-1, keepdims=True))
    offset = values - center
    spread = lax.optimization_barrier(jnp.mean(offset * offset, axis=-1, keepdims=True))
    return offset * lax.rsqrt(spread + norm_epsilon) * norm_gain + norm_shift

def relative_tables(rel_table, extent):
    spots = jnp.arange(extent, dtype=jnp.int32)[:, None] - jnp.arange(extent, dtype=jnp.int32)[None, :] + (extent - 1)
    return rel_table[spots]

def attend_rows(key_rows, value_rows, packed):
    query_rows, near_h, far_w = packed
    row_count = query_rows.shape[0]
    scores = jnp.einsum('nhc,mhc->hnm', query_rows, key_rows, precision=lax.Precision.HIGHEST) * HD ** (-0.5)
    offset = near_h[:, :, :, None] + far_w[:, :, None, :]
    offset = jnp.transpose(offset.reshape(row_count, HEADS, GH * GW), (1, 0, 2))
    scores = low_back(scores + offset)
    row_top = lax.optimization_barrier(jnp.max(scores, axis=-1, keepdims=True))
    log_norm = row_top + jnp.log(lax.optimization_barrier(jnp.sum(jnp.exp(scores - row_top), axis=-1, keepdims=True)))
    weights = low(jnp.exp(scores - log_norm))
    return jnp.einsum('hnm,mhc->nhc', weights, value_rows, precision=lax.Precision.HIGHEST)

def image_forward(params, image):
    gain_one, shift_one, weight_qkv, bias_qkv, table_h, table_w, weight_proj, bias_proj, gain_two, shift_two, weight_in, bias_in, weight_out, bias_out = params
    token_count = GH * GW
    normed = low(layer_norm(image, gain_one, shift_one))
    projected = jnp.einsum('nd,dje->nje', normed, weight_qkv, precision=lax.Precision.HIGHEST)
    bias_flat = bias_qkv.reshape(2, D)
    query = low(low_back(projected[:, 0] + bias_flat[0]))
    key_rows = low(low_back(projected[:, 1]))
    value_rows = low(low_back(projected[:, 2] + bias_flat[1]))
    query_grid = query.reshape(GH, GW, HEADS, HD)
    near_h = jnp.einsum('iwhc,irc->iwhr', query_grid, relative_tables(table_h, GH), precision=lax.Precision.HIGHEST)
    far_w = jnp.einsum('iwhc,wsc->iwhs', query_grid, relative_tables(table_w, GW), precision=lax.Precision.HIGHEST)
    rows_each = min(512, token_count)
    blocks = token_count // rows_each
    packed = (query.reshape(blocks, rows_each, HEADS, HD), near_h.reshape(blocks, rows_each, HEADS, GH), far_w.reshape(blocks, rows_each, HEADS, GW))
    step_rows = jax.checkpoint(partial(attend_rows, key_rows.reshape(token_count, HEADS, HD), value_rows.reshape(token_count, HEADS, HD)))
    attended = lax.map(step_rows, packed)
    heads_out = low(low_back(attended.reshape(token_count, D)))
    branch = low_back(jnp.dot(heads_out, weight_proj, precision=lax.Precision.HIGHEST) + bias_proj)
    middle = image + branch
    normed_two = low(layer_norm(middle, gain_two, shift_two))
    hidden = low_back(jnp.dot(normed_two, weight_in, precision=lax.Precision.HIGHEST) + bias_in.reshape(FF))
    active = low(jax.nn.gelu(hidden, approximate=False))
    branch_two = low_back(jnp.dot(active, weight_out, precision=lax.Precision.HIGHEST) + bias_out)
    return middle + branch_two

def reference(block_input, cotangent, norm1_gain, norm1_bias, qkv_weight, qkv_bias, rel_pos_h, rel_pos_w, proj_weight, proj_bias, norm2_gain, norm2_bias, mlp_in_weight, mlp_in_bias, mlp_out_weight, mlp_out_bias):
    params = (norm1_gain.astype(jnp.float32), norm1_bias.astype(jnp.float32), qkv_weight.astype(jnp.float32), qkv_bias.astype(jnp.float32), rel_pos_h.astype(jnp.float32), rel_pos_w.astype(jnp.float32), proj_weight.astype(jnp.float32), proj_bias.astype(jnp.float32), norm2_gain.astype(jnp.float32), norm2_bias.astype(jnp.float32), mlp_in_weight.astype(jnp.float32), mlp_in_bias.astype(jnp.float32), mlp_out_weight.astype(jnp.float32), mlp_out_bias.astype(jnp.float32))

    def one_image(totals, image_pair):
        image, upstream = image_pair
        result, pull_back = jax.vjp(image_forward, params, image.astype(jnp.float32))
        grad_params, grad_image = pull_back(upstream.astype(jnp.float32))
        totals = jax.tree.map(lambda left, right: left + right, totals, grad_params)
        return (totals, (result.astype(jnp.bfloat16), grad_image))
    zeros_start = tuple((jnp.zeros(parameter.shape, jnp.float32) for parameter in params))
    totals, (block_out, grad_input) = lax.scan(one_image, zeros_start, (block_input, cotangent))
    return (block_out, grad_input, totals[0], totals[1], totals[2], totals[3], totals[4], totals[5], totals[6], totals[7], totals[8], totals[9], totals[10], totals[11], totals[12], totals[13])
```

```python
import functools

import jax
import jax.numpy as jnp
from jax import lax
from jax.experimental import pallas as pl
from jax.experimental.pallas import tpu as pltpu
from jax.sharding import PartitionSpec as P

HD = 64
GW = 64
EPS = 1e-06
f32 = jnp.float32
bf16 = jnp.bfloat16
VMEM = 56 * 2**20


def iota(shape, dim):
    return lax.broadcasted_iota(jnp.int32, shape, dim)


def dot(a, b, ca, cb):
    return lax.dot_general(a, b, (((ca,), (cb,)), ((), ())), preferred_element_type=f32)


def make_qaug(qT, tab, il0, off, R):
    bq = qT.shape[1]
    qf = jnp.concatenate([qT.astype(f32), jnp.zeros((64, bq), f32)], 0).T
    g = dot(qT, tab, 0, 0)
    lane = iota((64, 128), 1)
    used = (lane < 64 + R) | ((lane >= 96) & (lane < 96 + R))
    outs = []
    for k in range(bq // 64):
        gh = g[k * 64 : (k + 1) * 64, :128]
        gw = g[k * 64 : (k + 1) * 64, 128:]
        sh = 63 - (il0 + k) + off
        h64 = pltpu.roll(gh, lax.rem(64 - sh + 256, 128), 1)
        h96 = pltpu.roll(gh, lax.rem(96 - sh + 256, 128), 1)
        w64 = pltpu.roll(gw, 1, 1, stride=1, stride_axis=0)
        w0 = pltpu.roll(gw, 65, 1, stride=1, stride_axis=0)
        a = jnp.where(lane < 64, qf[k * 64 : (k + 1) * 64], w64)
        wl = w0 - w0.astype(bf16).astype(f32)
        hl = h96 - h96.astype(bf16).astype(f32)
        b = jnp.where(lane < 64, wl, jnp.where(lane < 96, h64, hl))
        b = jnp.where(used, b, 0.0)
        outs.append(jnp.concatenate([a, b], 1).astype(bf16))
    return jnp.concatenate(outs, 0)


def build_kaug(kT, kaug, flipped=False):
    KB = kT.shape[1]
    ck = min(512, KB)
    for c in range(KB // ck):
        kf = kT[:, c * ck : (c + 1) * ck].astype(f32) * 0.125
        kf = jnp.concatenate([kf, jnp.zeros((64, ck), f32)], 0).T
        n = iota((ck, 128), 0) + c * ck
        lane = iota((ck, 128), 1)
        col, row = n & 63, n >> 6
        spot = 127 - col if flipped else 64 + col
        a = jnp.where(lane < 64, kf, (lane == spot).astype(f32))
        b = jnp.where(lane < 64, (lane == col).astype(f32), ((lane & 31) == row).astype(f32))
        kaug[c * ck : (c + 1) * ck, :] = jnp.concatenate([a, b], 1).astype(bf16)


def build_kaugT(kT, kaugT):
    KB = kT.shape[1]
    ck = min(512, KB)
    for c in range(KB // ck):
        f = iota((64, ck), 0)
        n = iota((64, ck), 1) + c * ck
        col, row = n & 63, n >> 6
        sl = slice(c * ck, (c + 1) * ck)
        kaugT[0:64, sl] = (kT[:, sl].astype(f32) * 0.125).astype(bf16)
        oc = (f == col).astype(f32).astype(bf16)
        kaugT[64:128, sl] = oc
        kaugT[128:192, sl] = oc
        kaugT[192:256, sl] = ((f & 31) == row).astype(f32).astype(bf16)


def fwd_kernel(off_ref, qT_ref, kvT_ref, tab_ref, *rest, R, bk, first, last):
    if first:
        rest = (None, None) + rest
    oi_ref, mli_ref, o_ref, ml_ref, *rest = rest
    ob_ref = rest[0] if last else None
    kaug, vaug = rest[-2:]
    KB = kvT_ref.shape[1]
    bq = qT_ref.shape[1]
    qi = pl.program_id(1)

    @pl.when(qi == 0)
    def _():
        build_kaug(kvT_ref[0:64, :], kaug)
        vaug[0:64, :] = kvT_ref[64:128, :]
        vaug[64:80, :] = (iota((16, KB), 0) == 0).astype(f32).astype(bf16)

    qaug = make_qaug(qT_ref[...], tab_ref[:, :256], qi * (bq // 64), off_ref[0], R)
    if first:
        m = jnp.full((1, bq), -3e38, f32)
        o = jnp.zeros((80, bq), f32)
    else:
        m = mli_ref[0:1, :]
        o = jnp.concatenate([oi_ref[...], jnp.broadcast_to(mli_ref[1:2, :], (16, bq))], 0)
    for c in range(KB // bk):
        s = dot(kaug[c * bk : (c + 1) * bk, :], qaug, 1, 1)
        mn = jnp.maximum(m, jnp.max(s, axis=0, keepdims=True))
        al = jnp.exp(m - mn)
        p = jnp.exp(s - mn).astype(bf16)
        o = o * al + jnp.dot(vaug[:, c * bk : (c + 1) * bk], p, preferred_element_type=f32)
        m = mn
    l = o[64:65, :]
    o = o[:64]
    if last:
        o = o * (1.0 / l)
        m = m + jnp.log(l)
        ob_ref[...] = o.astype(bf16)
    o_ref[...] = o
    ml_ref[...] = jnp.concatenate([m, l, jnp.zeros((6, bq), f32)], 0)


def attn_fwd(off, qT, kvT, tab, state, last, R, bq=1024, bk=512):
    H, _, T = qT.shape
    KB = kvT.shape[2]
    bq, bk = min(bq, T), min(bk, KB)
    first = state is None
    qs = lambda r: pl.BlockSpec((None, r, bq), lambda h, i, o: (h, 0, i))
    ins = [
        qs(64),
        pl.BlockSpec((None, 128, KB), lambda h, i, o: (h, 0, 0)),
        pl.BlockSpec((64, 384), lambda h, i, o: (0, 0)),
    ] + ([] if first else [qs(64), qs(8)])
    outs = [qs(64), qs(8)] + ([qs(64)] if last else [])
    shapes = [jax.ShapeDtypeStruct((H, 64, T), f32), jax.ShapeDtypeStruct((H, 8, T), f32)]
    shapes += [jax.ShapeDtypeStruct((H, 64, T), bf16)] if last else []
    return pl.pallas_call(
        functools.partial(fwd_kernel, R=R, bk=bk, first=first, last=last),
        grid_spec=pltpu.PrefetchScalarGridSpec(
            num_scalar_prefetch=1,
            grid=(H, T // bq),
            in_specs=ins,
            out_specs=outs,
            scratch_shapes=[pltpu.VMEM((KB, 256), bf16), pltpu.VMEM((80, KB), bf16)],
        ),
        out_shape=shapes,
        compiler_params=pltpu.CompilerParams(vmem_limit_bytes=VMEM),
        cost_estimate=pl.CostEstimate(
            flops=2 * H * T * KB * 512, bytes_accessed=H * T * 1200, transcendentals=H * T * KB
        ),
        name="attn_fwd",
    )(off, qT, kvT, tab, *([] if first else state))


def bwd_kernel(off_ref, qT_ref, kvT_ref, tab_ref, doT_ref, o_ref, ml_ref, *rest, R, bk, first):
    if first:
        rest = (None, None) + rest
    dqi_ref, dti_ref, dq_ref, dt_ref, dkv_ref, kaug, kaugT, vaug, acc = rest
    KB = kvT_ref.shape[1]
    bq = qT_ref.shape[1]
    hi, qi = pl.program_id(0), pl.program_id(1)

    @pl.when(qi == 0)
    def _():
        build_kaug(kvT_ref[0:64, :], kaug, True)
        build_kaugT(kvT_ref[0:64, :], kaugT)
        vaug[0:64, :] = kvT_ref[64:128, :]
        vaug[64:128, :] = (iota((64, KB), 0) < 3).astype(f32).astype(bf16)
        acc[...] = jnp.zeros_like(acc)

    @pl.when((qi == 0) & (hi == 0))
    def _():
        dt_ref[...] = jnp.zeros_like(dt_ref) if first else dti_ref[...]

    qT = qT_ref[...]
    doT = doT_ref[...]
    il0 = qi * (bq // 64)
    qaug = make_qaug(qT, tab_ref[:, :256], il0, off_ref[0], R)
    dof = doT.astype(f32)
    nd = -jnp.sum(dof * o_ref[...], axis=0, keepdims=True)
    d1 = nd.astype(bf16).astype(f32)
    d2 = (nd - d1).astype(bf16).astype(f32)
    d3 = nd - d1 - d2
    rid = iota((64, bq), 0)
    ext = jnp.where(rid == 2, d3, jnp.where(rid == 3, ml_ref[0:1, :], 0.0))
    ext = jnp.where(rid == 0, d1, jnp.where(rid == 1, d2, ext))
    t = jnp.concatenate([dof, ext], 0).T
    lse = t[:, 67:68]
    doaug = t.astype(bf16)
    dq = jnp.zeros((bq, 256), f32)
    for c in range(KB // bk):
        sl = slice(c * bk, (c + 1) * bk)
        s = jnp.dot(qaug, kaugT[:, sl], preferred_element_type=f32)
        p = jnp.exp(s - lse)
        dp = jnp.dot(doaug, vaug[:, sl], preferred_element_type=f32)
        pb = p.astype(bf16)
        ds = (p * dp).astype(bf16)
        acc[64:128, sl] += jnp.dot(doT, pb, preferred_element_type=f32)
        acc[0:64, sl] += jnp.dot(qT, ds, preferred_element_type=f32)
        dq += jnp.dot(ds, kaug[sl, :], preferred_element_type=f32)
    lane = iota((64, 128), 1)
    his, los = [], []
    for k in range(bq // 64):
        a = dq[k * 64 : (k + 1) * 64, :128]
        b = dq[k * 64 : (k + 1) * 64, 128:]
        gw = pltpu.roll(jnp.where(lane >= 64, a, 0.0), 64, 1, stride=1, stride_axis=0)
        sh = off_ref[0] - (il0 + k) - 1
        gh = pltpu.roll(
            jnp.where((lane >= 64) & (lane < 64 + R), b, 0.0), lax.rem(sh + 256, 128), 1
        )
        g = jnp.concatenate([gh, gw], 1)
        h = g.astype(bf16)
        his.append(h)
        los.append((g - h.astype(f32)).astype(bf16))
    gh = jnp.concatenate(his, 0)
    gl = jnp.concatenate(los, 0)
    tab = jnp.concatenate([tab_ref[:, :128], tab_ref[:, 256:]], 1)
    dqT = dq[:, :128].T[:64] + dot(tab, gh, 1, 1) + dot(tab, gl, 1, 1)
    dq_ref[...] = dqT if first else dqT + dqi_ref[...]
    dt_ref[...] += dot(qT, gh, 1, 0) + dot(qT, gl, 1, 0)

    @pl.when(qi == pl.num_programs(1) - 1)
    def _():
        dkv_ref[0:64, :] = (acc[0:64, :] * 0.125).astype(dkv_ref.dtype)
        dkv_ref[64:128, :] = acc[64:128, :].astype(dkv_ref.dtype)


def attn_bwd(off, qT, kvT, tab, doT, o, ml, state, dt, R, bq=1024, bk=512):
    H, _, T = qT.shape
    KB = kvT.shape[2]
    bq, bk = min(bq, T), min(bk, KB)
    first = state is None
    qs = lambda r: pl.BlockSpec((None, r, bq), lambda h, i, o: (h, 0, i))
    kvs = pl.BlockSpec((None, 128, KB), lambda h, i, o: (h, 0, 0))
    ts = pl.BlockSpec((64, 256), lambda h, i, o: (0, 0))
    tabs = pl.BlockSpec((64, 384), lambda h, i, o: (0, 0))
    ins = [qs(64), kvs, tabs, qs(64), qs(64), qs(8)] + ([] if first else [qs(64), ts])
    return pl.pallas_call(
        functools.partial(bwd_kernel, R=R, bk=bk, first=first),
        grid_spec=pltpu.PrefetchScalarGridSpec(
            num_scalar_prefetch=1,
            grid=(H, T // bq),
            in_specs=ins,
            out_specs=[qs(64), ts, kvs],
            scratch_shapes=[
                pltpu.VMEM((KB, 256), bf16),
                pltpu.VMEM((256, KB), bf16),
                pltpu.VMEM((128, KB), bf16),
                pltpu.VMEM((128, KB), f32),
            ],
        ),
        out_shape=[
            jax.ShapeDtypeStruct((H, 64, T), f32),
            jax.ShapeDtypeStruct((64, 256), f32),
            jax.ShapeDtypeStruct((H, 128, KB), dt),
        ],
        compiler_params=pltpu.CompilerParams(vmem_limit_bytes=VMEM),
        cost_estimate=pl.CostEstimate(
            flops=2 * H * T * KB * 1024, bytes_accessed=H * T * 2000, transcendentals=H * T * KB
        ),
        name="attn_bwd",
    )(off, qT, kvT, tab, doT, o, ml, *([] if first else state))


def mlp1_kernel(h2_ref, g_ref, wi_ref, wo_ref, b_ref, a_ref, du_ref, dh_ref, db_ref):
    fb = wi_ref.shape[-1]
    wi = wi_ref[...].reshape(-1, fb)
    wo = wo_ref[...].reshape(-1, fb)
    u = jnp.dot(h2_ref[...], wi, preferred_element_type=f32) + b_ref[...].astype(f32)
    ga = jnp.dot(g_ref[...], wo, preferred_element_type=f32)
    cdf = 0.5 + 0.5 * lax.erf(u * 0.7071067811865476)
    a_ref[...] = (u * cdf).astype(bf16)
    slope = cdf + u * (jnp.exp(-0.5 * u * u) * 0.3989422804014327)
    du = (slope * ga).astype(bf16)
    du_ref[...] = du
    db_ref[...] = jnp.sum(du.astype(f32), axis=0, keepdims=True)
    dh = dot(du, wi, 1, 1)
    step = pl.program_id(0) * pl.num_programs(1) + pl.program_id(1)

    @pl.when(step == 0)
    def _():
        dh_ref[...] = dh

    @pl.when(step > 0)
    def _():
        dh_ref[...] += dh


def mlp1(h2, g, W, bias, ft):
    N, D = h2.shape
    nd, nt, dd, _ = W.shape
    fb = ft // 2
    full = pl.BlockSpec((N, D), lambda t, j: (0, 0))
    act = pl.BlockSpec((None, N, fb), lambda t, j: (t, 0, j))
    row = pl.BlockSpec((None, 1, fb), lambda t, j: (t, 0, j))
    return pl.pallas_call(
        mlp1_kernel,
        grid=(nt, 2),
        in_specs=[
            full,
            full,
            pl.BlockSpec((nd, None, dd, fb), lambda t, j: (0, t, 0, j)),
            pl.BlockSpec((nd, None, dd, fb), lambda t, j: (0, t, 0, 2 + j)),
            row,
        ],
        out_specs=[act, act, full, row],
        out_shape=[
            jax.ShapeDtypeStruct((nt, N, ft), bf16),
            jax.ShapeDtypeStruct((nt, N, ft), bf16),
            jax.ShapeDtypeStruct((N, D), f32),
            jax.ShapeDtypeStruct((nt, 1, ft), f32),
        ],
        compiler_params=pltpu.CompilerParams(vmem_limit_bytes=VMEM),
        cost_estimate=pl.CostEstimate(
            flops=6 * N * D * ft * nt, bytes_accessed=20 * 2**20, transcendentals=2 * N * ft * nt
        ),
        name="mlp_grad",
    )(h2, g, W, W, bias)


def mlp2_kernel(h2_ref, g_ref, da_ref, a_ref, du_ref, oT_ref, w_ref, y_ref, b_ref, gw_ref, out_ref, hT, gT, dT, acc):
    t = pl.program_id(0)
    ft = a_ref.shape[-1]

    @pl.when(t == 0)
    def _():
        hT[...] = h2_ref[...].T
        gT[...] = g_ref[...].T
        dT[...] = da_ref[...].T
        acc[...] = jnp.zeros_like(acc)

    nd, dd = gw_ref.shape[0], gw_ref.shape[1]
    a = a_ref[...]
    acc[...] += dot(a, w_ref[...].reshape(-1, ft), 1, 1)
    gw_ref[:, :, 0:ft] = (
        jnp.dot(hT[...], du_ref[...], preferred_element_type=f32).astype(bf16).reshape(nd, dd, ft)
    )
    gw_ref[:, :, ft : 2 * ft] = (
        jnp.dot(gT[...], a, preferred_element_type=f32).astype(bf16).reshape(nd, dd, ft)
    )
    gp = dot(dT[...], oT_ref[...], 1, 1).astype(bf16)
    gw_ref[:, :, 2 * ft :] = gp.reshape(nd, dd, gp.shape[-1])

    @pl.when(t == pl.num_programs(0) - 1)
    def _():
        out_ref[...] = (y_ref[...] + (acc[...] + b_ref[...].astype(f32))).astype(bf16)


def mlp2(h2, g, da, a, du, oT, W, y1, bias):
    N, D = h2.shape
    nd, nt, dd, cols = W.shape
    ft = a.shape[-1]
    kt = oT.shape[1]
    full = pl.BlockSpec((N, D), lambda t: (0, 0))
    act = pl.BlockSpec((None, N, ft), lambda t: (t, 0, 0))
    return pl.pallas_call(
        mlp2_kernel,
        grid=(nt,),
        in_specs=[
            full,
            full,
            full,
            act,
            act,
            pl.BlockSpec((None, kt, N), lambda t: (t, 0, 0)),
            pl.BlockSpec((nd, None, dd, ft), lambda t: (0, t, 0, 1)),
            full,
            pl.BlockSpec((1, D), lambda t: (0, 0)),
        ],
        out_specs=[pl.BlockSpec((nd, None, dd, cols), lambda t: (0, t, 0, 0)), full],
        out_shape=[
            jax.ShapeDtypeStruct((nd, nt, dd, cols), bf16),
            jax.ShapeDtypeStruct((N, D), bf16),
        ],
        scratch_shapes=[pltpu.VMEM((D, N), bf16)] * 3 + [pltpu.VMEM((N, D), f32)],
        compiler_params=pltpu.CompilerParams(vmem_limit_bytes=VMEM),
        cost_estimate=pl.CostEstimate(
            flops=7 * N * D * ft * nt, bytes_accessed=24 * 2**20, transcendentals=0
        ),
        name="mlp_weights",
    )(h2, g, da, a, du, oT, W, y1, bias)


def shift(value, axis, steps):
    n = lax.axis_size(axis)
    return lax.ppermute(value, axis, [(s, (s + steps) % n) for s in range(n)])


def flip(value, axis, bit):
    n = lax.axis_size(axis)
    return lax.ppermute(value, axis, [(s, s ^ bit) for s in range(n)])


def pick(value, index, dim=0):
    return lax.dynamic_index_in_dim(value, index, dim, keepdims=False)


def put(buffer, value, index):
    return lax.dynamic_update_index_in_dim(buffer, value, index, 0)


def gather_direct(value, axis):
    n = lax.axis_size(axis)
    me = lax.axis_index(axis)
    out = jnp.zeros((n,) + value.shape, value.dtype)
    out = put(out, value, me)
    for k in range(1, n):
        out = put(out, shift(value, axis, k), (me - k) % n)
    return out


def gather_dp(value):
    me = lax.axis_index("dp")
    far = flip(value, "dp", 2)
    out = jnp.zeros((4,) + value.shape, value.dtype)
    out = put(put(out, value, me), far, me ^ 2)
    out = put(out, flip(value, "dp", 1), me ^ 1)
    return put(out, flip(far, "dp", 1), me ^ 3)


def scatter_direct(value, axis):
    n = lax.axis_size(axis)
    me = lax.axis_index(axis)
    parts = [pick(value, me)]
    for k in range(1, n):
        parts.append(shift(pick(value, (me + k) % n), axis, k))
    return sum(p.astype(f32) for p in parts)


def exchange(value, axis):
    n = lax.axis_size(axis)
    me = lax.axis_index(axis)
    out = value
    for k in range(1, n):
        out = put(out, shift(pick(value, (me + k) % n), axis, k), (me - k) % n)
    return out


def scatter_dp(value):
    me = lax.axis_index("dp")
    core, x = me & 1, me >> 1
    v = value.reshape((2, 2) + value.shape[1:])
    pair = pick(v, core, 1).astype(f32) + flip(pick(v, 1 - core, 1), "dp", 1).astype(f32)
    pair = pair.astype(bf16)
    return pick(pair, x).astype(f32) + flip(pick(pair, 1 - x), "dp", 2).astype(f32)


def total_ctx(value):
    v = value.astype(bf16)
    if lax.axis_size("ctx") == 2:
        return v.astype(f32) + flip(v, "ctx", 1).astype(f32)
    return lax.psum(v.astype(f32), "ctx")


def norm_parts(x):
    c = x - jnp.mean(x, axis=-1, keepdims=True)
    r = lax.rsqrt(jnp.mean(c * c, axis=-1, keepdims=True) + EPS)
    return c * r, r


def norm_back(dh, gain, xhat, r):
    e = dh * gain
    return (
        e - jnp.mean(e, axis=-1, keepdims=True) - xhat * jnp.mean(e * xhat, axis=-1, keepdims=True)
    ) * r


def per_device(
    block_input,
    cotangent,
    norm1_gain,
    norm1_bias,
    qkv_weight,
    qkv_bias,
    rel_pos_h,
    rel_pos_w,
    proj_weight,
    proj_bias,
    norm2_gain,
    norm2_bias,
    mlp_in_weight,
    mlp_in_bias,
    mlp_out_weight,
    mlp_out_bias,
):
    nt, nc = lax.axis_size("tensor"), lax.axis_size("ctx")
    me, pos = lax.axis_index("tensor"), lax.axis_index("ctx")
    T = block_input.shape[1]
    D = block_input.shape[2]
    N = T // nt
    R = T // GW
    dd = D // 4
    H = qkv_bias.shape[1]
    E = H * HD
    x2 = block_input.reshape(T, D)
    g2 = cotangent.reshape(T, D)

    vec = jnp.concatenate(
        [
            v.reshape(-1)
            for v in (
                norm1_gain,
                norm1_bias,
                norm2_gain,
                norm2_bias,
                proj_bias,
                mlp_out_bias,
                qkv_bias,
                mlp_in_bias,
                rel_pos_h,
                rel_pos_w,
            )
        ]
    )
    vec = lax.all_gather(vec, "dp", axis=0)
    gain1, shift1, gain2, shift2, bproj, bout = (
        vec[:, i * dd : (i + 1) * dd].reshape(1, D).astype(f32) for i in range(6)
    )
    at = 6 * dd
    bq = vec[:, at : at + 2 * H * 16].reshape(4, 2, H, 16)
    bq = bq.transpose(1, 2, 0, 3).reshape(2, H, HD).astype(f32)
    at += 2 * H * 16
    nb = mlp_in_bias.size
    bin_t = vec[:, at : at + nb].reshape(4, nb // 16, 16).transpose(1, 0, 2).reshape(-1)
    at += nb
    L = rel_pos_h.shape[0]
    th = vec[:, at : at + L * 16].reshape(4, L, 16)
    tw = vec[:, at + L * 16 :].reshape(4, L, 16)
    zero = jnp.zeros((HD, 1), bf16)
    th = th.transpose(0, 2, 1).reshape(HD, L)
    tw = tw.transpose(0, 2, 1).reshape(HD, L)
    tab = jnp.concatenate([th[:, ::-1], zero, tw[:, ::-1], zero, tw, zero], 1)
    bin_all = lax.all_gather(bin_t, "tensor", axis=0)
    ft = bin_t.shape[0]

    wqkv = lax.all_gather(qkv_weight, "dp", axis=0, tiled=True)

    xf = x2.astype(f32)
    xh, _ = norm_parts(xf)
    h1 = (xh * gain1 + shift1).astype(bf16)
    wkv = wqkv[:, 1:].reshape(D, 2, H, HD).transpose(0, 2, 1, 3).reshape(D, H * 2 * HD)
    bkv = jnp.stack([jnp.zeros_like(bq[1]), bq[1]], 1).reshape(H * 2 * HD, 1)
    kvT = (dot(wkv, h1, 0, 1) + bkv).astype(bf16).reshape(H, 2 * HD, T)
    kv_far = [shift(kvT, "ctx", k) for k in range(1, nc)]
    qT = (dot(wqkv[:, 0], h1, 0, 1) + bq[0].reshape(E, 1)).astype(bf16).reshape(H, HD, T)

    pack = jnp.concatenate([mlp_in_weight, mlp_out_weight.T, proj_weight.T], 1)
    W = gather_dp(gather_direct(pack, "tensor"))
    wq_full = gather_dp(gather_direct(qkv_weight.reshape(dd, 3 * E), "tensor"))

    offs = [(((pos - k) % nc) - pos) * R for k in range(nc)]
    offs = [jnp.reshape(o, (1,)).astype(jnp.int32) for o in offs]
    state = attn_fwd(offs[0], qT, kvT, tab, None, nc == 1, R)
    for k in range(1, nc):
        state = attn_fwd(offs[k], qT, kv_far[k - 1], tab, state[:2], k == nc - 1, R)
    o32, lse, o16 = state

    oT = exchange(o16.reshape(E, nt, N).transpose(1, 0, 2), "tensor")
    wp = W[:, :, :, 2 * ft :].transpose(0, 2, 1, 3).reshape(D, nt * E)
    xm = pick(x2.reshape(nt, N, D), me).astype(f32)
    gm = pick(g2.reshape(nt, N, D), me)
    gmf = gm.astype(f32)
    y1 = xm + (dot(oT.reshape(nt * E, N), wp, 0, 1) + bproj)
    xhat2, r2 = norm_parts(y1)
    h2 = (xhat2 * gain2 + shift2).astype(bf16)
    a, du, dh2, dbin = mlp1(h2, gm, W, bin_all.reshape(nt, 1, ft), ft)
    dy1 = gmf + norm_back(dh2, gain2, xhat2, r2)
    da = dy1.astype(bf16)
    doT = dot(wp, da, 0, 1).astype(bf16).reshape(nt, E, N)
    doT = exchange(doT, "tensor").transpose(1, 0, 2).reshape(H, HD, T)
    GW2, out = mlp2(h2, gm, da, a, du, oT, W, y1, bout.astype(bf16))
    block_out = gather_direct(out, "tensor").reshape(1, T, D)

    dstate = None
    far = []
    for k in range(1, nc):
        dq, dtab, dkv = attn_bwd(offs[k], qT, kv_far[k - 1], tab, doT, o32, lse, dstate, bf16, R)
        dstate = (dq, dtab)
        far.append(shift(dkv, "ctx", -k))
    dq, dtab, dkv = attn_bwd(offs[0], qT, kvT, tab, doT, o32, lse, dstate, f32, R)
    for f in far:
        dkv = dkv + f.astype(f32)
    dqkv = jnp.concatenate([dq, dkv], 1).astype(bf16)
    dall = exchange(dqkv.reshape(H * 3 * HD, nt, N).transpose(1, 0, 2), "tensor")

    wq = wq_full.reshape(4, nt, dd, 3, H, HD).transpose(0, 2, 1, 4, 3, 5).reshape(D, nt * 3 * E)
    dh1 = dot(dall.reshape(nt * 3 * E, N), wq, 0, 1)
    xhat1, r1 = norm_parts(xm)
    gin = (dy1 + norm_back(dh1, gain1, xhat1, r1)).astype(bf16)
    grad_input = gather_direct(gin, "tensor").reshape(1, T, D).astype(f32)

    gmine = scatter_direct(scatter_dp(GW2).astype(bf16), "tensor")
    gmine = total_ctx(gmine)
    g_in = gmine[:, :ft]
    g_out = gmine[:, ft : 2 * ft].T
    g_proj = gmine[:, 2 * ft :].T
    gq = dot(h1, dqkv.reshape(H * 3 * HD, T), 0, 1).astype(bf16)
    gq = total_ctx(scatter_dp(gq.reshape(4, dd, H * 3 * HD)))
    g_qkv = gq.reshape(dd, H, 3, HD).transpose(0, 2, 1, 3).reshape(dd, 3, E)

    dqf = dqkv.astype(f32)
    bsum = jnp.sum(dqf, axis=2).reshape(H, 3, HD)
    gbq = jnp.stack([bsum[:, 0], bsum[:, 2]])
    gbq = lax.dynamic_update_index_in_dim(jnp.zeros((2, nt, H, HD), f32), gbq, me, 1)
    flat = jnp.concatenate(
        [
            v.reshape(-1)
            for v in (
                jnp.sum(dh2 * xhat2, 0),
                jnp.sum(dh2, 0),
                jnp.sum(da.astype(f32), 0),
                jnp.sum(gmf, 0),
                dbin,
                gbq,
                dtab,
                jnp.sum(dh1 * xhat1, 0),
                jnp.sum(dh1, 0),
            )
        ]
    )
    flat = lax.psum(flat, ("dp", "ctx", "tensor"))
    dp = lax.axis_index("dp")
    gb2, gs2, gbp, gbo = (pick(flat[i * D : (i + 1) * D].reshape(4, dd), dp) for i in range(4))
    at = 4 * D
    gbin = flat[at : at + nt * ft].reshape(nt, ft // HD, 4, 16)
    gbin = pick(pick(gbin, me), dp, 1)
    at += nt * ft
    gbq = pick(pick(flat[at : at + 2 * nt * E].reshape(2, nt, H, 4, 16), me, 1), dp, 2)
    at += 2 * nt * E
    gtab = pick(flat[at : at + HD * 256].reshape(4, 16, 2, 128), dp)[:, :, :L]
    at += HD * 256
    gg1, gs1 = (pick(flat[at + i * D : at + (i + 1) * D].reshape(4, dd), dp) for i in range(2))
    return (
        block_out,
        grad_input,
        gg1,
        gs1,
        g_qkv,
        gbq,
        gtab[:, 0, ::-1].T,
        gtab[:, 1].T,
        g_proj,
        gbp,
        gb2,
        gs2,
        g_in,
        gbin,
        g_out,
        gbo,
    )


def solution(mesh):
    placed = (
        P("dp", "ctx", None),
        P("dp", "ctx", None),
        P("dp"),
        P("dp"),
        P("dp", None, "tensor"),
        P(None, "tensor", "dp"),
        P(None, "dp"),
        P(None, "dp"),
        P("tensor", "dp"),
        P("dp"),
        P("dp"),
        P("dp"),
        P("dp", "tensor"),
        P("tensor", "dp"),
        P("tensor", "dp"),
        P("dp"),
    )
    return jax.shard_map(
        per_device,
        mesh=mesh,
        in_specs=placed,
        out_specs=(placed[0], placed[0]) + placed[2:],
        check_vma=False,
    )
```

```python
import functools

import jax
import jax.numpy as jnp
from jax import lax
from jax.experimental import pallas as pl
from jax.experimental.pallas import tpu as pltpu
from jax.sharding import PartitionSpec as P

HD = 64
GW = 64
EPS = 1e-06
f32 = jnp.float32
bf16 = jnp.bfloat16
VMEM = 56 * 2**20


def iota(shape, dim):
    return lax.broadcasted_iota(jnp.int32, shape, dim)


def dot(a, b, ca, cb):
    return lax.dot_general(a, b, (((ca,), (cb,)), ((), ())), preferred_element_type=f32)


def make_qaug(qT, tab, il0, off, R):
    bq = qT.shape[1]
    qf = jnp.concatenate([qT.astype(f32), jnp.zeros((64, bq), f32)], 0).T
    g = dot(qT, tab, 0, 0)
    lane = iota((64, 128), 1)
    used = (lane < 64 + R) | ((lane >= 96) & (lane < 96 + R))
    outs = []
    for k in range(bq // 64):
        gh = g[k * 64 : (k + 1) * 64, :128]
        gw = g[k * 64 : (k + 1) * 64, 128:]
        sh = 63 - (il0 + k) + off
        h64 = pltpu.roll(gh, lax.rem(64 - sh + 256, 128), 1)
        h96 = pltpu.roll(gh, lax.rem(96 - sh + 256, 128), 1)
        w64 = pltpu.roll(gw, 1, 1, stride=1, stride_axis=0)
        w0 = pltpu.roll(gw, 65, 1, stride=1, stride_axis=0)
        a = jnp.where(lane < 64, qf[k * 64 : (k + 1) * 64], w64)
        wl = w0 - w0.astype(bf16).astype(f32)
        hl = h96 - h96.astype(bf16).astype(f32)
        b = jnp.where(lane < 64, wl, jnp.where(lane < 96, h64, hl))
        b = jnp.where(used, b, 0.0)
        outs.append(jnp.concatenate([a, b], 1).astype(bf16))
    return jnp.concatenate(outs, 0)


def build_kaug(kT, kaug, flipped=False):
    KB = kT.shape[1]
    ck = min(512, KB)
    for c in range(KB // ck):
        kf = kT[:, c * ck : (c + 1) * ck].astype(f32) * 0.125
        kf = jnp.concatenate([kf, jnp.zeros((64, ck), f32)], 0).T
        n = iota((ck, 128), 0) + c * ck
        lane = iota((ck, 128), 1)
        col, row = n & 63, n >> 6
        spot = 127 - col if flipped else 64 + col
        a = jnp.where(lane < 64, kf, (lane == spot).astype(f32))
        b = jnp.where(lane < 64, (lane == col).astype(f32), ((lane & 31) == row).astype(f32))
        kaug[c * ck : (c + 1) * ck, :] = jnp.concatenate([a, b], 1).astype(bf16)


def build_kaugT(kT, kaugT):
    KB = kT.shape[1]
    ck = min(512, KB)
    for c in range(KB // ck):
        f = iota((64, ck), 0)
        n = iota((64, ck), 1) + c * ck
        col, row = n & 63, n >> 6
        sl = slice(c * ck, (c + 1) * ck)
        kaugT[0:64, sl] = (kT[:, sl].astype(f32) * 0.125).astype(bf16)
        oc = (f == col).astype(f32).astype(bf16)
        kaugT[64:128, sl] = oc
        kaugT[128:192, sl] = oc
        kaugT[192:256, sl] = ((f & 31) == row).astype(f32).astype(bf16)


def fwd_kernel(sc_ref, qT_ref, kvT_ref, tab_ref, *rest, R, bk, first, last, nt):
    if first:
        rest = (None, None) + rest
    oi_ref, mli_ref, o_ref, ml_ref, *rest = rest
    KB = kvT_ref.shape[1]
    bq = qT_ref.shape[1]
    qi = pl.program_id(1)
    if last:
        kaug, vaug, och = rest[-3:]
    else:
        kaug, vaug = rest[-2:]

    @pl.when(qi == 0)
    def _():
        build_kaug(kvT_ref[0:64, :], kaug)
        vaug[0:64, :] = kvT_ref[64:128, :]
        vaug[64:80, :] = (iota((16, KB), 0) == 0).astype(f32).astype(bf16)

    qaug = make_qaug(qT_ref[...], tab_ref[:, :256], qi * (bq // 64), sc_ref[0], R)
    if first:
        m = jnp.full((1, bq), -3e38, f32)
        o = jnp.zeros((80, bq), f32)
    else:
        m = mli_ref[0:1, :]
        o = jnp.concatenate([oi_ref[...], jnp.broadcast_to(mli_ref[1:2, :], (16, bq))], 0)
    for c in range(KB // bk):
        s = dot(kaug[c * bk : (c + 1) * bk, :], qaug, 1, 1)
        mn = jnp.maximum(m, jnp.max(s, axis=0, keepdims=True))
        al = jnp.exp(m - mn)
        p = jnp.exp(s - mn).astype(bf16)
        o = o * al + jnp.dot(vaug[:, c * bk : (c + 1) * bk], p, preferred_element_type=f32)
        m = mn
    l = o[64:65, :]
    o = o[:64]
    if last:
        o = o * (1.0 / l)
        m = m + jnp.log(l)
        N = och.shape[2]
        ob = o.astype(bf16)
        for j in range(bq // N):
            och[qi * (bq // N) + j] = ob[:, j * N : (j + 1) * N]

        @pl.when(qi == pl.num_programs(1) - 1)
        def _():
            for k in range(nt):
                rest[k][...] = och[lax.rem(sc_ref[1] + k, nt)]

    o_ref[...] = o
    ml_ref[...] = jnp.concatenate([m, l, jnp.zeros((6, bq), f32)], 0)


def attn_fwd(sc, qT, kvT, tab, state, last, R, nt, bq=1024, bk=512):
    H, _, T = qT.shape
    KB = kvT.shape[2]
    N = T // nt
    bq, bk = min(bq, T), min(bk, KB)
    first = state is None
    qs = lambda r: pl.BlockSpec((None, r, bq), lambda h, i, o: (h, 0, i))
    ins = [
        qs(64),
        pl.BlockSpec((None, 128, KB), lambda h, i, o: (h, 0, 0)),
        pl.BlockSpec((64, 384), lambda h, i, o: (0, 0)),
    ] + ([] if first else [qs(64), qs(8)])
    outs = [qs(64), qs(8)]
    shapes = [jax.ShapeDtypeStruct((H, 64, T), f32), jax.ShapeDtypeStruct((H, 8, T), f32)]
    scratch = [pltpu.VMEM((KB, 256), bf16), pltpu.VMEM((80, KB), bf16)]
    if last:
        outs += [pl.BlockSpec((64, N), lambda h, i, o: (h, 0))] * nt
        shapes += [jax.ShapeDtypeStruct((H * 64, N), bf16)] * nt
        scratch += [pltpu.VMEM((nt, 64, N), bf16)]
    return pl.pallas_call(
        functools.partial(fwd_kernel, R=R, bk=bk, first=first, last=last, nt=nt),
        grid_spec=pltpu.PrefetchScalarGridSpec(
            num_scalar_prefetch=1,
            grid=(H, T // bq),
            in_specs=ins,
            out_specs=outs,
            scratch_shapes=scratch,
        ),
        out_shape=shapes,
        compiler_params=pltpu.CompilerParams(vmem_limit_bytes=VMEM),
        cost_estimate=pl.CostEstimate(
            flops=2 * H * T * KB * 512, bytes_accessed=H * T * 1200, transcendentals=H * T * KB
        ),
        name="attn_fwd",
    )(sc, qT, kvT, tab, *([] if first else state))


def bwd_kernel(sc_ref, qT_ref, kvT_ref, tab_ref, *rest, R, bk, first, last, nt):
    do_refs, rest = rest[:nt], rest[nt:]
    o_ref, ml_ref, *rest = rest
    dqi_ref = dti_ref = dki_ref = None
    if not first:
        dqi_ref, dti_ref, *rest = rest
    if last:
        dki_ref, *rest = rest
        dx_refs, rest = rest[:nt], rest[nt:]
        dt_ref, kaug, kaugT, vaug, acc, dch, fin = rest
    else:
        dq_ref, dkv_ref, dt_ref, kaug, kaugT, vaug, acc, dch = rest
    KB = kvT_ref.shape[1]
    bq = qT_ref.shape[1]
    N = dch.shape[2]
    per = bq // N
    qi = pl.program_id(0)

    @pl.when(qi == 0)
    def _():
        build_kaug(kvT_ref[0:64, :], kaug, True)
        build_kaugT(kvT_ref[0:64, :], kaugT)
        vaug[0:64, :] = kvT_ref[64:128, :]
        vaug[64:128, :] = (iota((64, KB), 0) < 3).astype(f32).astype(bf16)
        if last:
            acc[0:64, :] = dki_ref[0:64, :].astype(f32) * 8.0
            acc[64:128, :] = dki_ref[64:128, :].astype(f32)
        else:
            acc[...] = jnp.zeros_like(acc)
        for k in range(nt):
            dch[lax.rem(sc_ref[1] + k, nt)] = do_refs[k][...]
        dt_ref[...] = jnp.zeros_like(dt_ref) if first else dti_ref[...]

    qT = qT_ref[...]
    doT = jnp.concatenate([dch[qi * per + j] for j in range(per)], 1)
    il0 = qi * (bq // 64)
    off = sc_ref[0]
    qaug = make_qaug(qT, tab_ref[:, :256], il0, off, R)
    dof = doT.astype(f32)
    nd = -jnp.sum(dof * o_ref[...], axis=0, keepdims=True)
    d1 = nd.astype(bf16).astype(f32)
    d2 = (nd - d1).astype(bf16).astype(f32)
    d3 = nd - d1 - d2
    rid = iota((64, bq), 0)
    ext = jnp.where(rid == 2, d3, jnp.where(rid == 3, ml_ref[0:1, :], 0.0))
    ext = jnp.where(rid == 0, d1, jnp.where(rid == 1, d2, ext))
    t = jnp.concatenate([dof, ext], 0).T
    lse = t[:, 67:68]
    doaug = t.astype(bf16)
    dq = jnp.zeros((bq, 256), f32)
    for c in range(KB // bk):
        sl = slice(c * bk, (c + 1) * bk)
        s = jnp.dot(qaug, kaugT[:, sl], preferred_element_type=f32)
        p = jnp.exp(s - lse)
        dp = jnp.dot(doaug, vaug[:, sl], preferred_element_type=f32)
        pb = p.astype(bf16)
        ds = (p * dp).astype(bf16)
        acc[64:128, sl] += jnp.dot(doT, pb, preferred_element_type=f32)
        acc[0:64, sl] += jnp.dot(qT, ds, preferred_element_type=f32)
        dq += jnp.dot(ds, kaug[sl, :], preferred_element_type=f32)
    lane = iota((64, 128), 1)
    his, los = [], []
    for k in range(bq // 64):
        a = dq[k * 64 : (k + 1) * 64, :128]
        b = dq[k * 64 : (k + 1) * 64, 128:]
        gw = pltpu.roll(jnp.where(lane >= 64, a, 0.0), 64, 1, stride=1, stride_axis=0)
        sh = off - (il0 + k) - 1
        gh = pltpu.roll(
            jnp.where((lane >= 64) & (lane < 64 + R), b, 0.0), lax.rem(sh + 256, 128), 1
        )
        g = jnp.concatenate([gh, gw], 1)
        h = g.astype(bf16)
        his.append(h)
        los.append((g - h.astype(f32)).astype(bf16))
    gh = jnp.concatenate(his, 0)
    gl = jnp.concatenate(los, 0)
    tab = jnp.concatenate([tab_ref[:, :128], tab_ref[:, 256:]], 1)
    dqT = dq[:, :128].T[:64] + dot(tab, gh, 1, 1) + dot(tab, gl, 1, 1)
    if not first:
        dqT = dqT + dqi_ref[...]
    dt_ref[...] += dot(qT, gh, 1, 0) + dot(qT, gl, 1, 0)
    if last:
        dqb = dqT.astype(bf16)
        for j in range(per):
            fin[qi * per + j, 0:64, :] = dqb[:, j * N : (j + 1) * N]
    else:
        dq_ref[...] = dqT

    @pl.when(qi == pl.num_programs(0) - 1)
    def _():
        if last:
            for j in range(nt):
                fin[j, 64:128, :] = (acc[0:64, j * N : (j + 1) * N] * 0.125).astype(bf16)
                fin[j, 128:192, :] = acc[64:128, j * N : (j + 1) * N].astype(bf16)
            for k in range(nt):
                dx_refs[k][...] = fin[lax.rem(sc_ref[1] + k, nt)]
        else:
            dkv_ref[0:64, :] = (acc[0:64, :] * 0.125).astype(bf16)
            dkv_ref[64:128, :] = acc[64:128, :].astype(bf16)


def attn_bwd(sc, h, qT, kvT, tab, dos, o, ml, state, back, R, bq=1024, bk=512):
    _, _, T = qT.shape
    KB = kvT.shape[2]
    nt = len(dos)
    N = T // nt
    bq, bk = min(bq, T), min(bk, KB)
    first, last = state is None, back is not None
    qs = lambda r: pl.BlockSpec((None, r, bq), lambda i, s: (h, 0, i))
    kvs = pl.BlockSpec((None, 128, KB), lambda i, s: (h, 0, 0))
    fix = lambda shape: pl.BlockSpec(shape, lambda i, s: (0, 0))
    dqs = pl.BlockSpec((64, bq), lambda i, s: (0, i))
    ins = [qs(64), kvs, fix((64, 384))]
    ins += [pl.BlockSpec((64, N), lambda i, s: (h, 0))] * nt + [qs(64), qs(8)]
    args = [qT, kvT, tab, *dos, o, ml]
    if not first:
        ins += [dqs, fix((64, 256))]
        args += list(state)
    scratch = [
        pltpu.VMEM((KB, 256), bf16),
        pltpu.VMEM((256, KB), bf16),
        pltpu.VMEM((128, KB), bf16),
        pltpu.VMEM((128, KB), f32),
        pltpu.VMEM((nt, 64, N), bf16),
    ]
    if last:
        ins += [fix((128, KB))]
        args += [back]
        outs = [fix((192, N))] * nt
        shapes = [jax.ShapeDtypeStruct((192, N), bf16)] * nt
        scratch += [pltpu.VMEM((nt, 192, N), bf16)]
    else:
        outs = [dqs, fix((128, KB))]
        shapes = [jax.ShapeDtypeStruct((64, T), f32), jax.ShapeDtypeStruct((128, KB), bf16)]
    return pl.pallas_call(
        functools.partial(bwd_kernel, R=R, bk=bk, first=first, last=last, nt=nt),
        grid_spec=pltpu.PrefetchScalarGridSpec(
            num_scalar_prefetch=1,
            grid=(T // bq,),
            in_specs=ins,
            out_specs=outs + [fix((64, 256))],
            scratch_shapes=scratch,
        ),
        out_shape=shapes + [jax.ShapeDtypeStruct((64, 256), f32)],
        compiler_params=pltpu.CompilerParams(vmem_limit_bytes=VMEM),
        cost_estimate=pl.CostEstimate(
            flops=2 * T * KB * 1280, bytes_accessed=T * 3000, transcendentals=T * KB
        ),
        name="attn_bwd",
    )(sc, *args)


def rows_of(sc_ref, r, dd):
    return pl.ds(pl.multiple_of((sc_ref[2] ^ r) * dd, dd), dd)


def whole_spec(shape):
    return pl.BlockSpec(shape, lambda *_: (0,) * len(shape))


def norm_parts(x):
    c = x - jnp.mean(x, axis=-1, keepdims=True)
    r = lax.rsqrt(jnp.mean(c * c, axis=-1, keepdims=True) + EPS)
    return c * r, r


def norm_back(dh, gain, xhat, r):
    e = dh * gain
    return (
        e - jnp.mean(e, axis=-1, keepdims=True) - xhat * jnp.mean(e * xhat, axis=-1, keepdims=True)
    ) * r


def call(kernel, sc, grid, ins, args, outs, shapes, scratch, name, flops, nbytes):
    return pl.pallas_call(
        kernel,
        grid_spec=pltpu.PrefetchScalarGridSpec(
            num_scalar_prefetch=1, grid=grid, in_specs=ins, out_specs=outs, scratch_shapes=scratch
        ),
        out_shape=[jax.ShapeDtypeStruct(s, d) for s, d in shapes],
        compiler_params=pltpu.CompilerParams(vmem_limit_bytes=VMEM),
        cost_estimate=pl.CostEstimate(flops=flops, bytes_accessed=nbytes, transcendentals=0),
        name=name,
    )(sc, *args)


def pack_kernel(sc_ref, rh, rw, n1g, n1b, n2g, n2b, pb, ob, qb, mb, out):
    L = rh.shape[0]
    t, l = iota((L, 128), 0), iota((L, 128), 1)
    back = (t == L - 1 - l).astype(f32).astype(bf16)
    same = (t == l).astype(f32).astype(bf16)
    out[...] = jnp.zeros_like(out)
    out[0:16, 0:128] = dot(rh[...], back, 0, 0).astype(bf16)
    out[0:16, 128:256] = dot(rw[...], back, 0, 0).astype(bf16)
    out[0:16, 256:384] = dot(rw[...], same, 0, 0).astype(bf16)
    dd = n1g.shape[1]
    rows = [v[...].astype(f32) for v in (n1g, n1b, n2g, n2b, pb, ob)]
    out[16:32, 0:dd] = jnp.concatenate(rows + [jnp.zeros((10, dd), f32)], 0).astype(bf16)
    q = qb[...].astype(f32)
    q = jnp.concatenate([q, jnp.zeros((16 - q.shape[0], 16), f32)], 0)
    out[16:32, 256:272] = q.astype(bf16)
    m = mb[...].astype(f32)
    m = jnp.concatenate([m, jnp.zeros((16 - m.shape[0], 16), f32)], 0)
    out[0:16, 384:400] = m.astype(bf16)


def unpack_kernel(sc_ref, s0, s1, s2, s3, tab_ref, v_ref, b_ref, all4, *, H):
    for r, s in enumerate((s0, s1, s2, s3)):
        all4[sc_ref[2] ^ r] = s[...]
    for j in range(4):
        tab_ref[j * 16 : (j + 1) * 16, :] = all4[j, 0:16, 0:384]
    low = [all4[j, 16:32, :].astype(f32) for j in range(4)]
    dd = v_ref.shape[1] // 4
    v_ref[...] = jnp.concatenate([z[0:8, 0:dd] for z in low], 1)
    q = jnp.concatenate([z[:, 256:272] for z in low] + [jnp.zeros((16, 64), f32)], 1)
    q = q.T[0:64]
    for h in range(H):
        b_ref[h * 192 : h * 192 + 64, :] = q[:, h : h + 1]
        b_ref[h * 192 + 64 : h * 192 + 128, :] = jnp.zeros((64, 1), f32)
        b_ref[h * 192 + 128 : (h + 1) * 192, :] = q[:, H + h : H + h + 1]


def norm1_kernel(sc_ref, x_ref, v_ref, h_ref, xh_ref):
    xh, _ = norm_parts(x_ref[...].astype(f32))
    xh_ref[...] = xh.astype(bf16)
    h_ref[...] = (xh * v_ref[0:1, :] + v_ref[1:2, :]).astype(bf16)


def norm1(sc, x, vecs):
    T, D = x.shape
    bt = min(512, T)
    rows = pl.BlockSpec((bt, D), lambda i, s: (i, 0))
    return call(
        norm1_kernel, sc, (T // bt,), [rows, whole_spec(vecs.shape)], [x, vecs], [rows, rows],
        [((T, D), bf16)] * 2, [], "norm1", 20 * T * D, 6 * T * D,
    )


def qkv_kernel(sc_ref, h_ref, b_ref, w0, w1, w2, w3, q_ref, kv_ref, wt_ref, wn):
    dd = w0.shape[0]

    @pl.when(pl.program_id(0) == 0)
    def _():
        for r, w in enumerate((w0, w1, w2, w3)):
            wn[rows_of(sc_ref, r, dd), :] = w[...]
        wt_ref[...] = wn[...].T

    y = dot(wt_ref[...], h_ref[...], 1, 1) + b_ref[...]
    y = y.astype(bf16)
    for h in range(q_ref.shape[0]):
        q_ref[h] = y[h * 192 : h * 192 + 64]
        kv_ref[h] = y[h * 192 + 64 : (h + 1) * 192]


def qkv(sc, h1, bias, ws):
    T, D = h1.shape
    E3 = ws[0].shape[1]
    H = E3 // 192
    bt = min(512, T)
    return call(
        qkv_kernel, sc, (T // bt,),
        [pl.BlockSpec((bt, D), lambda i, s: (i, 0)), whole_spec(bias.shape)]
        + [whole_spec(ws[0].shape)] * 4,
        [h1, bias, *ws],
        [pl.BlockSpec((H, n, bt), lambda i, s: (0, 0, i)) for n in (64, 128)]
        + [whole_spec((E3, D))],
        [((H, 64, T), bf16), ((H, 128, T), bf16), ((E3, D), bf16)],
        [pltpu.VMEM((D, E3), bf16)],
        "qkv", 2 * T * D * E3, 4 * T * D,
    )


def mlp1_kernel(sc_ref, x_ref, g_ref, v_ref, *rest, nt, fb):
    os, (p1, p2), rest = rest[:nt], rest[nt : nt + 2], rest[nt + 2 :]
    a_ref, du_ref, h2_ref, da_ref, y1_ref, dy_ref, sm_ref, db_ref, *rest = rest
    dos, (dh, bias) = rest[:nt], rest[nt:]
    D = x_ref.shape[1]
    dd = D // 4
    ft = a_ref.shape[1]
    k = pl.program_id(0)

    def proj(kk):
        w = p2[:, lax.rem(sc_ref[1] + nt - kk, nt), :, ft:]
        return w.reshape(D, w.shape[2])

    @pl.when(k == 0)
    def _():
        y = x_ref[...].astype(f32) + v_ref[4:5, :]
        for kk in range(nt):
            y = y + dot(os[kk][...], proj(kk), 0, 1)
        y1_ref[...] = y
        xh, _ = norm_parts(y)
        h2_ref[...] = (xh * v_ref[2:3, :] + v_ref[3:4, :]).astype(bf16)
        dh[...] = jnp.zeros_like(dh)

    rows = jnp.concatenate([p1[j, dd:, 0:16].astype(f32) for j in range(4)], 1)
    for i in range(ft // 64):
        bias[:, i * 64 : (i + 1) * 64] = rows[i : i + 1]
    for j in range(ft // fb):
        sl = slice(j * fb, (j + 1) * fb)
        wi = p1[:, 0:dd, sl].reshape(D, fb)
        wo = p2[:, lax.rem(sc_ref[1] + nt - k, nt), :, sl].reshape(D, fb)
        u = jnp.dot(h2_ref[...], wi, preferred_element_type=f32) + bias[:, sl]
        ga = jnp.dot(g_ref[...], wo, preferred_element_type=f32)
        cdf = 0.5 + 0.5 * lax.erf(u * 0.7071067811865476)
        a_ref[:, sl] = (u * cdf).astype(bf16)
        slope = cdf + u * (jnp.exp(-0.5 * u * u) * 0.3989422804014327)
        du = (slope * ga).astype(bf16)
        du_ref[:, sl] = du
        db_ref[:, sl] = jnp.sum(du.astype(f32), axis=0, keepdims=True)
        dh[...] += dot(du, wi, 1, 1)

    @pl.when(k == pl.num_programs(0) - 1)
    def _():
        g = g_ref[...].astype(f32)
        xh, r = norm_parts(y1_ref[...])
        d = dh[...]
        dy = g + norm_back(d, v_ref[2:3, :], xh, r)
        dy_ref[...] = dy
        da = dy.astype(bf16)
        da_ref[...] = da
        sums = [jnp.sum(z, axis=0, keepdims=True) for z in (d * xh, d, da.astype(f32), g)]
        sm_ref[...] = jnp.concatenate(sums + [jnp.zeros((4, D), f32)], 0)
        for kk in range(nt):
            dos[kk][...] = dot(proj(kk), da, 0, 1).astype(bf16)


def back_block(nd, rows, cols, nt):
    return pl.BlockSpec(
        (nd, None, rows, cols), lambda k, s: (0, lax.rem(s[1] + nt - k, nt), 0, 0)
    )


def mlp1(sc, x, g, vecs, os, p1, p2):
    D = x.shape[1]
    nd, nt, rows, ft = p1.shape
    kt, N = os[0].shape
    mine = pl.BlockSpec((N, D), lambda k, s: (s[1], 0))
    act = pl.BlockSpec((None, N, ft), lambda k, s: (k, 0, 0))
    row = pl.BlockSpec((None, 1, ft), lambda k, s: (lax.rem(s[1] + nt - k, nt), 0, 0))
    full = whole_spec((N, D))
    return call(
        functools.partial(mlp1_kernel, nt=nt, fb=ft // 2), sc, (nt,),
        [mine, mine, whole_spec(vecs.shape)]
        + [whole_spec((kt, N))] * nt
        + [back_block(nd, rows, ft, nt), whole_spec(p2.shape)],
        [x, g, vecs, *os, p1, p2],
        [act, act, full, full, full, full, whole_spec((8, D)), row] + [whole_spec((kt, N))] * nt,
        [((nt, N, ft), bf16)] * 2
        + [((N, D), bf16)] * 2
        + [((N, D), f32)] * 2
        + [((8, D), f32), ((nt, 1, ft), f32)]
        + [((kt, N), bf16)] * nt,
        [pltpu.VMEM((N, D), f32), pltpu.VMEM((1, ft), f32)],
        "mlp_grad", 6 * N * D * ft * nt + 4 * N * D * D, 24 * 2**20,
    )


def mlp2_kernel(sc_ref, g_ref, v_ref, h2_ref, da_ref, y_ref, a_ref, du_ref, *rest, nt):
    os, (p2, *rest) = rest[:nt], rest[nt:]
    keep_ref, send_ref, out_ref, hT, gT, dT, oa, acc, acn = rest
    ft = a_ref.shape[1]
    D = h2_ref.shape[1]
    dd = D // 4
    k = pl.program_id(0)

    @pl.when(k == 0)
    def _():
        for src, dst in ((h2_ref, hT), (g_ref, gT), (da_ref, dT)):
            acn[...] = src[...].astype(f32).T
            for r in range(4):
                dst[r * dd : (r + 1) * dd, :] = acn[rows_of(sc_ref, r, dd), :].astype(bf16)
        for kk in range(nt):
            oa[kk] = os[kk][...]
        acc[...] = jnp.zeros_like(acc)

    a = a_ref[...]
    acc[...] += dot(a, p2[:, :, :ft].reshape(D, ft), 1, 1)

    def store(value, lo, hi):
        value = value.astype(bf16)
        for r in range(4):
            dst = send_ref if r & 1 else keep_ref
            dst[r // 2, :, lo:hi] = value[r * dd : (r + 1) * dd]

    store(jnp.dot(hT[...], du_ref[...], preferred_element_type=f32), 0, ft)
    store(jnp.dot(gT[...], a, preferred_element_type=f32), ft, 2 * ft)
    store(dot(dT[...], oa[k], 1, 1), 2 * ft, keep_ref.shape[2])

    @pl.when(k == pl.num_programs(0) - 1)
    def _():
        out_ref[...] = (y_ref[...] + (acc[...] + v_ref[5:6, :])).astype(bf16)


def mlp2(sc, g, vecs, h2, da, y1, a, du, os, p2):
    N, D = h2.shape
    nd, nt, dd, _ = p2.shape
    ft = a.shape[2]
    kt = os[0].shape[0]
    cols = 2 * ft + kt
    full = whole_spec((N, D))
    act = pl.BlockSpec((None, N, ft), lambda k, s: (k, 0, 0))
    gw = back_block(2, dd, cols, nt)
    return call(
        functools.partial(mlp2_kernel, nt=nt), sc, (nt,),
        [pl.BlockSpec((N, D), lambda k, s: (s[1], 0)), whole_spec(vecs.shape), full, full, full]
        + [act, act]
        + [whole_spec((kt, N))] * nt
        + [back_block(nd, dd, p2.shape[3], nt)],
        [g, vecs, h2, da, y1, a, du, *os, p2],
        [gw, gw, full],
        [((2, nt, dd, cols), bf16)] * 2 + [((N, D), bf16)],
        [pltpu.VMEM((D, N), bf16)] * 3
        + [pltpu.VMEM((nt, kt, N), bf16), pltpu.VMEM((N, D), f32), pltpu.VMEM((D, N), f32)],
        "mlp_weights", 7 * N * D * ft * nt, 24 * 2**20,
    )


def gqkv_kernel(sc_ref, x_ref, v_ref, wt_ref, *rest, nt, H):
    dx, (keep_ref, send_ref, b_ref, n_ref, g) = rest[: H * nt], rest[H * nt :]
    dd = keep_ref.shape[1]
    lane = iota((192, 128), 1)
    gain, shift = v_ref[0:1, :], v_ref[1:2, :]
    dg, db = jnp.zeros_like(gain), jnp.zeros_like(gain)
    for h in range(H):
        t = jnp.zeros((192, x_ref.shape[2]), f32)
        b = jnp.zeros((192, 1), f32)
        for k in range(nt):
            d = dx[h * nt + k][...]
            t = t + jnp.dot(d, x_ref[lax.rem(sc_ref[1] + k, nt)], preferred_element_type=f32)
            b = b + jnp.sum(d.astype(f32), axis=1, keepdims=True)
        w = wt_ref[h * 192 : (h + 1) * 192, :].astype(f32)
        dg = dg + jnp.sum(w * t, axis=0, keepdims=True)
        db = db + jnp.sum(w * b, axis=0, keepdims=True)
        g[:, h * 192 : (h + 1) * 192] = (t * gain + shift * b).T.astype(bf16)
        b_ref[h] = jnp.where(lane == 0, b, 0.0)
    n_ref[...] = jnp.concatenate([dg, db, jnp.zeros((6, dg.shape[1]), f32)], 0)
    for r in range(4):
        dst = send_ref if r & 1 else keep_ref
        dst[r // 2] = g[rows_of(sc_ref, r, dd), :]


def gqkv(sc, xh, vecs, wT, dx, nt):
    T, D = xh.shape
    H = len(dx) // nt
    N = T // nt
    dd = D // 4
    part = (2, dd, H * 192)
    return call(
        functools.partial(gqkv_kernel, nt=nt, H=H), sc, (1,),
        [whole_spec((nt, N, D)), whole_spec(vecs.shape), whole_spec(wT.shape)]
        + [whole_spec((192, N))] * len(dx),
        [xh.reshape(nt, N, D), vecs, wT, *dx],
        [whole_spec(part), whole_spec(part), whole_spec((H, 192, 128)), whole_spec((8, D))],
        [(part, bf16), (part, bf16), ((H, 192, 128), f32), ((8, D), f32)],
        [pltpu.VMEM((D, H * 192), bf16)],
        "qkv_weights", 2 * T * D * 192 * H, 8 * 2**20,
    )


def dh1_kernel(sc_ref, x_ref, dy_ref, v_ref, *rest, nt, H):
    dx, (p3, gi_ref, da) = rest[: H * nt], rest[H * nt :]
    D = x_ref.shape[1]
    E3 = H * 192
    for k in range(nt):
        for h in range(H):
            da[(k * H + h) * 192 : (k * H + h + 1) * 192, :] = dx[h * nt + k][...]
    t = jnp.zeros((D, da.shape[1]), f32)
    for k in range(nt):
        w = p3[:, lax.rem(sc_ref[1] + nt - k, nt)].reshape(D, E3)
        t = t + jnp.dot(w, da[k * E3 : (k + 1) * E3, :], preferred_element_type=f32)
    xh, r = norm_parts(x_ref[...].astype(f32))
    gi_ref[...] = (dy_ref[...] + norm_back(t.T, v_ref[0:1, :], xh, r)).astype(bf16)


def dh1(sc, x, dy1, vecs, dx, p3):
    N, D = dy1.shape
    nt = p3.shape[1]
    H = len(dx) // nt
    return call(
        functools.partial(dh1_kernel, nt=nt, H=H), sc, (1,),
        [pl.BlockSpec((N, D), lambda k, s: (s[1], 0)), whole_spec((N, D)), whole_spec(vecs.shape)]
        + [whole_spec((192, N))] * len(dx)
        + [whole_spec(p3.shape)],
        [x, dy1, vecs, *dx, p3],
        [whole_spec((N, D))],
        [((N, D), bf16)],
        [pltpu.VMEM((nt * H * 192, N), bf16)],
        "norm1_grad", 2 * N * D * D * 3, 8 * 2**20,
    )[0]


def place_kernel(sc_ref, *refs):
    for k, p in enumerate(refs[:-1]):

        @pl.when(pl.program_id(0) == k)
        def _(p=p):
            refs[-1][...] = p[...].astype(refs[-1].dtype)


def place(sc, parts, dtype):
    N, D = parts[0].shape
    nt = len(parts)
    return call(
        place_kernel, sc, (nt,), [whole_spec((N, D))] * nt, parts,
        [pl.BlockSpec((N, D), lambda k, s: (lax.rem(s[1] + nt - k, nt), 0))],
        [((nt * N, D), dtype)], [], "place", 0, 8 * nt * N * D,
    )[0]


def shift(value, axis, steps):
    n = lax.axis_size(axis)
    return lax.ppermute(value, axis, [(s, (s + steps) % n) for s in range(n)])


def flip(value, axis, bit):
    n = lax.axis_size(axis)
    return lax.ppermute(value, axis, [(s, s ^ bit) for s in range(n)])


def after(value, *others):
    return lax.optimization_barrier((value, *others))[0]


def gather_weights(shard):
    nd, nt = lax.axis_size("dp"), lax.axis_size("tensor")
    return lax.all_gather(shard, ("dp", "tensor")).reshape((nd, nt) + shard.shape)


def reduce_all(v):
    v = v + flip(v, "dp", 1)
    v = v + flip(v, "dp", 2)
    v = v + flip(v, "tensor", 1)
    v = v + flip(v, "tensor", 2)
    return v + flip(v, "ctx", 1) if lax.axis_size("ctx") == 2 else lax.psum(v, "ctx")


def total_ctx(value):
    v = value.astype(bf16)
    if lax.axis_size("ctx") == 2:
        return v.astype(f32) + flip(v, "ctx", 1).astype(f32)
    return lax.psum(v.astype(f32), "ctx")


def per_device(
    block_input,
    cotangent,
    norm1_gain,
    norm1_bias,
    qkv_weight,
    qkv_bias,
    rel_pos_h,
    rel_pos_w,
    proj_weight,
    proj_bias,
    norm2_gain,
    norm2_bias,
    mlp_in_weight,
    mlp_in_bias,
    mlp_out_weight,
    mlp_out_bias,
):
    nt, nc = lax.axis_size("tensor"), lax.axis_size("ctx")
    me, pos, dp = lax.axis_index("tensor"), lax.axis_index("ctx"), lax.axis_index("dp")
    T, D = block_input.shape[1:]
    R = T // GW
    dd = D // 4
    H = qkv_bias.shape[1]
    E = H * HD
    L = rel_pos_h.shape[0]
    ft = mlp_in_weight.shape[1]
    x2 = block_input.reshape(T, D)
    g2 = cotangent.reshape(T, D)

    def scalars(k):
        off = (((pos - k) % nc) - pos) * R
        return jnp.stack([off, me, dp]).astype(jnp.int32)

    sc = scalars(0)
    bar = lax.optimization_barrier

    w0 = qkv_weight.reshape(dd, 3, H, HD).transpose(0, 2, 1, 3).reshape(dd, 3 * E)
    ws = [w0] + [flip(w0, "dp", r) for r in (1, 2, 3)]
    vrow = lambda v: v.reshape(1, dd)
    smalls = [rel_pos_h, rel_pos_w]
    smalls += [vrow(v) for v in (norm1_gain, norm1_bias, norm2_gain, norm2_bias, proj_bias)]
    smalls += [vrow(mlp_out_bias), qkv_bias.reshape(2 * H, 16), mlp_in_bias]
    small = call(
        pack_kernel, sc, (1,), [whole_spec(v.shape) for v in smalls], smalls,
        [whole_spec((32, 512))], [((32, 512), bf16)], [], "pack", 0, 2**16,
    )[0]
    small = [small] + [flip(small, "dp", r) for r in (1, 2, 3)]
    tab, vecs, bqkv = call(
        functools.partial(unpack_kernel, H=H), sc, (1,), [whole_spec((32, 512))] * 4, small,
        [whole_spec((64, 384)), whole_spec((8, D)), whole_spec((3 * E, 1))],
        [((64, 384), bf16), ((8, D), f32), ((3 * E, 1), f32)],
        [pltpu.VMEM((4, 32, 512), bf16)], "unpack", 0, 2**17,
    )

    nb = mlp_in_bias.shape[0]
    p1 = jnp.concatenate([mlp_in_weight, jnp.pad(mlp_in_bias, ((0, 16 - nb), (0, ft - 16)))], 0)
    p1 = gather_weights(p1)
    p2 = gather_weights(jnp.concatenate([mlp_out_weight.T, proj_weight.T], 1))
    p3 = gather_weights(w0)

    h1, xh1 = norm1(sc, x2, vecs)
    qT, kvT, wT = qkv(sc, h1, bqkv, ws)
    kv_far = [shift(kvT, "ctx", k) for k in range(1, nc)]

    state = attn_fwd(sc, qT, kvT, tab, None, False, R, nt)
    for k in range(1, nc):
        state = attn_fwd(scalars(k), qT, kv_far[k - 1], tab, state[:2], k == nc - 1, R, nt)
    o32, lse, *os = state
    os = [os[0]] + [shift(os[k], "tensor", k) for k in range(1, nt)]

    a, du, h2, da, y1, dy1, sm2, dbin, *dos = mlp1(sc, x2, g2, vecs, os, p1, p2)
    dos = [dos[0]] + [shift(dos[k], "tensor", -k) for k in range(1, nt)]
    keep, send, out = mlp2(sc, g2, vecs, h2, da, y1, a, du, os, p2)
    out, dos = bar((out, dos))
    block_out = lax.all_gather(out, "tensor", axis=0, tiled=True).reshape(1, T, D)

    add = lambda *v: sum(z.astype(f32) for z in v).astype(bf16)
    core = flip(send, "dp", 1)
    dtab = None
    dqs, backs = [], []
    for h in range(H):
        back, dq = None, None
        for k in range(1, nc):
            st = None if dtab is None else (dq if dq is not None else jnp.zeros((64, T), f32), dtab)
            dq, dkv, dtab = attn_bwd(
                scalars(k), h, qT, kv_far[k - 1], tab, dos, o32, lse, st, None, R
            )
            dkv = shift(dkv, "ctx", -k)
            back = dkv if back is None else add(back, dkv)
        dqs.append(dq)
        backs.append(back)
        if h == 0:
            dtab, core = bar((dtab, core))
            xrec = flip(add(keep[1], core[1]), "dp", 2)
    dtab, xrec = bar((dtab, xrec))
    v = add(keep[0], core[0], xrec)
    halves = nc == 2
    if halves:
        v = v.reshape(nt, 2, dd // 2, v.shape[2])
        part = lambda i: lax.dynamic_index_in_dim(v, i, 1, keepdims=False)
        yrec = flip(part(1 - pos), "ctx", 1)
    dx, dxr = [], []
    for h in range(H):
        *d, dtab = attn_bwd(sc, h, qT, kvT, tab, dos, o32, lse, (dqs[h], dtab), backs[h], R)
        dx += d
        moved = [d[0]] + [shift(d[k], "tensor", k) for k in range(1, nt)]
        if h == 1:
            if halves:
                dtab, yrec, dxr = bar((dtab, yrec, dxr))
                v = add(part(pos), yrec)
            else:
                dtab, dxr = bar((dtab, dxr))
        if h == 2:
            dtab, dxr, xh1 = bar((dtab, dxr, xh1))
        dxr = dxr + moved
    gsum = lax.psum_scatter(v, "tensor", scatter_dimension=0)

    keepq, sendq, bq, sm1 = gqkv(sc, xh1, vecs, wT, dx, nt)
    coreq = flip(sendq, "dp", 1)
    gin = dh1(sc, x2, dy1, vecs, dxr, p3)
    gins = [gin] + [shift(gin, "tensor", k) for k in range(1, nt)]
    grad_input = place(sc, gins, f32).reshape(1, T, D)

    if halves:
        other = flip(gsum, "ctx", 1)
        gmine = jnp.concatenate(
            [jnp.where(pos == 0, gsum, other), jnp.where(pos == 0, other, gsum)], 0
        ).astype(f32)
    else:
        gmine = total_ctx(gsum)
    g_in = gmine[:, :ft]
    g_out = gmine[:, ft : 2 * ft].T
    g_proj = gmine[:, 2 * ft :].T
    farq = flip(add(keepq[1], coreq[1]), "dp", 2)
    gq = total_ctx(add(keepq[0], coreq[0], farq))
    g_qkv = gq.reshape(dd, H, 3, HD).transpose(0, 2, 1, 3).reshape(dd, 3, E)

    tid = jnp.arange(nt)
    bq = bq[:, :, 0].reshape(H, 3, HD)
    bq = jnp.stack([bq[:, 0], bq[:, 2]]).reshape(1, 2 * E)
    bq = jnp.where(tid[:, None] == me, bq, 0.0)
    flat = jnp.concatenate(
        [z.reshape(-1, 256) for z in (sm2[:4], sm1[:2], dbin, bq)] + [dtab]
    )
    flat = reduce_all(flat)
    vec = flat[: 6 * D // 256].reshape(6, 4, dd)
    vec = lax.dynamic_index_in_dim(vec, dp, 1, keepdims=False)
    at = 6 * D // 256
    gb = flat[at : at + nt * ft // 256].reshape(nt, ft // 64, 4, 16)
    gb = lax.dynamic_index_in_dim(gb, me, 0, keepdims=False)
    gb = lax.dynamic_index_in_dim(gb, dp, 1, keepdims=False)
    at += nt * ft // 256
    gbq = flat[at : at + nt * 2 * E // 256].reshape(nt, 2, H, 4, 16)
    gbq = lax.dynamic_index_in_dim(gbq, me, 0, keepdims=False)
    gbq = lax.dynamic_index_in_dim(gbq, dp, 2, keepdims=False)
    at += nt * 2 * E // 256
    gtab = lax.dynamic_index_in_dim(flat[at:].reshape(4, 16, 2, 128), dp, 0, keepdims=False)
    return (
        block_out,
        grad_input,
        vec[4],
        vec[5],
        g_qkv,
        gbq,
        gtab[:, 0, :L][:, ::-1].T,
        gtab[:, 1, :L].T,
        g_proj,
        vec[2],
        vec[0],
        vec[1],
        g_in,
        gb,
        g_out,
        vec[3],
    )


def solution(mesh):
    placed = (
        P("dp", "ctx", None),
        P("dp", "ctx", None),
        P("dp"),
        P("dp"),
        P("dp", None, "tensor"),
        P(None, "tensor", "dp"),
        P(None, "dp"),
        P(None, "dp"),
        P("tensor", "dp"),
        P("dp"),
        P("dp"),
        P("dp"),
        P("dp", "tensor"),
        P("tensor", "dp"),
        P("tensor", "dp"),
        P("dp"),
    )
    return jax.shard_map(
        per_device,
        mesh=mesh,
        in_specs=placed,
        out_specs=(placed[0], placed[0]) + placed[2:],
        check_vma=False,
    )
```

```python
import functools

import jax
import jax.numpy as jnp
from jax import lax
from jax.experimental import pallas as pl
from jax.experimental.pallas import tpu as pltpu
from jax.sharding import PartitionSpec as P

HD = 64
GW = 64
EPS = 1e-06
f32 = jnp.float32
bf16 = jnp.bfloat16
VMEM = 56 * 2**20


def iota(shape, dim):
    return lax.broadcasted_iota(jnp.int32, shape, dim)


def dot(a, b, ca, cb):
    return lax.dot_general(a, b, (((ca,), (cb,)), ((), ())), preferred_element_type=f32)


def make_qaug(qT, tab, il0, off, R):
    bq = qT.shape[1]
    qf = jnp.concatenate([qT.astype(f32), jnp.zeros((64, bq), f32)], 0).T
    g = dot(qT, tab, 0, 0)
    lane = iota((64, 128), 1)
    used = (lane < 64 + R) | ((lane >= 96) & (lane < 96 + R))
    outs = []
    for k in range(bq // 64):
        gh = g[k * 64 : (k + 1) * 64, :128]
        gw = g[k * 64 : (k + 1) * 64, 128:]
        sh = 63 - (il0 + k) + off
        h64 = pltpu.roll(gh, lax.rem(64 - sh + 256, 128), 1)
        h96 = pltpu.roll(gh, lax.rem(96 - sh + 256, 128), 1)
        w64 = pltpu.roll(gw, 1, 1, stride=1, stride_axis=0)
        w0 = pltpu.roll(gw, 65, 1, stride=1, stride_axis=0)
        a = jnp.where(lane < 64, qf[k * 64 : (k + 1) * 64], w64)
        wl = w0 - w0.astype(bf16).astype(f32)
        hl = h96 - h96.astype(bf16).astype(f32)
        b = jnp.where(lane < 64, wl, jnp.where(lane < 96, h64, hl))
        b = jnp.where(used, b, 0.0)
        outs.append(jnp.concatenate([a, b], 1).astype(bf16))
    return jnp.concatenate(outs, 0)


def build_kaug(kT, kaug, flipped=False):
    KB = kT.shape[1]
    ck = min(512, KB)
    for c in range(KB // ck):
        kf = kT[:, c * ck : (c + 1) * ck].astype(f32) * 0.125
        kf = jnp.concatenate([kf, jnp.zeros((64, ck), f32)], 0).T
        n = iota((ck, 128), 0) + c * ck
        lane = iota((ck, 128), 1)
        col, row = n & 63, n >> 6
        spot = 127 - col if flipped else 64 + col
        a = jnp.where(lane < 64, kf, (lane == spot).astype(f32))
        b = jnp.where(lane < 64, (lane == col).astype(f32), ((lane & 31) == row).astype(f32))
        kaug[c * ck : (c + 1) * ck, :] = jnp.concatenate([a, b], 1).astype(bf16)


def build_kaugT(kT, kaugT):
    KB = kT.shape[1]
    ck = min(512, KB)
    for c in range(KB // ck):
        f = iota((64, ck), 0)
        n = iota((64, ck), 1) + c * ck
        col, row = n & 63, n >> 6
        sl = slice(c * ck, (c + 1) * ck)
        kaugT[0:64, sl] = (kT[:, sl].astype(f32) * 0.125).astype(bf16)
        oc = (f == col).astype(f32).astype(bf16)
        kaugT[64:128, sl] = oc
        kaugT[128:192, sl] = oc
        kaugT[192:256, sl] = ((f & 31) == row).astype(f32).astype(bf16)


def fwd_kernel(sc_ref, qT_ref, tab_ref, *rest, R, bk, first, last, nt, n):
    kvs, rest = rest[:n], rest[n:]
    if first:
        rest = (None, None) + rest
    oi_ref, mli_ref, o_ref, ml_ref, *rest = rest
    KB = kvs[0].shape[1]
    bq = qT_ref.shape[1]
    hi, qi = pl.program_id(0), pl.program_id(1)
    if last:
        kaug, vaug, och = rest[-3:]
    else:
        kaug, vaug = rest[-2:]

    for g, kv in enumerate(kvs):

        @pl.when((qi == 0) & (hi == g))
        def _(kv=kv):
            build_kaug(kv[0:64, :], kaug)
            vaug[0:64, :] = kv[64:128, :]
            vaug[64:80, :] = (iota((16, KB), 0) == 0).astype(f32).astype(bf16)

    qaug = make_qaug(qT_ref[...], tab_ref[:, :256], qi * (bq // 64), sc_ref[0], R)
    if first:
        m = jnp.full((1, bq), -3e38, f32)
        o = jnp.zeros((80, bq), f32)
    else:
        m = mli_ref[0:1, :]
        o = jnp.concatenate([oi_ref[...], jnp.broadcast_to(mli_ref[1:2, :], (16, bq))], 0)
    for c in range(KB // bk):
        s = dot(kaug[c * bk : (c + 1) * bk, :], qaug, 1, 1)
        mn = jnp.maximum(m, jnp.max(s, axis=0, keepdims=True))
        al = jnp.exp(m - mn)
        p = jnp.exp(s - mn).astype(bf16)
        o = o * al + jnp.dot(vaug[:, c * bk : (c + 1) * bk], p, preferred_element_type=f32)
        m = mn
    l = o[64:65, :]
    o = o[:64]
    if last:
        o = o * (1.0 / l)
        m = m + jnp.log(l)
        N = och.shape[2]
        ob = o.astype(bf16)
        for j in range(bq // N):
            och[qi * (bq // N) + j] = ob[:, j * N : (j + 1) * N]

        @pl.when(qi == pl.num_programs(1) - 1)
        def _():
            for k in range(nt):
                rest[k][...] = och[sc_ref[1] ^ k]

    o_ref[...] = o
    ml_ref[...] = jnp.concatenate([m, l, jnp.zeros((6, bq), f32)], 0)


def attn_fwd(sc, h0, qT, kvs, tab, state, last, R, nt, bq=2048, bk=512):
    H, _, T = qT.shape
    n = len(kvs)
    KB = kvs[0].shape[1]
    N = T // nt
    bq, bk = min(bq, T), min(bk, KB)
    first = state is None
    qs = lambda r: pl.BlockSpec((None, r, bq), lambda h, i, o: (h0 + h, 0, i))
    ins = [qs(64), pl.BlockSpec((64, 384), lambda h, i, o: (0, 0))]
    ins += [pl.BlockSpec((128, KB), lambda h, i, o: (0, 0))] * n
    ins += [] if first else [qs(64), qs(8)]
    outs = [qs(64), qs(8)]
    shapes = [jax.ShapeDtypeStruct((H, 64, T), f32), jax.ShapeDtypeStruct((H, 8, T), f32)]
    scratch = [pltpu.VMEM((KB, 256), bf16), pltpu.VMEM((80, KB), bf16)]
    if last:
        outs += [pl.BlockSpec((64, N), lambda h, i, o: (h, 0))] * nt
        shapes += [jax.ShapeDtypeStruct((n * 64, N), bf16)] * nt
        scratch += [pltpu.VMEM((nt, 64, N), bf16)]
    return pl.pallas_call(
        functools.partial(fwd_kernel, R=R, bk=bk, first=first, last=last, nt=nt, n=n),
        grid_spec=pltpu.PrefetchScalarGridSpec(
            num_scalar_prefetch=1,
            grid=(n, T // bq),
            in_specs=ins,
            out_specs=outs,
            scratch_shapes=scratch,
        ),
        out_shape=shapes,
        input_output_aliases={} if first else {3 + n: 0, 4 + n: 1},
        compiler_params=pltpu.CompilerParams(vmem_limit_bytes=VMEM),
        cost_estimate=pl.CostEstimate(
            flops=2 * n * T * KB * 512, bytes_accessed=n * T * 1200, transcendentals=n * T * KB
        ),
        name="attn_fwd",
    )(sc, qT, tab, *kvs, *([] if first else state))


def bwd_kernel(sc_ref, qT_ref, tab_ref, *rest, R, bk, has_dq, has_dt, last, nt, n):
    kvs, rest = rest[:n], rest[n:]
    do_refs, rest = rest[:nt], rest[nt:]
    o_ref, ml_ref, *rest = rest
    dqi_ref = dti_ref = dki_ref = None
    if has_dq:
        dqi_ref, *rest = rest
    if has_dt:
        dti_ref, *rest = rest
    if last:
        dki_ref, *rest = rest
        dx_refs, rest = rest[:nt], rest[nt:]
        dt_ref, kaug, kaugT, vaug, acc, dch, fin = rest
    else:
        dq_ref, dkv_ref, dt_ref, kaug, kaugT, vaug, acc, dch = rest
    KB = kvs[0].shape[1]
    bq = qT_ref.shape[1]
    N = dch.shape[2]
    per = bq // N
    hi, qi = pl.program_id(0), pl.program_id(1)

    for g, kv in enumerate(kvs):

        @pl.when((qi == 0) & (hi == g))
        def _(kv=kv):
            build_kaug(kv[0:64, :], kaug, True)
            build_kaugT(kv[0:64, :], kaugT)
            vaug[0:64, :] = kv[64:128, :]
            vaug[64:128, :] = (iota((64, KB), 0) < 3).astype(f32).astype(bf16)

    @pl.when(qi == 0)
    def _():
        if last:
            acc[0:64, :] = dki_ref[0:64, :].astype(f32) * 8.0
            acc[64:128, :] = dki_ref[64:128, :].astype(f32)
        else:
            acc[...] = jnp.zeros_like(acc)
        for k in range(nt):
            dch[sc_ref[1] ^ k] = do_refs[k][...]

    @pl.when((qi == 0) & (hi == 0))
    def _():
        dt_ref[...] = dti_ref[...] if has_dt else jnp.zeros_like(dt_ref)

    qT = qT_ref[...]
    doT = jnp.concatenate([dch[qi * per + j] for j in range(per)], 1)
    il0 = qi * (bq // 64)
    off = sc_ref[0]
    qaug = make_qaug(qT, tab_ref[:, :256], il0, off, R)
    dof = doT.astype(f32)
    nd = -jnp.sum(dof * o_ref[...], axis=0, keepdims=True)
    d1 = nd.astype(bf16).astype(f32)
    d2 = (nd - d1).astype(bf16).astype(f32)
    d3 = nd - d1 - d2
    rid = iota((64, bq), 0)
    ext = jnp.where(rid == 2, d3, jnp.where(rid == 3, ml_ref[0:1, :], 0.0))
    ext = jnp.where(rid == 0, d1, jnp.where(rid == 1, d2, ext))
    t = jnp.concatenate([dof, ext], 0).T
    lse = t[:, 67:68]
    doaug = t.astype(bf16)
    dq = jnp.zeros((bq, 256), f32)
    for c in range(KB // bk):
        sl = slice(c * bk, (c + 1) * bk)
        s = jnp.dot(qaug, kaugT[:, sl], preferred_element_type=f32)
        p = jnp.exp(s - lse)
        dp = jnp.dot(doaug, vaug[:, sl], preferred_element_type=f32)
        pb = p.astype(bf16)
        ds = (p * dp).astype(bf16)
        acc[64:128, sl] += jnp.dot(doT, pb, preferred_element_type=f32)
        acc[0:64, sl] += jnp.dot(qT, ds, preferred_element_type=f32)
        dq += jnp.dot(ds, kaug[sl, :], preferred_element_type=f32)
    lane = iota((64, 128), 1)
    his, los = [], []
    for k in range(bq // 64):
        a = dq[k * 64 : (k + 1) * 64, :128]
        b = dq[k * 64 : (k + 1) * 64, 128:]
        gw = pltpu.roll(jnp.where(lane >= 64, a, 0.0), 64, 1, stride=1, stride_axis=0)
        sh = off - (il0 + k) - 1
        gh = pltpu.roll(
            jnp.where((lane >= 64) & (lane < 64 + R), b, 0.0), lax.rem(sh + 256, 128), 1
        )
        g = jnp.concatenate([gh, gw], 1)
        h = g.astype(bf16)
        his.append(h)
        los.append((g - h.astype(f32)).astype(bf16))
    gh = jnp.concatenate(his, 0)
    gl = jnp.concatenate(los, 0)
    tab = jnp.concatenate([tab_ref[:, :128], tab_ref[:, 256:]], 1)
    dqT = dq[:, :128].T[:64] + dot(tab, gh, 1, 1) + dot(tab, gl, 1, 1)
    if has_dq:
        dqT = dqT + dqi_ref[...]
    dt_ref[...] += dot(qT, gh, 1, 0) + dot(qT, gl, 1, 0)
    if last:
        dqb = dqT.astype(bf16)
        for j in range(per):
            fin[qi * per + j, 0:64, :] = dqb[:, j * N : (j + 1) * N]
    else:
        dq_ref[...] = dqT

    @pl.when(qi == pl.num_programs(1) - 1)
    def _():
        if last:
            for j in range(nt):
                fin[j, 64:128, :] = (acc[0:64, j * N : (j + 1) * N] * 0.125).astype(bf16)
                fin[j, 128:192, :] = acc[64:128, j * N : (j + 1) * N].astype(bf16)
            for k in range(nt):
                dx_refs[k][...] = fin[sc_ref[1] ^ k]
        else:
            dkv_ref[0:64, :] = (acc[0:64, :] * 0.125).astype(bf16)
            dkv_ref[64:128, :] = acc[64:128, :].astype(bf16)


def attn_bwd(sc, h0, qT, kvs, tab, dos, o, ml, dq, dt, back, R, bq=2048, bk=512):
    _, _, T = qT.shape
    n = len(kvs)
    KB = kvs[0].shape[1]
    nt = len(dos)
    N = T // nt
    bq, bk = min(bq, T), min(bk, KB)
    last = back is not None
    qs = lambda r, h0=h0: pl.BlockSpec((None, r, bq), lambda h, i, s: (h0 + h, 0, i))
    fix = lambda shape: pl.BlockSpec(shape, lambda h, i, s: (0, 0))
    ins = [qs(64), fix((64, 384))] + [fix((128, KB))] * n
    ins += [pl.BlockSpec((64, N), lambda h, i, s: (h0 + h, 0))] * nt + [qs(64), qs(8)]
    args = [qT, tab, *kvs, *dos, o, ml]
    if dq is not None:
        ins += [qs(64, dq[1])]
        args += [dq[0]]
    if dt is not None:
        ins += [fix((64, 256))]
        args += [dt]
    scratch = [
        pltpu.VMEM((KB, 256), bf16),
        pltpu.VMEM((256, KB), bf16),
        pltpu.VMEM((128, KB), bf16),
        pltpu.VMEM((128, KB), f32),
        pltpu.VMEM((nt, 64, N), bf16),
    ]
    if last:
        ins += [pl.BlockSpec((None, 128, KB), lambda h, i, s: (back[1], 0, 0))]
        args += [back[0]]
        outs = [fix((192, N))] * nt
        shapes = [jax.ShapeDtypeStruct((192, N), bf16)] * nt
        scratch += [pltpu.VMEM((nt, 192, N), bf16)]
    else:
        outs = [qs(64, 0), pl.BlockSpec((None, 128, KB), lambda h, i, s: (h, 0, 0))]
        shapes = [jax.ShapeDtypeStruct((n, 64, T), f32), jax.ShapeDtypeStruct((n, 128, KB), bf16)]
    return pl.pallas_call(
        functools.partial(
            bwd_kernel, R=R, bk=bk, has_dq=dq is not None, has_dt=dt is not None, last=last,
            nt=nt, n=n,
        ),
        grid_spec=pltpu.PrefetchScalarGridSpec(
            num_scalar_prefetch=1,
            grid=(n, T // bq),
            in_specs=ins,
            out_specs=outs + [fix((64, 256))],
            scratch_shapes=scratch,
        ),
        out_shape=shapes + [jax.ShapeDtypeStruct((64, 256), f32)],
        compiler_params=pltpu.CompilerParams(vmem_limit_bytes=VMEM),
        cost_estimate=pl.CostEstimate(
            flops=(2 if dt is not None else 40) * n * T * KB * 1280, bytes_accessed=n * T * 3000, transcendentals=n * T * KB
        ),
        name="attn_bwd",
    )(sc, *args)


def rows_of(sc_ref, r, dd):
    return pl.ds(pl.multiple_of((sc_ref[2] ^ r) * dd, dd), dd)


def whole_spec(shape):
    return pl.BlockSpec(shape, lambda *_: (0,) * len(shape))


def norm_parts(x):
    c = x - jnp.mean(x, axis=-1, keepdims=True)
    r = lax.rsqrt(jnp.mean(c * c, axis=-1, keepdims=True) + EPS)
    return c * r, r


def norm_back(dh, gain, xhat, r):
    e = dh * gain
    return (
        e - jnp.mean(e, axis=-1, keepdims=True) - xhat * jnp.mean(e * xhat, axis=-1, keepdims=True)
    ) * r


def call(kernel, sc, grid, ins, args, outs, shapes, scratch, name, flops, nbytes):
    return pl.pallas_call(
        kernel,
        grid_spec=pltpu.PrefetchScalarGridSpec(
            num_scalar_prefetch=1, grid=grid, in_specs=ins, out_specs=outs, scratch_shapes=scratch
        ),
        out_shape=[jax.ShapeDtypeStruct(s, d) for s, d in shapes],
        compiler_params=pltpu.CompilerParams(vmem_limit_bytes=VMEM),
        cost_estimate=pl.CostEstimate(flops=flops, bytes_accessed=nbytes, transcendentals=0),
        name=name,
    )(sc, *args)


def pack_kernel(sc_ref, w, rh, rw, n1g, n1b, n2g, n2b, pb, ob, qb, out):
    dd, E3 = w.shape[1], 3 * w.shape[2]
    for h in range(E3 // 192):
        cols = [w[j, :, h * 64 : (h + 1) * 64].astype(f32) for j in range(3)]
        out[0:dd, h * 192 : (h + 1) * 192] = jnp.concatenate(cols, 1).astype(bf16)
    out[dd:, :] = jnp.zeros((32, E3), bf16)
    L = rh.shape[1]
    t, l = iota((L, 128), 0), iota((L, 128), 1)
    back = (t == L - 1 - l).astype(f32).astype(bf16)
    same = (t == l).astype(f32).astype(bf16)
    out[dd : dd + 16, 0:128] = dot(rh[...], back, 1, 0).astype(bf16)
    out[dd : dd + 16, 128:256] = dot(rw[...], back, 1, 0).astype(bf16)
    out[dd : dd + 16, 256:384] = dot(rw[...], same, 1, 0).astype(bf16)
    rows = [v[...].astype(f32).reshape(1, dd) for v in (n1g, n1b, n2g, n2b, pb, ob)]
    rows = jnp.concatenate(rows + [jnp.zeros((10, dd), f32)], 0)
    out[dd + 16 :, 0:dd] = rows.astype(bf16)
    q = [qb[h].astype(f32) for h in range(qb.shape[0])]
    q = jnp.concatenate(q + [jnp.zeros((16 - 2 * len(q), 16), f32)], 0)
    out[dd + 16 :, 256:272] = q.astype(bf16)


def front_kernel(sc_ref, x_ref, s0, s1, s2, s3, tab_ref, v_ref, q_ref, *rest, H):
    kvs, (wt_ref, xh_ref, wn, all4, bias) = rest[:H], rest[H:]
    dd = s0.shape[0] - 32

    @pl.when(pl.program_id(0) == 0)
    def _():
        for r, s in enumerate((s0, s1, s2, s3)):
            all4[sc_ref[2] ^ r] = s[dd:, :]
            wn[rows_of(sc_ref, r, dd), :] = s[0:dd, :]
        wt_ref[...] = wn[...].T
        for j in range(4):
            tab_ref[j * 16 : (j + 1) * 16, :] = all4[j, 0:16, 0:384]
        low = [all4[j, 16:32, :].astype(f32) for j in range(4)]
        v_ref[...] = jnp.concatenate([z[0:8, 0:dd] for z in low], 1)
        q = jnp.concatenate([z[:, 256:272] for z in low] + [jnp.zeros((16, 64), f32)], 1)
        q = q.T[0:64]
        for h in range(H):
            bias[h * 192 : h * 192 + 64, :] = q[:, 2 * h : 2 * h + 1]
            bias[h * 192 + 64 : h * 192 + 128, :] = jnp.zeros((64, 1), f32)
            bias[h * 192 + 128 : (h + 1) * 192, :] = q[:, 2 * h + 1 : 2 * h + 2]

    xh, _ = norm_parts(x_ref[...].astype(f32))
    xh_ref[...] = xh.astype(bf16)
    h1 = (xh * v_ref[0:1, :] + v_ref[1:2, :]).astype(bf16)
    y = dot(wt_ref[...], h1, 1, 1) + bias[...]
    y = y.astype(bf16)
    for h in range(H):
        q_ref[h] = y[h * 192 : h * 192 + 64]
        kvs[h][...] = y[h * 192 + 64 : (h + 1) * 192]


def front(sc, x, ss, H):
    T, D = x.shape
    E3 = H * 192
    bt = min(512, T)
    rows = pl.BlockSpec((bt, D), lambda i, s: (i, 0))
    return call(
        functools.partial(front_kernel, H=H), sc, (T // bt,),
        [rows] + [whole_spec(ss[0].shape)] * 4, [x, *ss],
        [whole_spec((64, 384)), whole_spec((8, D))]
        + [pl.BlockSpec((H, 64, bt), lambda i, s: (0, 0, i))]
        + [pl.BlockSpec((128, bt), lambda i, s: (0, i))] * H
        + [whole_spec((E3, D)), rows],
        [((64, 384), bf16), ((8, D), f32), ((H, 64, T), bf16)]
        + [((128, T), bf16)] * H
        + [((E3, D), bf16), ((T, D), bf16)],
        [pltpu.VMEM((D, E3), bf16), pltpu.VMEM((4, 32, E3), bf16), pltpu.VMEM((E3, 1), f32)],
        "front", 2 * T * D * E3, 6 * T * D,
    )


def mlpa_kernel(sc_ref, x_ref, v_ref, *rest, nt, fb):
    no = 2 * nt
    os, ps, p1, rest = rest[:no], rest[no : no + 4], rest[no + 4], rest[no + 5 :]
    a_ref, sl_ref, h2_ref, y1_ref, wt_ref, wp, b4, bias = rest
    dd, ft = p1.shape[1:]
    D = 4 * dd
    k = pl.program_id(0)

    @pl.when(k == 0)
    def _():
        y = x_ref[...].astype(f32) + v_ref[4:5, :]
        na = os[0].shape[0]
        for kk in range(nt):
            for r in range(4):
                wp[rows_of(sc_ref, r, dd), :] = ps[r][kk, 0:dd]
            wt = wp[...].T
            wt_ref[kk] = wt
            y = y + dot(os[kk][...], wt[:na], 0, 0)
            y = y + dot(os[nt + kk][...], wt[na:], 0, 0)
        y1_ref[...] = y
        xh, _ = norm_parts(y)
        h2_ref[...] = (xh * v_ref[2:3, :] + v_ref[3:4, :]).astype(bf16)

    for r in range(4):
        b4[sc_ref[2] ^ r] = ps[r][k, dd:, :].astype(f32)
    rows = jnp.concatenate([b4[j, :, 0:16] for j in range(4)], 1)
    for i in range(ft // 64):
        bias[:, i * 64 : (i + 1) * 64] = rows[i : i + 1]
    for j in range(ft // fb):
        sl = slice(j * fb, (j + 1) * fb)
        wi = p1[:, :, sl].reshape(D, fb)
        u = jnp.dot(h2_ref[...], wi, preferred_element_type=f32) + bias[:, sl]
        cdf = 0.5 + 0.5 * lax.erf(u * 0.7071067811865476)
        a_ref[:, sl] = (u * cdf).astype(bf16)
        slope = cdf + u * (jnp.exp(-0.5 * u * u) * 0.3989422804014327)
        sl_ref[:, sl] = slope.astype(sl_ref.dtype)


def back_block(nd, rows, cols):
    return pl.BlockSpec((nd, None, rows, cols), lambda k, s: (0, s[1] ^ k, 0, 0))


def mlpa(sc, x, vecs, os, ps, p1):
    D = x.shape[1]
    nd, nt, dd, ft = p1.shape
    N = os[0].shape[1]
    kt = ps[0].shape[2]
    mine = pl.BlockSpec((N, D), lambda k, s: (s[1], 0))
    act = pl.BlockSpec((None, N, ft), lambda k, s: (k, 0, 0))
    full = whole_spec((N, D))
    return call(
        functools.partial(mlpa_kernel, nt=nt, fb=256), sc, (nt,),
        [mine, whole_spec(vecs.shape)]
        + [whole_spec(o.shape) for o in os]
        + [whole_spec(p.shape) for p in ps]
        + [back_block(nd, dd, ft)],
        [x, vecs, *os, *ps, p1],
        [act, act, full, full, whole_spec((nt, kt, D))],
        [((nt, N, ft), bf16), ((nt, N, ft), f32), ((N, D), bf16), ((N, D), f32)]
        + [((nt, kt, D), bf16)],
        [pltpu.VMEM((D, kt), bf16), pltpu.VMEM((4, 16, kt), f32), pltpu.VMEM((1, ft), f32)],
        "mlp_in", 3 * N * D * ft * nt, 24 * 2**20,
    )


def mlpb_kernel(sc_ref, g_ref, v_ref, y1_ref, sl_ref, *rest, nt, fb):
    wt_ref, p1, p2, du_ref, da_ref, dy_ref, sm_ref, db_ref, *dos, dh = rest
    D, ft = p1.shape[0] * p1.shape[1], p1.shape[2]
    k = pl.program_id(0)

    @pl.when(k == 0)
    def _():
        dh[...] = jnp.zeros_like(dh)

    for j in range(ft // fb):
        sl = slice(j * fb, (j + 1) * fb)
        ga = jnp.dot(g_ref[...], p2[:, :, sl].reshape(D, fb), preferred_element_type=f32)
        du = (sl_ref[:, sl] * ga).astype(bf16)
        du_ref[:, sl] = du
        db_ref[:, sl] = jnp.sum(du.astype(f32), axis=0, keepdims=True)
        dh[...] += dot(du, p1[:, :, sl].reshape(D, fb), 1, 1)

    @pl.when(k == pl.num_programs(0) - 1)
    def _():
        g = g_ref[...].astype(f32)
        xh, r = norm_parts(y1_ref[...])
        d = dh[...]
        dy = g + norm_back(d, v_ref[2:3, :], xh, r)
        dy_ref[...] = dy
        da = dy.astype(bf16)
        da_ref[...] = da
        sums = [jnp.sum(z, axis=0, keepdims=True) for z in (d * xh, d, da.astype(f32), g)]
        sm_ref[...] = jnp.concatenate(sums + [jnp.zeros((4, D), f32)], 0)
        for kk in range(nt):
            dos[kk][...] = dot(wt_ref[kk], da, 1, 1).astype(bf16)


def mlpb(sc, g, vecs, y1, slope, wt, p1, p2):
    N, D = y1.shape
    nd, nt, dd, ft = p1.shape
    kt = wt.shape[1]
    act = pl.BlockSpec((None, N, ft), lambda k, s: (k, 0, 0))
    row = pl.BlockSpec((None, 1, ft), lambda k, s: (s[1] ^ k, 0, 0))
    full = whole_spec((N, D))
    return call(
        functools.partial(mlpb_kernel, nt=nt, fb=256), sc, (nt,),
        [pl.BlockSpec((N, D), lambda k, s: (s[1], 0)), whole_spec(vecs.shape), full, act]
        + [whole_spec(wt.shape)]
        + [back_block(nd, dd, ft)] * 2,
        [g, vecs, y1, slope, wt, p1, p2],
        [act, full, full, whole_spec((8, D)), row] + [whole_spec((kt, N))] * nt,
        [((nt, N, ft), bf16), ((N, D), bf16), ((N, D), f32), ((8, D), f32), ((nt, 1, ft), f32)]
        + [((kt, N), bf16)] * nt,
        [pltpu.VMEM((N, D), f32)],
        "mlp_grad", 5 * N * D * ft * nt, 24 * 2**20,
    )


def mlp2_kernel(sc_ref, g_ref, v_ref, h2_ref, da_ref, y_ref, a_ref, du_ref, *rest, nt):
    no = 2 * nt
    os, (p2, *rest) = rest[:no], rest[no:]
    gws, (out_ref, hT, gT, dT, oa, acc, acn) = rest[:4], rest[4:]
    ft = a_ref.shape[1]
    D = h2_ref.shape[1]
    dd = D // 4
    k = pl.program_id(0)

    @pl.when(k == 0)
    def _():
        for src, dst in ((h2_ref, hT), (g_ref, gT), (da_ref, dT)):
            acn[...] = src[...].astype(f32).T
            for r in range(4):
                dst[r * dd : (r + 1) * dd, :] = acn[rows_of(sc_ref, r, dd), :].astype(bf16)
        na = os[0].shape[0]
        for kk in range(nt):
            oa[kk, :na] = os[kk][...]
            oa[kk, na:] = os[nt + kk][...]
        acc[...] = jnp.zeros_like(acc)

    a = a_ref[...]
    acc[...] += dot(a, p2[...].reshape(D, ft), 1, 1)

    def store(value, lo, hi):
        value = value.astype(bf16)
        for r in range(4):
            gws[r][:, lo:hi] = value[r * dd : (r + 1) * dd]

    store(jnp.dot(hT[...], du_ref[...], preferred_element_type=f32), 0, ft)
    store(jnp.dot(gT[...], a, preferred_element_type=f32), ft, 2 * ft)
    store(dot(dT[...], oa[k], 1, 1), 2 * ft, gws[0].shape[1])

    @pl.when(k == pl.num_programs(0) - 1)
    def _():
        out_ref[...] = (y_ref[...] + (acc[...] + v_ref[5:6, :])).astype(bf16)


def mlp2(sc, g, vecs, h2, da, y1, a, du, os, p2):
    N, D = h2.shape
    nd, nt, dd, ft = p2.shape
    kt = os[0].shape[0] + os[nt].shape[0]
    cols = 2 * ft + kt
    full = whole_spec((N, D))
    act = pl.BlockSpec((None, N, ft), lambda k, s: (k, 0, 0))
    gw = pl.BlockSpec((None, dd, cols), lambda k, s: (s[1] ^ k, 0, 0))
    return call(
        functools.partial(mlp2_kernel, nt=nt), sc, (nt,),
        [pl.BlockSpec((N, D), lambda k, s: (s[1], 0)), whole_spec(vecs.shape), full, full, full]
        + [act, act]
        + [whole_spec(o.shape) for o in os]
        + [back_block(nd, dd, ft)],
        [g, vecs, h2, da, y1, a, du, *os, p2],
        [gw] * 4 + [full],
        [((nt, dd, cols), bf16)] * 4 + [((N, D), bf16)],
        [pltpu.VMEM((D, N), bf16)] * 3
        + [pltpu.VMEM((nt, kt, N), bf16), pltpu.VMEM((N, D), f32), pltpu.VMEM((D, N), f32)],
        "mlp_weights", 7 * N * D * ft * nt, 24 * 2**20,
    )


def gqkv_kernel(sc_ref, x_ref, v_ref, wt_ref, *rest, nt, H):
    dx, (keep_ref, send_ref, b_ref, n_ref, g) = rest[: H * nt], rest[H * nt :]
    dd = keep_ref.shape[1]
    lane = iota((192, 128), 1)
    gain, shift = v_ref[0:1, :], v_ref[1:2, :]
    dg, db = jnp.zeros_like(gain), jnp.zeros_like(gain)
    for h in range(H):
        t = jnp.zeros((192, x_ref.shape[2]), f32)
        b = jnp.zeros((192, 1), f32)
        for k in range(nt):
            d = dx[h * nt + k][...]
            t = t + jnp.dot(d, x_ref[sc_ref[1] ^ k], preferred_element_type=f32)
            b = b + jnp.sum(d.astype(f32), axis=1, keepdims=True)
        w = wt_ref[h * 192 : (h + 1) * 192, :].astype(f32)
        dg = dg + jnp.sum(w * t, axis=0, keepdims=True)
        db = db + jnp.sum(w * b, axis=0, keepdims=True)
        g[:, h * 192 : (h + 1) * 192] = (t * gain + shift * b).T.astype(bf16)
        b_ref[h] = jnp.where(lane == 0, b, 0.0)
    n_ref[...] = jnp.concatenate([dg, db, jnp.zeros((6, dg.shape[1]), f32)], 0)
    for r in range(4):
        dst = send_ref if r & 1 else keep_ref
        dst[r // 2] = g[rows_of(sc_ref, r, dd), :]


def gqkv(sc, xh, vecs, wT, dx, nt):
    T, D = xh.shape
    H = len(dx) // nt
    N = T // nt
    dd = D // 4
    part = (2, dd, H * 192)
    return call(
        functools.partial(gqkv_kernel, nt=nt, H=H), sc, (1,),
        [whole_spec((nt, N, D)), whole_spec(vecs.shape), whole_spec(wT.shape)]
        + [whole_spec((192, N))] * len(dx),
        [xh.reshape(nt, N, D), vecs, wT, *dx],
        [whole_spec(part), whole_spec(part), whole_spec((H, 192, 128)), whole_spec((8, D))],
        [(part, bf16), (part, bf16), ((H, 192, 128), f32), ((8, D), f32)],
        [pltpu.VMEM((D, H * 192), bf16)],
        "qkv_weights", 2 * T * D * 192 * H, 8 * 2**20,
    )


def dh1_kernel(sc_ref, x_ref, dy_ref, v_ref, *rest, nt, H):
    dx, (p3, gi_ref, da) = rest[: H * nt], rest[H * nt :]
    D = x_ref.shape[1]
    E3 = H * 192
    for k in range(nt):
        for h in range(H):
            da[(k * H + h) * 192 : (k * H + h + 1) * 192, :] = dx[h * nt + k][...]
    t = jnp.zeros((D, da.shape[1]), f32)
    for k in range(nt):
        w = p3[:, sc_ref[1] ^ k].reshape(D, E3)
        t = t + jnp.dot(w, da[k * E3 : (k + 1) * E3, :], preferred_element_type=f32)
    xh, r = norm_parts(x_ref[...].astype(f32))
    gi_ref[...] = (dy_ref[...] + norm_back(t.T, v_ref[0:1, :], xh, r)).astype(bf16)


def dh1(sc, x, dy1, vecs, dx, p3):
    N, D = dy1.shape
    nt = p3.shape[1]
    H = len(dx) // nt
    return call(
        functools.partial(dh1_kernel, nt=nt, H=H), sc, (1,),
        [pl.BlockSpec((N, D), lambda k, s: (s[1], 0)), whole_spec((N, D)), whole_spec(vecs.shape)]
        + [whole_spec((192, N))] * len(dx)
        + [whole_spec(p3.shape)],
        [x, dy1, vecs, *dx, p3],
        [whole_spec((N, D))],
        [((N, D), bf16)],
        [pltpu.VMEM((nt * H * 192, N), bf16)],
        "norm1_grad", 2 * N * D * D * 3, 8 * 2**20,
    )[0]


def copy_kernel(sc_ref, a, b):
    b[...] = a[...].astype(b.dtype)


def copied(sc, v, dtype):
    rows = pl.BlockSpec((v.shape[0] // 4, v.shape[1]), lambda i, s: (i, 0))
    return call(
        copy_kernel, sc, (4,), [rows], [v], [rows], [(v.shape, dtype)], [], "copied", 0, 2**22
    )[0]


def shift(value, axis, steps):
    n = lax.axis_size(axis)
    return lax.ppermute(value, axis, [(s, (s + steps) % n) for s in range(n)])


def flip(value, axis, bit):
    n = lax.axis_size(axis)
    return lax.ppermute(value, axis, [(s, s ^ bit) for s in range(n)])


def after(value, *others):
    return lax.optimization_barrier((value, *others))[0]


def gather_weights(shard):
    nd, nt = lax.axis_size("dp"), lax.axis_size("tensor")
    return lax.all_gather(shard, ("dp", "tensor")).reshape((nd, nt) + shard.shape)


def spread(parts):
    return [parts[0]] + [flip(p, "tensor", k) for k, p in enumerate(parts) if k]


def total_ctx(value):
    v = value.astype(bf16)
    if lax.axis_size("ctx") == 2:
        return v.astype(f32) + flip(v, "ctx", 1).astype(f32)
    return lax.psum(v.astype(f32), "ctx")


def per_device(
    block_input,
    cotangent,
    norm1_gain,
    norm1_bias,
    qkv_weight,
    qkv_bias,
    rel_pos_h,
    rel_pos_w,
    proj_weight,
    proj_bias,
    norm2_gain,
    norm2_bias,
    mlp_in_weight,
    mlp_in_bias,
    mlp_out_weight,
    mlp_out_bias,
):
    nt, nc = lax.axis_size("tensor"), lax.axis_size("ctx")
    me, pos, dp = lax.axis_index("tensor"), lax.axis_index("ctx"), lax.axis_index("dp")
    T, D = block_input.shape[1:]
    R = T // GW
    dd = D // 4
    N = T // nt
    H = qkv_bias.shape[1]
    E = H * HD
    L = rel_pos_h.shape[0]
    ft = mlp_in_weight.shape[1]
    x2 = block_input.reshape(T, D)
    g2 = cotangent.reshape(T, D)

    def scalars(k):
        off = (((pos - k) % nc) - pos) * R
        return jnp.stack([off, me, dp]).astype(jnp.int32)

    sc = scalars(0)
    bar = lax.optimization_barrier

    smalls = [qkv_weight.transpose(1, 0, 2), rel_pos_h.T, rel_pos_w.T]
    smalls += [norm1_gain, norm1_bias, norm2_gain, norm2_bias, proj_bias, mlp_out_bias]
    smalls += [qkv_bias.transpose(1, 0, 2)]
    small = call(
        pack_kernel, sc, (1,), [whole_spec(v.shape) for v in smalls], smalls,
        [whole_spec((dd + 32, 3 * E))], [((dd + 32, 3 * E), bf16)], [], "pack", 0, 2**16,
    )[0]
    p1 = gather_weights(mlp_in_weight)
    p2 = gather_weights(mlp_out_weight.T)
    brow = jnp.pad(mlp_in_bias, ((0, 16 - mlp_in_bias.shape[0]), (0, E - 16)))
    own = jnp.concatenate([proj_weight.T, brow], 0)
    near = flip(own, "tensor", 1)
    small = [small] + [flip(small, "dp", r) for r in (1, 2, 3)]
    near, small = bar((near, small))
    own = jnp.stack([own, near])
    two = flip(own, "tensor", 2)

    tab, vecs, qT, *rest = front(sc, x2, small, H)
    kvs, (wT, xh1) = rest[:H], rest[H:]
    kv_far = [[shift(kv, "ctx", k) for kv in kvs] for k in range(1, nc)]

    state = attn_fwd(sc, 0, qT, kvs, tab, None, False, R, nt)
    state, two = bar((state, two))
    own = jnp.concatenate([own, two])
    far = flip(own, "dp", 2)
    for k in range(1, nc - 1):
        state = attn_fwd(scalars(k), 0, qT, kv_far[k - 1], tab, state, False, R, nt)
    os = []
    for h0, h1 in ((0, H - 1), (H - 1, H)):
        *state, o0, o1, o2, o3 = attn_fwd(
            scalars(nc - 1), h0, qT, kv_far[-1][h0:h1], tab, state, True, R, nt
        )
        if h0 == 0:
            state, far = bar((state, far))
            ps = [own, flip(own, "dp", 1), far, flip(far, "dp", 1)]
        else:
            o0, ps = bar((o0, ps))
        os += spread([o0, o1, o2, o3])
    o32, lse = state
    p3 = gather_weights(after(small[0], *os)[:dd])
    a, slope, h2, y1, wt = mlpa(sc, x2, vecs, os, ps, p1)
    du, da, dy1, sm2, dbin, *dos = mlpb(sc, g2, vecs, y1, slope, wt, p1, p2)
    dos = spread(dos)
    *gws, out = mlp2(sc, g2, vecs, h2, da, y1, a, du, os, p2)

    add = lambda *v: sum(z.astype(f32) for z in v).astype(bf16)
    out, dos, p3 = bar((out, dos, p3))
    core = [flip(gws[1], "dp", 1), flip(gws[3], "dp", 1)]
    halves = nc == 2
    part = lambda v, i: lax.dynamic_index_in_dim(
        v.reshape(v.shape[:-2] + (2, dd // 2, v.shape[-1])), i, v.ndim - 2, keepdims=False
    )
    dtab = None
    dqs, backs = [], []
    for h0, h1 in ((0, 1), (1, H)):
        back, dq = None, None
        for k in range(1, nc):
            dq, dkv, dtab = attn_bwd(
                scalars(k), h0, qT, kv_far[k - 1][h0:h1], tab, dos, o32, lse, dq, dtab, None, R
            )
            dq = (dq, 0)
            dkv = shift(dkv, "ctx", -k)
            back = dkv if back is None else add(back, dkv)
        dqs += [(dq[0], i) for i in range(h1 - h0)]
        backs += [(back, i) for i in range(h1 - h0)]
        if h0 == 0:
            dtab, core = bar((dtab, core))
            pair = [add(gws[0], core[0]), add(gws[2], core[1])]
            if halves:
                xa = flip(pair[1][: nt // 2], "dp", 2)
                low = jnp.concatenate([z[nt // 2 :] for z in pair])
                yb = flip(part(low, 1 - pos), "ctx", 1)
            else:
                xa = flip(pair[1], "dp", 2)
    block_out = lax.all_gather(out.reshape(1, N, D), "tensor", axis=1, tiled=True)
    if halves:
        dtab, xa, yb = bar((dtab, xa, yb))
        va = add(pair[0][: nt // 2], xa)
        vb = add(part(low, pos), yb)
        ya = flip(part(va, 1 - pos), "ctx", 1)
        xb = flip(vb[nt // 2 :], "dp", 2)
    else:
        dtab, xa = bar((dtab, xa))
        v = add(pair[0], xa)
    dx, dxr = [], []
    for h in range(H):
        *d, dtab = attn_bwd(
            sc, h, qT, kvs[h : h + 1], tab, dos, o32, lse, dqs[h], dtab, backs[h], R
        )
        dx += d
        if h == 0 and halves:
            dtab, xb = bar((dtab, xb))
        if h == 1:
            if halves:
                dtab, ya = bar((dtab, ya))
                v = jnp.concatenate([add(part(va, pos), ya), add(vb[: nt // 2], xb)])
            dtab, dxr, v = bar((dtab, dxr, v))
        if h == 2:
            dtab, dxr, xh1 = bar((dtab, dxr, xh1))
        dxr = dxr + spread(d)
    gsum = lax.psum_scatter(v, "tensor", scatter_dimension=0)

    keepq, sendq, bq, sm1 = gqkv(sc, xh1, vecs, wT, dx, nt)

    tid = jnp.arange(nt)
    bq = bq[:, :, 0].reshape(H, 3, HD)
    bq = jnp.stack([bq[:, 0], bq[:, 2]]).reshape(1, 2 * E)
    bq = jnp.where(tid[:, None] == me, bq, 0.0)
    flat = jnp.concatenate(
        [z.reshape(-1, 256) for z in (sm2[:4], sm1[:2], dbin, bq)] + [dtab]
    )
    flat, sendq, dxr = bar((flat, sendq, dxr))
    flats = [flat] + [flip(flat, "tensor", k) for k in range(1, nt)]

    gin = dh1(sc, x2, dy1, vecs, dxr, p3)
    gin, sendq, flats = bar((gin, sendq, flats))
    gall = lax.all_gather(gin, "tensor", axis=0, tiled=True)
    while len(flats) > 1:
        flats = [flats[i] + flats[i + 1] for i in range(0, len(flats), 2)]
    flat = flats[0] + flip(flats[0], "dp", 1)
    flat = flat + flip(flat, "dp", 2)
    flat = flat + flip(flat, "ctx", 1) if nc == 2 else lax.psum(flat, "ctx")

    coreq = flip(sendq, "dp", 1)
    if halves:
        gsum = gsum.astype(bf16)
        other = flip(gsum, "ctx", 1)
        gmine = jnp.concatenate(
            [jnp.where(pos == 0, gsum, other), jnp.where(pos == 0, other, gsum)], 0
        ).astype(f32)
    else:
        gmine = total_ctx(gsum)
    g_in = gmine[:, :ft]
    g_out = gmine[:, ft : 2 * ft].T
    g_proj = gmine[:, 2 * ft :].T
    farq = flip(add(keepq[1], coreq[1]), "dp", 2)
    gq = total_ctx(add(keepq[0], coreq[0], farq))
    g_qkv = gq.reshape(dd, H, 3, HD).transpose(0, 2, 1, 3).reshape(dd, 3, E)

    vec = flat[: 6 * D // 256].reshape(6, 4, dd)
    vec = lax.dynamic_index_in_dim(vec, dp, 1, keepdims=False)
    at = 6 * D // 256
    gb = flat[at : at + nt * ft // 256].reshape(nt, ft // 64, 4, 16)
    gb = lax.dynamic_index_in_dim(gb, me, 0, keepdims=False)
    gb = lax.dynamic_index_in_dim(gb, dp, 1, keepdims=False)
    at += nt * ft // 256
    gbq = flat[at : at + nt * 2 * E // 256].reshape(nt, 2, H, 4, 16)
    gbq = lax.dynamic_index_in_dim(gbq, me, 0, keepdims=False)
    gbq = lax.dynamic_index_in_dim(gbq, dp, 2, keepdims=False)
    at += nt * 2 * E // 256
    gtab = lax.dynamic_index_in_dim(flat[at:].reshape(4, 16, 2, 128), dp, 0, keepdims=False)
    gtab_h, gtab_w = gtab[:, 0, :L][:, ::-1].T, gtab[:, 1, :L].T
    block_out = copied(sc, after(block_out, gin).reshape(T, D), bf16)
    gall, vec, block_out, g_qkv, gbq, gtab_h, gtab_w, gb, g_in, g_out, g_proj = bar(
        (gall, vec, block_out, g_qkv, gbq, gtab_h, gtab_w, gb, g_in, g_out, g_proj)
    )
    grad_input = gall.astype(f32).reshape(1, T, D)
    return (
        block_out.reshape(1, T, D),
        grad_input,
        vec[4],
        vec[5],
        g_qkv,
        gbq,
        gtab_h,
        gtab_w,
        g_proj,
        vec[2],
        vec[0],
        vec[1],
        g_in,
        gb,
        g_out,
        vec[3],
    )


def solution(mesh):
    placed = (
        P("dp", "ctx", None),
        P("dp", "ctx", None),
        P("dp"),
        P("dp"),
        P("dp", None, "tensor"),
        P(None, "tensor", "dp"),
        P(None, "dp"),
        P(None, "dp"),
        P("tensor", "dp"),
        P("dp"),
        P("dp"),
        P("dp"),
        P("dp", "tensor"),
        P("tensor", "dp"),
        P("tensor", "dp"),
        P("dp"),
    )
    return jax.shard_map(
        per_device,
        mesh=mesh,
        in_specs=placed,
        out_specs=(placed[0], placed[0]) + placed[2:],
        check_vma=False,
    )
```

```python
import functools

import jax
import jax.numpy as jnp
from jax import lax
from jax.experimental import pallas as pl
from jax.experimental.pallas import tpu as pltpu
from jax.sharding import PartitionSpec as P

HD = 64
GW = 64
EPS = 1e-06
f32 = jnp.float32
bf16 = jnp.bfloat16
VMEM = 56 * 2**20


def iota(shape, dim):
    return lax.broadcasted_iota(jnp.int32, shape, dim)


def dot(a, b, ca, cb):
    return lax.dot_general(a, b, (((ca,), (cb,)), ((), ())), preferred_element_type=f32)


def make_qaug(qT, tab, il0, off, R):
    bq = qT.shape[1]
    qf = jnp.concatenate([qT.astype(f32), jnp.zeros((64, bq), f32)], 0).T
    g = dot(qT, tab, 0, 0)
    lane = iota((64, 128), 1)
    used = (lane < 64 + R) | ((lane >= 96) & (lane < 96 + R))
    outs = []
    for k in range(bq // 64):
        gh = g[k * 64 : (k + 1) * 64, :128]
        gw = g[k * 64 : (k + 1) * 64, 128:]
        sh = 63 - (il0 + k) + off
        h64 = pltpu.roll(gh, lax.rem(64 - sh + 256, 128), 1)
        h96 = pltpu.roll(gh, lax.rem(96 - sh + 256, 128), 1)
        w64 = pltpu.roll(gw, 1, 1, stride=1, stride_axis=0)
        w0 = pltpu.roll(gw, 65, 1, stride=1, stride_axis=0)
        a = jnp.where(lane < 64, qf[k * 64 : (k + 1) * 64], w64)
        wl = w0 - w0.astype(bf16).astype(f32)
        hl = h96 - h96.astype(bf16).astype(f32)
        b = jnp.where(lane < 64, wl, jnp.where(lane < 96, h64, hl))
        b = jnp.where(used, b, 0.0)
        outs.append(jnp.concatenate([a, b], 1).astype(bf16))
    return jnp.concatenate(outs, 0)


def build_kaug(kT, kaug, flipped=False):
    KB = kT.shape[1]
    ck = min(512, KB)
    for c in range(KB // ck):
        kf = kT[:, c * ck : (c + 1) * ck].astype(f32) * 0.125
        kf = jnp.concatenate([kf, jnp.zeros((64, ck), f32)], 0).T
        n = iota((ck, 128), 0) + c * ck
        lane = iota((ck, 128), 1)
        col, row = n & 63, n >> 6
        spot = 127 - col if flipped else 64 + col
        a = jnp.where(lane < 64, kf, (lane == spot).astype(f32))
        b = jnp.where(lane < 64, (lane == col).astype(f32), ((lane & 31) == row).astype(f32))
        kaug[c * ck : (c + 1) * ck, :] = jnp.concatenate([a, b], 1).astype(bf16)


def build_kaugT(kT, kaugT):
    KB = kT.shape[1]
    ck = min(512, KB)
    for c in range(KB // ck):
        f = iota((64, ck), 0)
        n = iota((64, ck), 1) + c * ck
        col, row = n & 63, n >> 6
        sl = slice(c * ck, (c + 1) * ck)
        kaugT[0:64, sl] = (kT[:, sl].astype(f32) * 0.125).astype(bf16)
        oc = (f == col).astype(f32).astype(bf16)
        kaugT[64:128, sl] = oc
        kaugT[128:192, sl] = oc
        kaugT[192:256, sl] = ((f & 31) == row).astype(f32).astype(bf16)


def fwd_kernel(sc_ref, qT_ref, tab_ref, *rest, R, bk, first, last, nt, n):
    kvs, rest = rest[:n], rest[n:]
    if first:
        rest = (None, None) + rest
    oi_ref, mli_ref, o_ref, ml_ref, *rest = rest
    KB = kvs[0].shape[1]
    bq = qT_ref.shape[1]
    hi, qi = pl.program_id(0), pl.program_id(1)
    if last:
        kaug, vaug, och = rest[-3:]
    else:
        kaug, vaug = rest[-2:]

    for g, kv in enumerate(kvs):

        @pl.when((qi == 0) & (hi == g))
        def _(kv=kv):
            build_kaug(kv[0:64, :], kaug)
            vaug[0:64, :] = kv[64:128, :]
            vaug[64:80, :] = (iota((16, KB), 0) == 0).astype(f32).astype(bf16)

    qaug = make_qaug(qT_ref[...], tab_ref[:, :256], qi * (bq // 64), sc_ref[0], R)
    if first:
        m = jnp.full((1, bq), -3e38, f32)
        o = jnp.zeros((80, bq), f32)
    else:
        m = mli_ref[0:1, :]
        o = jnp.concatenate([oi_ref[...], jnp.broadcast_to(mli_ref[1:2, :], (16, bq))], 0)
    for c in range(KB // bk):
        s = dot(kaug[c * bk : (c + 1) * bk, :], qaug, 1, 1)
        mn = jnp.maximum(m, jnp.max(s, axis=0, keepdims=True))
        al = jnp.exp(m - mn)
        p = jnp.exp(s - mn).astype(bf16)
        o = o * al + jnp.dot(vaug[:, c * bk : (c + 1) * bk], p, preferred_element_type=f32)
        m = mn
    l = o[64:65, :]
    o = o[:64]
    if last:
        o = o * (1.0 / l)
        m = m + jnp.log(l)
        N = och.shape[2]
        ob = o.astype(bf16)
        for j in range(bq // N):
            och[qi * (bq // N) + j] = ob[:, j * N : (j + 1) * N]

        @pl.when(qi == pl.num_programs(1) - 1)
        def _():
            for k in range(nt):
                rest[k][...] = och[sc_ref[1] ^ k]

    o_ref[...] = o
    ml_ref[...] = jnp.concatenate([m, l, jnp.zeros((6, bq), f32)], 0)


def attn_fwd(sc, h0, qT, kvs, tab, state, last, R, nt, bq=2048, bk=512):
    H, _, T = qT.shape
    n = len(kvs)
    KB = kvs[0].shape[1]
    N = T // nt
    bq, bk = min(bq, T), min(bk, KB)
    first = state is None
    qs = lambda r: pl.BlockSpec((None, r, bq), lambda h, i, o: (h0 + h, 0, i))
    ins = [qs(64), pl.BlockSpec((64, 384), lambda h, i, o: (0, 0))]
    ins += [pl.BlockSpec((128, KB), lambda h, i, o: (0, 0))] * n
    ins += [] if first else [qs(64), qs(8)]
    outs = [qs(64), qs(8)]
    shapes = [jax.ShapeDtypeStruct((H, 64, T), f32), jax.ShapeDtypeStruct((H, 8, T), f32)]
    scratch = [pltpu.VMEM((KB, 256), bf16), pltpu.VMEM((80, KB), bf16)]
    if last:
        outs += [pl.BlockSpec((64, N), lambda h, i, o: (h, 0))] * nt
        shapes += [jax.ShapeDtypeStruct((n * 64, N), bf16)] * nt
        scratch += [pltpu.VMEM((nt, 64, N), bf16)]
    return pl.pallas_call(
        functools.partial(fwd_kernel, R=R, bk=bk, first=first, last=last, nt=nt, n=n),
        grid_spec=pltpu.PrefetchScalarGridSpec(
            num_scalar_prefetch=1,
            grid=(n, T // bq),
            in_specs=ins,
            out_specs=outs,
            scratch_shapes=scratch,
        ),
        out_shape=shapes,
        input_output_aliases={} if first else {3 + n: 0, 4 + n: 1},
        compiler_params=pltpu.CompilerParams(vmem_limit_bytes=VMEM),
        cost_estimate=pl.CostEstimate(
            flops=2 * n * T * KB * 512, bytes_accessed=n * T * 1200, transcendentals=n * T * KB
        ),
        name="attn_fwd",
    )(sc, qT, tab, *kvs, *([] if first else state))


def bwd_kernel(sc_ref, qT_ref, tab_ref, *rest, R, bk, has_dq, has_dt, last, nt, n):
    kvs, rest = rest[:n], rest[n:]
    do_refs, rest = rest[:nt], rest[nt:]
    o_ref, ml_ref, *rest = rest
    dqi_ref = dti_ref = dki_ref = None
    if has_dq:
        dqi_ref, *rest = rest
    if has_dt:
        dti_ref, *rest = rest
    if last:
        dki_ref, *rest = rest
        dx_refs, rest = rest[:nt], rest[nt:]
        dt_ref, kaug, kaugT, vaug, acc, dch, fin = rest
    else:
        dq_ref, dkv_ref, dt_ref, kaug, kaugT, vaug, acc, dch = rest
    KB = kvs[0].shape[1]
    bq = qT_ref.shape[1]
    N = dch.shape[2]
    per = bq // N
    hi, qi = pl.program_id(0), pl.program_id(1)

    for g, kv in enumerate(kvs):

        @pl.when((qi == 0) & (hi == g))
        def _(kv=kv):
            build_kaug(kv[0:64, :], kaug, True)
            build_kaugT(kv[0:64, :], kaugT)
            vaug[0:64, :] = kv[64:128, :]
            vaug[64:128, :] = (iota((64, KB), 0) < 3).astype(f32).astype(bf16)

    @pl.when(qi == 0)
    def _():
        if last:
            acc[0:64, :] = dki_ref[0:64, :].astype(f32) * 8.0
            acc[64:128, :] = dki_ref[64:128, :].astype(f32)
        else:
            acc[...] = jnp.zeros_like(acc)
        for k in range(nt):
            dch[sc_ref[1] ^ k] = do_refs[k][...]

    @pl.when((qi == 0) & (hi == 0))
    def _():
        dt_ref[...] = dti_ref[...] if has_dt else jnp.zeros_like(dt_ref)

    qT = qT_ref[...]
    doT = jnp.concatenate([dch[qi * per + j] for j in range(per)], 1)
    il0 = qi * (bq // 64)
    off = sc_ref[0]
    qaug = make_qaug(qT, tab_ref[:, :256], il0, off, R)
    dof = doT.astype(f32)
    nd = -jnp.sum(dof * o_ref[...], axis=0, keepdims=True)
    d1 = nd.astype(bf16).astype(f32)
    d2 = (nd - d1).astype(bf16).astype(f32)
    d3 = nd - d1 - d2
    rid = iota((64, bq), 0)
    ext = jnp.where(rid == 2, d3, jnp.where(rid == 3, ml_ref[0:1, :], 0.0))
    ext = jnp.where(rid == 0, d1, jnp.where(rid == 1, d2, ext))
    t = jnp.concatenate([dof, ext], 0).T
    lse = t[:, 67:68]
    doaug = t.astype(bf16)
    dq = jnp.zeros((bq, 256), f32)
    for c in range(KB // bk):
        sl = slice(c * bk, (c + 1) * bk)
        s = jnp.dot(qaug, kaugT[:, sl], preferred_element_type=f32)
        p = jnp.exp(s - lse)
        dp = jnp.dot(doaug, vaug[:, sl], preferred_element_type=f32)
        pb = p.astype(bf16)
        ds = (p * dp).astype(bf16)
        acc[64:128, sl] += jnp.dot(doT, pb, preferred_element_type=f32)
        acc[0:64, sl] += jnp.dot(qT, ds, preferred_element_type=f32)
        dq += jnp.dot(ds, kaug[sl, :], preferred_element_type=f32)
    lane = iota((64, 128), 1)
    his, los = [], []
    for k in range(bq // 64):
        a = dq[k * 64 : (k + 1) * 64, :128]
        b = dq[k * 64 : (k + 1) * 64, 128:]
        gw = pltpu.roll(jnp.where(lane >= 64, a, 0.0), 64, 1, stride=1, stride_axis=0)
        sh = off - (il0 + k) - 1
        gh = pltpu.roll(
            jnp.where((lane >= 64) & (lane < 64 + R), b, 0.0), lax.rem(sh + 256, 128), 1
        )
        g = jnp.concatenate([gh, gw], 1)
        h = g.astype(bf16)
        his.append(h)
        los.append((g - h.astype(f32)).astype(bf16))
    gh = jnp.concatenate(his, 0)
    gl = jnp.concatenate(los, 0)
    tab = jnp.concatenate([tab_ref[:, :128], tab_ref[:, 256:]], 1)
    dqT = dq[:, :128].T[:64] + dot(tab, gh, 1, 1) + dot(tab, gl, 1, 1)
    if has_dq:
        dqT = dqT + dqi_ref[...]
    dt_ref[...] += dot(qT, gh, 1, 0) + dot(qT, gl, 1, 0)
    if last:
        dqb = dqT.astype(bf16)
        for j in range(per):
            fin[qi * per + j, 0:64, :] = dqb[:, j * N : (j + 1) * N]
    else:
        dq_ref[...] = dqT

    @pl.when(qi == pl.num_programs(1) - 1)
    def _():
        if last:
            for j in range(nt):
                fin[j, 64:128, :] = (acc[0:64, j * N : (j + 1) * N] * 0.125).astype(bf16)
                fin[j, 128:192, :] = acc[64:128, j * N : (j + 1) * N].astype(bf16)
            for k in range(nt):
                dx_refs[k][...] = fin[sc_ref[1] ^ k]
        else:
            dkv_ref[0:64, :] = (acc[0:64, :] * 0.125).astype(bf16)
            dkv_ref[64:128, :] = acc[64:128, :].astype(bf16)


def attn_bwd(sc, h0, qT, kvs, tab, dos, o, ml, dq, dt, back, R, bq=2048, bk=512):
    _, _, T = qT.shape
    n = len(kvs)
    KB = kvs[0].shape[1]
    nt = len(dos)
    N = T // nt
    bq, bk = min(bq, T), min(bk, KB)
    last = back is not None
    qs = lambda r, h0=h0: pl.BlockSpec((None, r, bq), lambda h, i, s: (h0 + h, 0, i))
    fix = lambda shape: pl.BlockSpec(shape, lambda h, i, s: (0, 0))
    ins = [qs(64), fix((64, 384))] + [fix((128, KB))] * n
    ins += [pl.BlockSpec((64, N), lambda h, i, s: (h0 + h, 0))] * nt + [qs(64), qs(8)]
    args = [qT, tab, *kvs, *dos, o, ml]
    if dq is not None:
        ins += [qs(64, dq[1])]
        args += [dq[0]]
    if dt is not None:
        ins += [fix((64, 256))]
        args += [dt]
    scratch = [
        pltpu.VMEM((KB, 256), bf16),
        pltpu.VMEM((256, KB), bf16),
        pltpu.VMEM((128, KB), bf16),
        pltpu.VMEM((128, KB), f32),
        pltpu.VMEM((nt, 64, N), bf16),
    ]
    if last:
        ins += [pl.BlockSpec((None, 128, KB), lambda h, i, s: (back[1], 0, 0))]
        args += [back[0]]
        outs = [fix((192, N))] * nt
        shapes = [jax.ShapeDtypeStruct((192, N), bf16)] * nt
        scratch += [pltpu.VMEM((nt, 192, N), bf16)]
    else:
        outs = [qs(64, 0), pl.BlockSpec((None, 128, KB), lambda h, i, s: (h, 0, 0))]
        shapes = [jax.ShapeDtypeStruct((n, 64, T), f32), jax.ShapeDtypeStruct((n, 128, KB), bf16)]
    return pl.pallas_call(
        functools.partial(
            bwd_kernel, R=R, bk=bk, has_dq=dq is not None, has_dt=dt is not None, last=last,
            nt=nt, n=n,
        ),
        grid_spec=pltpu.PrefetchScalarGridSpec(
            num_scalar_prefetch=1,
            grid=(n, T // bq),
            in_specs=ins,
            out_specs=outs + [fix((64, 256))],
            scratch_shapes=scratch,
        ),
        out_shape=shapes + [jax.ShapeDtypeStruct((64, 256), f32)],
        compiler_params=pltpu.CompilerParams(vmem_limit_bytes=VMEM),
        cost_estimate=pl.CostEstimate(
            flops=(2 if dt is not None else 40) * n * T * KB * 1280, bytes_accessed=n * T * 3000, transcendentals=n * T * KB
        ),
        name="attn_bwd",
    )(sc, *args)


def rows_of(sc_ref, r, dd):
    return pl.ds(pl.multiple_of((sc_ref[2] ^ r) * dd, dd), dd)


def whole_spec(shape):
    return pl.BlockSpec(shape, lambda *_: (0,) * len(shape))


def norm_parts(x):
    c = x - jnp.mean(x, axis=-1, keepdims=True)
    r = lax.rsqrt(jnp.mean(c * c, axis=-1, keepdims=True) + EPS)
    return c * r, r


def norm_back(dh, gain, xhat, r):
    e = dh * gain
    return (
        e - jnp.mean(e, axis=-1, keepdims=True) - xhat * jnp.mean(e * xhat, axis=-1, keepdims=True)
    ) * r


def call(kernel, sc, grid, ins, args, outs, shapes, scratch, name, flops, nbytes):
    return pl.pallas_call(
        kernel,
        grid_spec=pltpu.PrefetchScalarGridSpec(
            num_scalar_prefetch=1, grid=grid, in_specs=ins, out_specs=outs, scratch_shapes=scratch
        ),
        out_shape=[jax.ShapeDtypeStruct(s, d) for s, d in shapes],
        compiler_params=pltpu.CompilerParams(vmem_limit_bytes=VMEM),
        cost_estimate=pl.CostEstimate(flops=flops, bytes_accessed=nbytes, transcendentals=0),
        name=name,
    )(sc, *args)


def pack_kernel(sc_ref, w, rh, rw, n1g, n1b, n2g, n2b, pb, ob, qb, out):
    dd, E3 = w.shape[1], 3 * w.shape[2]
    for h in range(E3 // 192):
        cols = [w[j, :, h * 64 : (h + 1) * 64].astype(f32) for j in range(3)]
        out[0:dd, h * 192 : (h + 1) * 192] = jnp.concatenate(cols, 1).astype(bf16)
    out[dd:, :] = jnp.zeros((32, E3), bf16)
    L = rh.shape[1]
    t, l = iota((L, 128), 0), iota((L, 128), 1)
    back = (t == L - 1 - l).astype(f32).astype(bf16)
    same = (t == l).astype(f32).astype(bf16)
    out[dd : dd + 16, 0:128] = dot(rh[...], back, 1, 0).astype(bf16)
    out[dd : dd + 16, 128:256] = dot(rw[...], back, 1, 0).astype(bf16)
    out[dd : dd + 16, 256:384] = dot(rw[...], same, 1, 0).astype(bf16)
    rows = [v[...].astype(f32).reshape(1, dd) for v in (n1g, n1b, n2g, n2b, pb, ob)]
    rows = jnp.concatenate(rows + [jnp.zeros((10, dd), f32)], 0)
    out[dd + 16 :, 0:dd] = rows.astype(bf16)
    q = [qb[h].astype(f32) for h in range(qb.shape[0])]
    q = jnp.concatenate(q + [jnp.zeros((16 - 2 * len(q), 16), f32)], 0)
    out[dd + 16 :, 256:272] = q.astype(bf16)


def front_kernel(sc_ref, x_ref, s0, s1, s2, s3, tab_ref, v_ref, q_ref, *rest, H):
    kvs, (wt_ref, xh_ref, wn, all4, bias) = rest[:H], rest[H:]
    dd = s0.shape[0] - 32

    @pl.when(pl.program_id(0) == 0)
    def _():
        for r, s in enumerate((s0, s1, s2, s3)):
            all4[sc_ref[2] ^ r] = s[dd:, :]
            wn[rows_of(sc_ref, r, dd), :] = s[0:dd, :]
        wt_ref[...] = wn[...].T
        for j in range(4):
            tab_ref[j * 16 : (j + 1) * 16, :] = all4[j, 0:16, 0:384]
        low = [all4[j, 16:32, :].astype(f32) for j in range(4)]
        v_ref[...] = jnp.concatenate([z[0:8, 0:dd] for z in low], 1)
        q = jnp.concatenate([z[:, 256:272] for z in low] + [jnp.zeros((16, 64), f32)], 1)
        q = q.T[0:64]
        for h in range(H):
            bias[h * 192 : h * 192 + 64, :] = q[:, 2 * h : 2 * h + 1]
            bias[h * 192 + 64 : h * 192 + 128, :] = jnp.zeros((64, 1), f32)
            bias[h * 192 + 128 : (h + 1) * 192, :] = q[:, 2 * h + 1 : 2 * h + 2]

    xh, _ = norm_parts(x_ref[...].astype(f32))
    xh_ref[...] = xh.astype(bf16)
    h1 = (xh * v_ref[0:1, :] + v_ref[1:2, :]).astype(bf16)
    y = dot(wt_ref[...], h1, 1, 1) + bias[...]
    y = y.astype(bf16)
    for h in range(H):
        q_ref[h] = y[h * 192 : h * 192 + 64]
        kvs[h][...] = y[h * 192 + 64 : (h + 1) * 192]


def front(sc, x, ss, H):
    T, D = x.shape
    E3 = H * 192
    bt = min(512, T)
    rows = pl.BlockSpec((bt, D), lambda i, s: (i, 0))
    return call(
        functools.partial(front_kernel, H=H), sc, (T // bt,),
        [rows] + [whole_spec(ss[0].shape)] * 4, [x, *ss],
        [whole_spec((64, 384)), whole_spec((8, D))]
        + [pl.BlockSpec((H, 64, bt), lambda i, s: (0, 0, i))]
        + [pl.BlockSpec((128, bt), lambda i, s: (0, i))] * H
        + [whole_spec((E3, D)), rows],
        [((64, 384), bf16), ((8, D), f32), ((H, 64, T), bf16)]
        + [((128, T), bf16)] * H
        + [((E3, D), bf16), ((T, D), bf16)],
        [pltpu.VMEM((D, E3), bf16), pltpu.VMEM((4, 32, E3), bf16), pltpu.VMEM((E3, 1), f32)],
        "front", 2 * T * D * E3, 6 * T * D,
    )


def mlpa_kernel(sc_ref, x_ref, v_ref, *rest, nt, fb):
    no = 2 * nt
    os, ps, p1, rest = rest[:no], rest[no : no + 4], rest[no + 4 : no + 8], rest[no + 8 :]
    a_ref, sl_ref, h2_ref, y1_ref, wt_ref, wp, b4, bias, wi = rest
    dd, ft = p1[0].shape
    D = 4 * dd
    k = pl.program_id(0)

    @pl.when(k == 0)
    def _():
        y = x_ref[...].astype(f32) + v_ref[4:5, :]
        na = os[0].shape[0]
        for kk in range(nt):
            for r in range(4):
                wp[rows_of(sc_ref, r, dd), :] = ps[r][kk, 0:dd]
            wt = wp[...].T
            wt_ref[kk] = wt
            y = y + dot(os[kk][...], wt[:na], 0, 0)
            y = y + dot(os[nt + kk][...], wt[na:], 0, 0)
        y1_ref[...] = y
        xh, _ = norm_parts(y)
        h2_ref[...] = (xh * v_ref[2:3, :] + v_ref[3:4, :]).astype(bf16)

    assemble(sc_ref, wi, p1)
    for r in range(4):
        b4[sc_ref[2] ^ r] = ps[r][k, dd:, :].astype(f32)
    rows = jnp.concatenate([b4[j, :, 0:16] for j in range(4)], 1)
    for i in range(ft // 64):
        bias[:, i * 64 : (i + 1) * 64] = rows[i : i + 1]
    for j in range(ft // fb):
        sl = slice(j * fb, (j + 1) * fb)
        u = jnp.dot(h2_ref[...], wi[:, sl], preferred_element_type=f32) + bias[:, sl]
        cdf = 0.5 + 0.5 * lax.erf(u * 0.7071067811865476)
        a_ref[:, sl] = (u * cdf).astype(bf16)
        slope = cdf + u * (jnp.exp(-0.5 * u * u) * 0.3989422804014327)
        sl_ref[:, sl] = slope.astype(sl_ref.dtype)


def piece_specs(w):
    n2, dd, cols = w[0].shape
    at = lambda add: pl.BlockSpec((None, dd, cols), lambda k, s: (add + (s[1] ^ k), 0, 0))
    return [at(0), at(0), at(n2 // 2), at(n2 // 2)]


def pieces(w):
    return [w[0], w[1], w[0], w[1]]


def assemble(sc_ref, whole, parts):
    for r, p in enumerate(parts):
        whole[rows_of(sc_ref, r, p.shape[0]), :] = p[...]


def mlpa(sc, x, vecs, os, ps, p1):
    D = x.shape[1]
    nt, ft = ps[0].shape[0], p1[0].shape[2]
    N = os[0].shape[1]
    kt = ps[0].shape[2]
    mine = pl.BlockSpec((N, D), lambda k, s: (s[1], 0))
    act = pl.BlockSpec((None, N, ft), lambda k, s: (k, 0, 0))
    full = whole_spec((N, D))
    return call(
        functools.partial(mlpa_kernel, nt=nt, fb=256), sc, (nt,),
        [mine, whole_spec(vecs.shape)]
        + [whole_spec(o.shape) for o in os]
        + [whole_spec(p.shape) for p in ps]
        + piece_specs(p1),
        [x, vecs, *os, *ps, *pieces(p1)],
        [act, act, full, full, whole_spec((nt, kt, D))],
        [((nt, N, ft), bf16), ((nt, N, ft), f32), ((N, D), bf16), ((N, D), f32)]
        + [((nt, kt, D), bf16)],
        [pltpu.VMEM((D, kt), bf16), pltpu.VMEM((4, 16, kt), f32), pltpu.VMEM((1, ft), f32)]
        + [pltpu.VMEM((D, ft), bf16)],
        "mlp_in", 3 * N * D * ft * nt, 24 * 2**20,
    )


def mlpb_kernel(sc_ref, g_ref, v_ref, y1_ref, sl_ref, *rest, nt, fb):
    wt_ref, p1, p2, rest = rest[0], rest[1:5], rest[5:9], rest[9:]
    du_ref, da_ref, dy_ref, sm_ref, db_ref, *dos, dh, wi, wo = rest
    D, ft = wi.shape
    k = pl.program_id(0)

    @pl.when(k == 0)
    def _():
        dh[...] = jnp.zeros_like(dh)

    assemble(sc_ref, wo, p2)
    assemble(sc_ref, wi, p1)
    for j in range(ft // fb):
        sl = slice(j * fb, (j + 1) * fb)
        ga = jnp.dot(g_ref[...], wo[:, sl], preferred_element_type=f32)
        du = (sl_ref[:, sl] * ga).astype(bf16)
        du_ref[:, sl] = du
        db_ref[:, sl] = jnp.sum(du.astype(f32), axis=0, keepdims=True)
        dh[...] += dot(du, wi[:, sl], 1, 1)

    @pl.when(k == pl.num_programs(0) - 1)
    def _():
        g = g_ref[...].astype(f32)
        xh, r = norm_parts(y1_ref[...])
        d = dh[...]
        dy = g + norm_back(d, v_ref[2:3, :], xh, r)
        dy_ref[...] = dy
        da = dy.astype(bf16)
        da_ref[...] = da
        sums = [jnp.sum(z, axis=0, keepdims=True) for z in (d * xh, d, da.astype(f32), g)]
        sm_ref[...] = jnp.concatenate(sums + [jnp.zeros((4, D), f32)], 0)
        for kk in range(nt):
            dos[kk][...] = dot(wt_ref[kk], da, 1, 1).astype(bf16)


def mlpb(sc, g, vecs, y1, slope, wt, p1, p2):
    N, D = y1.shape
    nt, kt = wt.shape[:2]
    ft = p1[0].shape[2]
    act = pl.BlockSpec((None, N, ft), lambda k, s: (k, 0, 0))
    row = pl.BlockSpec((None, 1, ft), lambda k, s: (s[1] ^ k, 0, 0))
    full = whole_spec((N, D))
    return call(
        functools.partial(mlpb_kernel, nt=nt, fb=256), sc, (nt,),
        [pl.BlockSpec((N, D), lambda k, s: (s[1], 0)), whole_spec(vecs.shape), full, act]
        + [whole_spec(wt.shape)]
        + piece_specs(p1)
        + piece_specs(p2),
        [g, vecs, y1, slope, wt, *pieces(p1), *pieces(p2)],
        [act, full, full, whole_spec((8, D)), row] + [whole_spec((kt, N))] * nt,
        [((nt, N, ft), bf16), ((N, D), bf16), ((N, D), f32), ((8, D), f32), ((nt, 1, ft), f32)]
        + [((kt, N), bf16)] * nt,
        [pltpu.VMEM((N, D), f32)] + [pltpu.VMEM((D, ft), bf16)] * 2,
        "mlp_grad", 5 * N * D * ft * nt, 24 * 2**20,
    )


def mlp2_kernel(sc_ref, g_ref, v_ref, h2_ref, da_ref, y_ref, a_ref, du_ref, *rest, nt):
    no = 2 * nt
    os, p2, rest = rest[:no], rest[no : no + 4], rest[no + 4 :]
    gws, (out_ref, hT, gT, dT, oa, acc, acn, wo) = rest[:4], rest[4:]
    ft = a_ref.shape[1]
    D = h2_ref.shape[1]
    dd = D // 4
    k = pl.program_id(0)

    @pl.when(k == 0)
    def _():
        for src, dst in ((h2_ref, hT), (g_ref, gT), (da_ref, dT)):
            acn[...] = src[...].astype(f32).T
            for r in range(4):
                dst[r * dd : (r + 1) * dd, :] = acn[rows_of(sc_ref, r, dd), :].astype(bf16)
        na = os[0].shape[0]
        for kk in range(nt):
            oa[kk, :na] = os[kk][...]
            oa[kk, na:] = os[nt + kk][...]
        acc[...] = jnp.zeros_like(acc)

    a = a_ref[...]
    assemble(sc_ref, wo, p2)
    acc[...] += dot(a, wo[...], 1, 1)

    def store(value, lo, hi):
        value = value.astype(bf16)
        for r in range(4):
            gws[r][:, lo:hi] = value[r * dd : (r + 1) * dd]

    store(jnp.dot(hT[...], du_ref[...], preferred_element_type=f32), 0, ft)
    store(jnp.dot(gT[...], a, preferred_element_type=f32), ft, 2 * ft)
    store(dot(dT[...], oa[k], 1, 1), 2 * ft, gws[0].shape[1])

    @pl.when(k == pl.num_programs(0) - 1)
    def _():
        out_ref[...] = (y_ref[...] + (acc[...] + v_ref[5:6, :])).astype(bf16)


def mlp2(sc, g, vecs, h2, da, y1, a, du, os, p2):
    N, D = h2.shape
    nt, _, ft = a.shape
    dd = D // 4
    kt = os[0].shape[0] + os[nt].shape[0]
    cols = 2 * ft + kt
    full = whole_spec((N, D))
    act = pl.BlockSpec((None, N, ft), lambda k, s: (k, 0, 0))
    gw = pl.BlockSpec((None, dd, cols), lambda k, s: (s[1] ^ k, 0, 0))
    return call(
        functools.partial(mlp2_kernel, nt=nt), sc, (nt,),
        [pl.BlockSpec((N, D), lambda k, s: (s[1], 0)), whole_spec(vecs.shape), full, full, full]
        + [act, act]
        + [whole_spec(o.shape) for o in os]
        + piece_specs(p2),
        [g, vecs, h2, da, y1, a, du, *os, *pieces(p2)],
        [gw] * 4 + [full],
        [((nt, dd, cols), bf16)] * 4 + [((N, D), bf16)],
        [pltpu.VMEM((D, N), bf16)] * 3
        + [
            pltpu.VMEM((nt, kt, N), bf16),
            pltpu.VMEM((N, D), f32),
            pltpu.VMEM((D, N), f32),
            pltpu.VMEM((D, ft), bf16),
        ],
        "mlp_weights", 7 * N * D * ft * nt, 24 * 2**20,
    )


def gqkv_kernel(sc_ref, x_ref, v_ref, wt_ref, *rest, nt, H):
    dx, (keep_ref, send_ref, b_ref, n_ref, g) = rest[: H * nt], rest[H * nt :]
    dd = keep_ref.shape[1]
    lane = iota((192, 128), 1)
    gain, shift = v_ref[0:1, :], v_ref[1:2, :]
    dg, db = jnp.zeros_like(gain), jnp.zeros_like(gain)
    for h in range(H):
        t = jnp.zeros((192, x_ref.shape[2]), f32)
        b = jnp.zeros((192, 1), f32)
        for k in range(nt):
            d = dx[h * nt + k][...]
            t = t + jnp.dot(d, x_ref[sc_ref[1] ^ k], preferred_element_type=f32)
            b = b + jnp.sum(d.astype(f32), axis=1, keepdims=True)
        w = wt_ref[h * 192 : (h + 1) * 192, :].astype(f32)
        dg = dg + jnp.sum(w * t, axis=0, keepdims=True)
        db = db + jnp.sum(w * b, axis=0, keepdims=True)
        g[:, h * 192 : (h + 1) * 192] = (t * gain + shift * b).T.astype(bf16)
        b_ref[h] = jnp.where(lane == 0, b, 0.0)
    n_ref[...] = jnp.concatenate([dg, db, jnp.zeros((6, dg.shape[1]), f32)], 0)
    for r in range(4):
        dst = send_ref if r & 1 else keep_ref
        dst[r // 2] = g[rows_of(sc_ref, r, dd), :]


def gqkv(sc, xh, vecs, wT, dx, nt):
    T, D = xh.shape
    H = len(dx) // nt
    N = T // nt
    dd = D // 4
    part = (2, dd, H * 192)
    return call(
        functools.partial(gqkv_kernel, nt=nt, H=H), sc, (1,),
        [whole_spec((nt, N, D)), whole_spec(vecs.shape), whole_spec(wT.shape)]
        + [whole_spec((192, N))] * len(dx),
        [xh.reshape(nt, N, D), vecs, wT, *dx],
        [whole_spec(part), whole_spec(part), whole_spec((H, 192, 128)), whole_spec((8, D))],
        [(part, bf16), (part, bf16), ((H, 192, 128), f32), ((8, D), f32)],
        [pltpu.VMEM((D, H * 192), bf16)],
        "qkv_weights", 2 * T * D * 192 * H, 8 * 2**20,
    )


def dh1_kernel(sc_ref, x_ref, dy_ref, v_ref, *rest, nt, H):
    dx, (p3, gi_ref, da) = rest[: H * nt], rest[H * nt :]
    D = x_ref.shape[1]
    E3 = H * 192
    for k in range(nt):
        for h in range(H):
            da[(k * H + h) * 192 : (k * H + h + 1) * 192, :] = dx[h * nt + k][...]
    t = jnp.zeros((D, da.shape[1]), f32)
    for k in range(nt):
        w = p3[:, sc_ref[1] ^ k].reshape(D, E3)
        t = t + jnp.dot(w, da[k * E3 : (k + 1) * E3, :], preferred_element_type=f32)
    xh, r = norm_parts(x_ref[...].astype(f32))
    gi_ref[...] = (dy_ref[...] + norm_back(t.T, v_ref[0:1, :], xh, r)).astype(bf16)


def dh1(sc, x, dy1, vecs, dx, p3):
    N, D = dy1.shape
    nt = p3.shape[1]
    H = len(dx) // nt
    return call(
        functools.partial(dh1_kernel, nt=nt, H=H), sc, (1,),
        [pl.BlockSpec((N, D), lambda k, s: (s[1], 0)), whole_spec((N, D)), whole_spec(vecs.shape)]
        + [whole_spec((192, N))] * len(dx)
        + [whole_spec(p3.shape)],
        [x, dy1, vecs, *dx, p3],
        [whole_spec((N, D))],
        [((N, D), bf16)],
        [pltpu.VMEM((nt * H * 192, N), bf16)],
        "norm1_grad", 2 * N * D * D * 3, 8 * 2**20,
    )[0]


def copy_kernel(sc_ref, a, b):
    b[...] = a[...].astype(b.dtype)


def copied(sc, v, dtype):
    rows = pl.BlockSpec((v.shape[0] // 4, v.shape[1]), lambda i, s: (i, 0))
    return call(
        copy_kernel, sc, (4,), [rows], [v], [rows], [(v.shape, dtype)], [], "copied", 0, 2**22
    )[0]


def shift(value, axis, steps):
    n = lax.axis_size(axis)
    return lax.ppermute(value, axis, [(s, (s + steps) % n) for s in range(n)])


def flip(value, axis, bit):
    n = lax.axis_size(axis)
    return lax.ppermute(value, axis, [(s, s ^ bit) for s in range(n)])


def after(value, *others):
    return lax.optimization_barrier((value, *others))[0]


def gather_weights(shard):
    nd, nt = lax.axis_size("dp"), lax.axis_size("tensor")
    return lax.all_gather(shard, ("dp", "tensor")).reshape((nd, nt) + shard.shape)


def spread(parts):
    return [parts[0]] + [flip(p, "tensor", k) for k, p in enumerate(parts) if k]


def total_ctx(value):
    v = value.astype(bf16)
    if lax.axis_size("ctx") == 2:
        return v.astype(f32) + flip(v, "ctx", 1).astype(f32)
    return lax.psum(v.astype(f32), "ctx")


def per_device(
    block_input,
    cotangent,
    norm1_gain,
    norm1_bias,
    qkv_weight,
    qkv_bias,
    rel_pos_h,
    rel_pos_w,
    proj_weight,
    proj_bias,
    norm2_gain,
    norm2_bias,
    mlp_in_weight,
    mlp_in_bias,
    mlp_out_weight,
    mlp_out_bias,
):
    nt, nc = lax.axis_size("tensor"), lax.axis_size("ctx")
    me, pos, dp = lax.axis_index("tensor"), lax.axis_index("ctx"), lax.axis_index("dp")
    T, D = block_input.shape[1:]
    R = T // GW
    dd = D // 4
    N = T // nt
    H = qkv_bias.shape[1]
    E = H * HD
    L = rel_pos_h.shape[0]
    ft = mlp_in_weight.shape[1]
    x2 = block_input.reshape(T, D)
    g2 = cotangent.reshape(T, D)

    def scalars(k):
        off = (((pos - k) % nc) - pos) * R
        return jnp.stack([off, me, dp]).astype(jnp.int32)

    sc = scalars(0)
    bar = lax.optimization_barrier

    smalls = [qkv_weight.transpose(1, 0, 2), rel_pos_h.T, rel_pos_w.T]
    smalls += [norm1_gain, norm1_bias, norm2_gain, norm2_bias, proj_bias, mlp_out_bias]
    smalls += [qkv_bias.transpose(1, 0, 2)]
    small = call(
        pack_kernel, sc, (1,), [whole_spec(v.shape) for v in smalls], smalls,
        [whole_spec((dd + 32, 3 * E))], [((dd + 32, 3 * E), bf16)], [], "pack", 0, 2**16,
    )[0]
    p1 = lax.all_gather(mlp_in_weight, "tensor", axis=0)
    p2 = lax.all_gather(mlp_out_weight.T, "tensor", axis=0)
    brow = jnp.pad(mlp_in_bias, ((0, 16 - mlp_in_bias.shape[0]), (0, E - 16)))
    own = jnp.concatenate([proj_weight.T, brow], 0)
    near = flip(own, "tensor", 1)
    small = [small] + [flip(small, "dp", r) for r in (1, 2, 3)]
    near, small = bar((near, small))
    own = jnp.stack([own, near])
    two = flip(own, "tensor", 2)

    tab, vecs, qT, *rest = front(sc, x2, small, H)
    kvs, (wT, xh1) = rest[:H], rest[H:]
    kv_far = [[shift(kv, "ctx", k) for kv in kvs] for k in range(1, nc)]

    state = attn_fwd(sc, 0, qT, kvs, tab, None, False, R, nt)
    state, two, p1 = bar((state, two, p1))
    p1x = flip(p1, "dp", 2)
    own = jnp.concatenate([own, two])
    far = flip(own, "dp", 2)
    for k in range(1, nc - 1):
        state = attn_fwd(scalars(k), 0, qT, kv_far[k - 1], tab, state, False, R, nt)
    os = []
    for h0, h1 in ((0, H - 1), (H - 1, H)):
        *state, o0, o1, o2, o3 = attn_fwd(
            scalars(nc - 1), h0, qT, kv_far[-1][h0:h1], tab, state, True, R, nt
        )
        if h0 == 0:
            state, far, p2 = bar((state, far, p2))
            p2x = flip(p2, "dp", 2)
            ps = [own, flip(own, "dp", 1), far, flip(far, "dp", 1)]
        else:
            o0, ps, p1, p1x, os = bar((o0, ps, p1, p1x, os))
            p1 = jnp.concatenate([p1, p1x])
            p1 = (p1, flip(p1, "dp", 1))
        os += spread([o0, o1, o2, o3])
    o32, lse = state
    os, p2x = bar((os, p2x))
    p2 = jnp.concatenate([p2, p2x])
    p2 = (p2, flip(p2, "dp", 1))
    p3 = gather_weights(after(small[0], *os)[:dd])
    a, slope, h2, y1, wt = mlpa(sc, x2, vecs, os, ps, p1)
    du, da, dy1, sm2, dbin, *dos = mlpb(sc, g2, vecs, y1, slope, wt, p1, p2)
    dos = spread(dos)
    *gws, out = mlp2(sc, g2, vecs, h2, da, y1, a, du, os, p2)

    add = lambda *v: sum(z.astype(f32) for z in v).astype(bf16)
    out, dos, p3 = bar((out, dos, p3))
    core = [flip(gws[1], "dp", 1), flip(gws[3], "dp", 1)]
    halves = nc == 2
    part = lambda v, i: lax.dynamic_index_in_dim(
        v.reshape(v.shape[:-2] + (2, dd // 2, v.shape[-1])), i, v.ndim - 2, keepdims=False
    )
    dtab = None
    dqs, backs = [], []
    for h0, h1 in ((0, 1), (1, H)):
        back, dq = None, None
        for k in range(1, nc):
            dq, dkv, dtab = attn_bwd(
                scalars(k), h0, qT, kv_far[k - 1][h0:h1], tab, dos, o32, lse, dq, dtab, None, R
            )
            dq = (dq, 0)
            dkv = shift(dkv, "ctx", -k)
            back = dkv if back is None else add(back, dkv)
        dqs += [(dq[0], i) for i in range(h1 - h0)]
        backs += [(back, i) for i in range(h1 - h0)]
        if h0 == 0:
            dtab, core = bar((dtab, core))
            pair = [add(gws[0], core[0]), add(gws[2], core[1])]
            if halves:
                xa = flip(pair[1][: nt // 2], "dp", 2)
                low = jnp.concatenate([z[nt // 2 :] for z in pair])
                yb = flip(part(low, 1 - pos), "ctx", 1)
            else:
                xa = flip(pair[1], "dp", 2)
    block_out = lax.all_gather(out.reshape(1, N, D), "tensor", axis=1, tiled=True)
    if halves:
        dtab, xa, yb = bar((dtab, xa, yb))
        va = add(pair[0][: nt // 2], xa)
        vb = add(part(low, pos), yb)
        ya = flip(part(va, 1 - pos), "ctx", 1)
        xb = flip(vb[nt // 2 :], "dp", 2)
    else:
        dtab, xa = bar((dtab, xa))
        v = add(pair[0], xa)
    dx, dxr = [], []
    for h in range(H):
        *d, dtab = attn_bwd(
            sc, h, qT, kvs[h : h + 1], tab, dos, o32, lse, dqs[h], dtab, backs[h], R
        )
        dx += d
        if h == 0 and halves:
            dtab, xb = bar((dtab, xb))
        if h == 1:
            if halves:
                dtab, ya = bar((dtab, ya))
                v = jnp.concatenate([add(part(va, pos), ya), add(vb[: nt // 2], xb)])
            dtab, dxr, v, block_out = bar((dtab, dxr, v, block_out))
        if h == 2:
            dtab, dxr, xh1 = bar((dtab, dxr, xh1))
        dxr = dxr + spread(d)
    gsum = lax.psum_scatter(v, "tensor", scatter_dimension=0)

    keepq, sendq, bq, sm1 = gqkv(sc, xh1, vecs, wT, dx, nt)

    tid = jnp.arange(nt)
    bq = bq[:, :, 0].reshape(H, 3, HD)
    bq = jnp.stack([bq[:, 0], bq[:, 2]]).reshape(1, 2 * E)
    bq = jnp.where(tid[:, None] == me, bq, 0.0)
    flat = jnp.concatenate(
        [z.reshape(-1, 256) for z in (sm2[:4], sm1[:2], dbin, bq)] + [dtab]
    )
    flat, sendq, dxr = bar((flat, sendq, dxr))
    flats = [flat] + [flip(flat, "tensor", k) for k in range(1, nt)]

    gin = dh1(sc, x2, dy1, vecs, dxr, p3)
    gin, sendq, flats = bar((gin, sendq, flats))
    gall = lax.all_gather(gin, "tensor", axis=0, tiled=True)
    while len(flats) > 1:
        flats = [flats[i] + flats[i + 1] for i in range(0, len(flats), 2)]
    flat = flats[0] + flip(flats[0], "dp", 1)
    flat = flat + flip(flat, "dp", 2)
    flat = flat + flip(flat, "ctx", 1) if nc == 2 else lax.psum(flat, "ctx")

    coreq = flip(sendq, "dp", 1)
    if halves:
        gsum = gsum.astype(bf16)
        other = flip(gsum, "ctx", 1)
        gmine = jnp.concatenate(
            [jnp.where(pos == 0, gsum, other), jnp.where(pos == 0, other, gsum)], 0
        ).astype(f32)
    else:
        gmine = total_ctx(gsum)
    g_in = gmine[:, :ft]
    g_out = gmine[:, ft : 2 * ft].T
    g_proj = gmine[:, 2 * ft :].T
    farq = flip(add(keepq[1], coreq[1]), "dp", 2)
    gq = total_ctx(add(keepq[0], coreq[0], farq))
    g_qkv = gq.reshape(dd, H, 3, HD).transpose(0, 2, 1, 3).reshape(dd, 3, E)

    vec = flat[: 6 * D // 256].reshape(6, 4, dd)
    vec = lax.dynamic_index_in_dim(vec, dp, 1, keepdims=False)
    at = 6 * D // 256
    gb = flat[at : at + nt * ft // 256].reshape(nt, ft // 64, 4, 16)
    gb = lax.dynamic_index_in_dim(gb, me, 0, keepdims=False)
    gb = lax.dynamic_index_in_dim(gb, dp, 1, keepdims=False)
    at += nt * ft // 256
    gbq = flat[at : at + nt * 2 * E // 256].reshape(nt, 2, H, 4, 16)
    gbq = lax.dynamic_index_in_dim(gbq, me, 0, keepdims=False)
    gbq = lax.dynamic_index_in_dim(gbq, dp, 2, keepdims=False)
    at += nt * 2 * E // 256
    gtab = lax.dynamic_index_in_dim(flat[at:].reshape(4, 16, 2, 128), dp, 0, keepdims=False)
    gtab_h, gtab_w = gtab[:, 0, :L][:, ::-1].T, gtab[:, 1, :L].T
    block_out = copied(sc, after(block_out, gin).reshape(T, D), bf16)
    gall, vec, block_out, g_qkv, gbq, gtab_h, gtab_w, gb, g_in, g_out, g_proj = bar(
        (gall, vec, block_out, g_qkv, gbq, gtab_h, gtab_w, gb, g_in, g_out, g_proj)
    )
    grad_input = gall.astype(f32).reshape(1, T, D)
    return (
        block_out.reshape(1, T, D),
        grad_input,
        vec[4],
        vec[5],
        g_qkv,
        gbq,
        gtab_h,
        gtab_w,
        g_proj,
        vec[2],
        vec[0],
        vec[1],
        g_in,
        gb,
        g_out,
        vec[3],
    )


def solution(mesh):
    placed = (
        P("dp", "ctx", None),
        P("dp", "ctx", None),
        P("dp"),
        P("dp"),
        P("dp", None, "tensor"),
        P(None, "tensor", "dp"),
        P(None, "dp"),
        P(None, "dp"),
        P("tensor", "dp"),
        P("dp"),
        P("dp"),
        P("dp"),
        P("dp", "tensor"),
        P("tensor", "dp"),
        P("tensor", "dp"),
        P("dp"),
    )
    return jax.shard_map(
        per_device,
        mesh=mesh,
        in_specs=placed,
        out_specs=(placed[0], placed[0]) + placed[2:],
        check_vma=False,
    )
```

```python
import functools

import jax
import jax.numpy as jnp
from jax import lax
from jax.experimental import pallas as pl
from jax.experimental.pallas import tpu as pltpu
from jax.sharding import PartitionSpec as P

HD = 64
GW = 64
EPS = 1e-06
f32 = jnp.float32
bf16 = jnp.bfloat16
VMEM = 56 * 2**20


def iota(shape, dim):
    return lax.broadcasted_iota(jnp.int32, shape, dim)


def dot(a, b, ca, cb):
    return lax.dot_general(a, b, (((ca,), (cb,)), ((), ())), preferred_element_type=f32)


def make_qaug(qT, tab, il0, off, R):
    bq = qT.shape[1]
    qf = jnp.concatenate([qT.astype(f32), jnp.zeros((64, bq), f32)], 0).T
    g = dot(qT, tab, 0, 0)
    lane = iota((64, 128), 1)
    used = (lane < 64 + R) | ((lane >= 96) & (lane < 96 + R))
    outs = []
    for k in range(bq // 64):
        gh = g[k * 64 : (k + 1) * 64, :128]
        gw = g[k * 64 : (k + 1) * 64, 128:]
        sh = 63 - (il0 + k) + off
        h64 = pltpu.roll(gh, lax.rem(64 - sh + 256, 128), 1)
        h96 = pltpu.roll(gh, lax.rem(96 - sh + 256, 128), 1)
        w64 = pltpu.roll(gw, 1, 1, stride=1, stride_axis=0)
        w0 = pltpu.roll(gw, 65, 1, stride=1, stride_axis=0)
        a = jnp.where(lane < 64, qf[k * 64 : (k + 1) * 64], w64)
        wl = w0 - w0.astype(bf16).astype(f32)
        hl = h96 - h96.astype(bf16).astype(f32)
        b = jnp.where(lane < 64, wl, jnp.where(lane < 96, h64, hl))
        b = jnp.where(used, b, 0.0)
        outs.append(jnp.concatenate([a, b], 1).astype(bf16))
    return jnp.concatenate(outs, 0)


def build_kaug(kT, kaug, flipped=False):
    KB = kT.shape[1]
    ck = min(512, KB)
    for c in range(KB // ck):
        kf = kT[:, c * ck : (c + 1) * ck].astype(f32) * 0.125
        kf = jnp.concatenate([kf, jnp.zeros((64, ck), f32)], 0).T
        n = iota((ck, 128), 0) + c * ck
        lane = iota((ck, 128), 1)
        col, row = n & 63, n >> 6
        spot = 127 - col if flipped else 64 + col
        a = jnp.where(lane < 64, kf, (lane == spot).astype(f32))
        b = jnp.where(lane < 64, (lane == col).astype(f32), ((lane & 31) == row).astype(f32))
        kaug[c * ck : (c + 1) * ck, :] = jnp.concatenate([a, b], 1).astype(bf16)


def build_kaugT(kT, kaugT):
    KB = kT.shape[1]
    ck = min(512, KB)
    for c in range(KB // ck):
        f = iota((64, ck), 0)
        n = iota((64, ck), 1) + c * ck
        col, row = n & 63, n >> 6
        sl = slice(c * ck, (c + 1) * ck)
        kaugT[0:64, sl] = (kT[:, sl].astype(f32) * 0.125).astype(bf16)
        oc = (f == col).astype(f32).astype(bf16)
        kaugT[64:128, sl] = oc
        kaugT[128:192, sl] = oc
        kaugT[192:256, sl] = ((f & 31) == row).astype(f32).astype(bf16)


def fwd_kernel(sc_ref, qT_ref, tab_ref, *rest, R, bk, first, last, nt, n):
    kvs, rest = rest[:n], rest[n:]
    if first:
        rest = (None, None) + rest
    oi_ref, mli_ref, o_ref, ml_ref, *rest = rest
    KB = kvs[0].shape[1]
    bq = qT_ref.shape[1]
    hi, qi = pl.program_id(0), pl.program_id(1)
    if last:
        kaug, vaug, och = rest[-3:]
    else:
        kaug, vaug = rest[-2:]

    for g, kv in enumerate(kvs):

        @pl.when((qi == 0) & (hi == g))
        def _(kv=kv):
            build_kaug(kv[0:64, :], kaug)
            vaug[0:64, :] = kv[64:128, :]
            vaug[64:80, :] = (iota((16, KB), 0) == 0).astype(f32).astype(bf16)

    qaug = make_qaug(qT_ref[...], tab_ref[:, :256], qi * (bq // 64), sc_ref[0], R)
    if first:
        m = jnp.full((1, bq), -3e38, f32)
        o = jnp.zeros((80, bq), f32)
    else:
        m = mli_ref[0:1, :]
        o = jnp.concatenate([oi_ref[...], jnp.broadcast_to(mli_ref[1:2, :], (16, bq))], 0)
    for c in range(KB // bk):
        s = dot(kaug[c * bk : (c + 1) * bk, :], qaug, 1, 1)
        mn = jnp.maximum(m, jnp.max(s, axis=0, keepdims=True))
        al = jnp.exp(m - mn)
        p = jnp.exp(s - mn).astype(bf16)
        o = o * al + jnp.dot(vaug[:, c * bk : (c + 1) * bk], p, preferred_element_type=f32)
        m = mn
    l = o[64:65, :]
    o = o[:64]
    if last:
        o = o * (1.0 / l)
        m = m + jnp.log(l)
        N = och.shape[2]
        ob = o.astype(bf16)
        for j in range(bq // N):
            och[qi * (bq // N) + j] = ob[:, j * N : (j + 1) * N]

        @pl.when(qi == pl.num_programs(1) - 1)
        def _():
            for k in range(nt):
                rest[k][...] = och[sc_ref[1] ^ k]

    o_ref[...] = o
    ml_ref[...] = jnp.concatenate([m, l, jnp.zeros((6, bq), f32)], 0)


def attn_fwd(sc, h0, qT, kvs, tab, state, last, R, nt, bq=2048, bk=512):
    H, _, T = qT.shape
    n = len(kvs)
    KB = kvs[0].shape[1]
    N = T // nt
    bq, bk = min(bq, T), min(bk, KB)
    first = state is None
    qs = lambda r: pl.BlockSpec((None, r, bq), lambda h, i, o: (h0 + h, 0, i))
    ins = [qs(64), pl.BlockSpec((64, 384), lambda h, i, o: (0, 0))]
    ins += [pl.BlockSpec((128, KB), lambda h, i, o: (0, 0))] * n
    ins += [] if first else [qs(64), qs(8)]
    outs = [qs(64), qs(8)]
    shapes = [jax.ShapeDtypeStruct((H, 64, T), f32), jax.ShapeDtypeStruct((H, 8, T), f32)]
    scratch = [pltpu.VMEM((KB, 256), bf16), pltpu.VMEM((80, KB), bf16)]
    if last:
        outs += [pl.BlockSpec((64, N), lambda h, i, o: (h, 0))] * nt
        shapes += [jax.ShapeDtypeStruct((n * 64, N), bf16)] * nt
        scratch += [pltpu.VMEM((nt, 64, N), bf16)]
    return pl.pallas_call(
        functools.partial(fwd_kernel, R=R, bk=bk, first=first, last=last, nt=nt, n=n),
        grid_spec=pltpu.PrefetchScalarGridSpec(
            num_scalar_prefetch=1,
            grid=(n, T // bq),
            in_specs=ins,
            out_specs=outs,
            scratch_shapes=scratch,
        ),
        out_shape=shapes,
        input_output_aliases={} if first else {3 + n: 0, 4 + n: 1},
        compiler_params=pltpu.CompilerParams(vmem_limit_bytes=VMEM),
        cost_estimate=pl.CostEstimate(
            flops=2 * n * T * KB * 512, bytes_accessed=n * T * 1200, transcendentals=n * T * KB
        ),
        name="attn_fwd",
    )(sc, qT, tab, *kvs, *([] if first else state))


def bwd_kernel(sc_ref, qT_ref, tab_ref, *rest, R, bk, has_dq, has_dt, last, nt, n):
    kvs, rest = rest[:n], rest[n:]
    do_refs, rest = rest[:nt], rest[nt:]
    o_ref, ml_ref, *rest = rest
    dqi_ref = dti_ref = dki_ref = None
    if has_dq:
        dqi_ref, *rest = rest
    if has_dt:
        dti_ref, *rest = rest
    if last:
        dki_ref, *rest = rest
        dx_refs, rest = rest[:nt], rest[nt:]
        dt_ref, kaug, kaugT, vaug, acc, dch, fin = rest
    else:
        dq_ref, dkv_ref, dt_ref, kaug, kaugT, vaug, acc, dch = rest
    KB = kvs[0].shape[1]
    bq = qT_ref.shape[1]
    N = dch.shape[2]
    per = bq // N
    hi, qi = pl.program_id(0), pl.program_id(1)

    for g, kv in enumerate(kvs):

        @pl.when((qi == 0) & (hi == g))
        def _(kv=kv):
            build_kaug(kv[0:64, :], kaug, True)
            build_kaugT(kv[0:64, :], kaugT)
            vaug[0:64, :] = kv[64:128, :]
            vaug[64:128, :] = (iota((64, KB), 0) < 3).astype(f32).astype(bf16)

    @pl.when(qi == 0)
    def _():
        if last:
            acc[0:64, :] = dki_ref[0:64, :].astype(f32) * 8.0
            acc[64:128, :] = dki_ref[64:128, :].astype(f32)
        else:
            acc[...] = jnp.zeros_like(acc)
        for k in range(nt):
            dch[sc_ref[1] ^ k] = do_refs[k][...]

    @pl.when((qi == 0) & (hi == 0))
    def _():
        dt_ref[...] = dti_ref[...] if has_dt else jnp.zeros_like(dt_ref)

    qT = qT_ref[...]
    doT = jnp.concatenate([dch[qi * per + j] for j in range(per)], 1)
    il0 = qi * (bq // 64)
    off = sc_ref[0]
    qaug = make_qaug(qT, tab_ref[:, :256], il0, off, R)
    dof = doT.astype(f32)
    nd = -jnp.sum(dof * o_ref[...], axis=0, keepdims=True)
    d1 = nd.astype(bf16).astype(f32)
    d2 = (nd - d1).astype(bf16).astype(f32)
    d3 = nd - d1 - d2
    rid = iota((64, bq), 0)
    ext = jnp.where(rid == 2, d3, jnp.where(rid == 3, ml_ref[0:1, :], 0.0))
    ext = jnp.where(rid == 0, d1, jnp.where(rid == 1, d2, ext))
    t = jnp.concatenate([dof, ext], 0).T
    lse = t[:, 67:68]
    doaug = t.astype(bf16)
    dq = jnp.zeros((bq, 256), f32)
    for c in range(KB // bk):
        sl = slice(c * bk, (c + 1) * bk)
        s = jnp.dot(qaug, kaugT[:, sl], preferred_element_type=f32)
        p = jnp.exp(s - lse)
        dp = jnp.dot(doaug, vaug[:, sl], preferred_element_type=f32)
        pb = p.astype(bf16)
        ds = (p * dp).astype(bf16)
        acc[64:128, sl] += jnp.dot(doT, pb, preferred_element_type=f32)
        acc[0:64, sl] += jnp.dot(qT, ds, preferred_element_type=f32)
        dq += jnp.dot(ds, kaug[sl, :], preferred_element_type=f32)
    lane = iota((64, 128), 1)
    his, los = [], []
    for k in range(bq // 64):
        a = dq[k * 64 : (k + 1) * 64, :128]
        b = dq[k * 64 : (k + 1) * 64, 128:]
        gw = pltpu.roll(jnp.where(lane >= 64, a, 0.0), 64, 1, stride=1, stride_axis=0)
        sh = off - (il0 + k) - 1
        gh = pltpu.roll(
            jnp.where((lane >= 64) & (lane < 64 + R), b, 0.0), lax.rem(sh + 256, 128), 1
        )
        g = jnp.concatenate([gh, gw], 1)
        h = g.astype(bf16)
        his.append(h)
        los.append((g - h.astype(f32)).astype(bf16))
    gh = jnp.concatenate(his, 0)
    gl = jnp.concatenate(los, 0)
    tab = jnp.concatenate([tab_ref[:, :128], tab_ref[:, 256:]], 1)
    dqT = dq[:, :128].T[:64] + dot(tab, gh, 1, 1) + dot(tab, gl, 1, 1)
    if has_dq:
        dqT = dqT + dqi_ref[...]
    dt_ref[...] += dot(qT, gh, 1, 0) + dot(qT, gl, 1, 0)
    if last:
        dqb = dqT.astype(bf16)
        for j in range(per):
            fin[qi * per + j, 0:64, :] = dqb[:, j * N : (j + 1) * N]
    else:
        dq_ref[...] = dqT

    @pl.when(qi == pl.num_programs(1) - 1)
    def _():
        if last:
            for j in range(nt):
                fin[j, 64:128, :] = (acc[0:64, j * N : (j + 1) * N] * 0.125).astype(bf16)
                fin[j, 128:192, :] = acc[64:128, j * N : (j + 1) * N].astype(bf16)
            for k in range(nt):
                dx_refs[k][...] = fin[sc_ref[1] ^ k]
        else:
            dkv_ref[0:64, :] = (acc[0:64, :] * 0.125).astype(bf16)
            dkv_ref[64:128, :] = acc[64:128, :].astype(bf16)


def attn_bwd(sc, h0, qT, kvs, tab, dos, o, ml, dq, dt, back, R, bq=2048, bk=512):
    _, _, T = qT.shape
    n = len(kvs)
    KB = kvs[0].shape[1]
    nt = len(dos)
    N = T // nt
    bq, bk = min(bq, T), min(bk, KB)
    last = back is not None
    qs = lambda r, h0=h0: pl.BlockSpec((None, r, bq), lambda h, i, s: (h0 + h, 0, i))
    fix = lambda shape: pl.BlockSpec(shape, lambda h, i, s: (0, 0))
    ins = [qs(64), fix((64, 384))] + [fix((128, KB))] * n
    ins += [pl.BlockSpec((64, N), lambda h, i, s: (h0 + h, 0))] * nt + [qs(64), qs(8)]
    args = [qT, tab, *kvs, *dos, o, ml]
    if dq is not None:
        ins += [qs(64, dq[1])]
        args += [dq[0]]
    if dt is not None:
        ins += [fix((64, 256))]
        args += [dt]
    scratch = [
        pltpu.VMEM((KB, 256), bf16),
        pltpu.VMEM((256, KB), bf16),
        pltpu.VMEM((128, KB), bf16),
        pltpu.VMEM((128, KB), f32),
        pltpu.VMEM((nt, 64, N), bf16),
    ]
    if last:
        ins += [pl.BlockSpec((None, 128, KB), lambda h, i, s: (back[1], 0, 0))]
        args += [back[0]]
        outs = [fix((192, N))] * nt
        shapes = [jax.ShapeDtypeStruct((192, N), bf16)] * nt
        scratch += [pltpu.VMEM((nt, 192, N), bf16)]
    else:
        outs = [qs(64, 0), pl.BlockSpec((None, 128, KB), lambda h, i, s: (h, 0, 0))]
        shapes = [jax.ShapeDtypeStruct((n, 64, T), f32), jax.ShapeDtypeStruct((n, 128, KB), bf16)]
    return pl.pallas_call(
        functools.partial(
            bwd_kernel, R=R, bk=bk, has_dq=dq is not None, has_dt=dt is not None, last=last,
            nt=nt, n=n,
        ),
        grid_spec=pltpu.PrefetchScalarGridSpec(
            num_scalar_prefetch=1,
            grid=(n, T // bq),
            in_specs=ins,
            out_specs=outs + [fix((64, 256))],
            scratch_shapes=scratch,
        ),
        out_shape=shapes + [jax.ShapeDtypeStruct((64, 256), f32)],
        compiler_params=pltpu.CompilerParams(vmem_limit_bytes=VMEM),
        cost_estimate=pl.CostEstimate(
            flops=(2 if dt is not None else 40) * n * T * KB * 1280,
            bytes_accessed=n * T * 3000,
            transcendentals=n * T * KB,
        ),
        name="attn_bwd",
    )(sc, *args)


def rows_of(sc_ref, r, dd):
    return pl.ds(pl.multiple_of((sc_ref[2] ^ r) * dd, dd), dd)


def whole_spec(shape):
    return pl.BlockSpec(shape, lambda *_: (0,) * len(shape))


def norm_parts(x):
    c = x - jnp.mean(x, axis=-1, keepdims=True)
    r = lax.rsqrt(jnp.mean(c * c, axis=-1, keepdims=True) + EPS)
    return c * r, r


def norm_back(dh, gain, xhat, r):
    e = dh * gain
    return (
        e - jnp.mean(e, axis=-1, keepdims=True) - xhat * jnp.mean(e * xhat, axis=-1, keepdims=True)
    ) * r


def call(kernel, sc, grid, ins, args, outs, shapes, scratch, name, flops, nbytes):
    return pl.pallas_call(
        kernel,
        grid_spec=pltpu.PrefetchScalarGridSpec(
            num_scalar_prefetch=1, grid=grid, in_specs=ins, out_specs=outs, scratch_shapes=scratch
        ),
        out_shape=[jax.ShapeDtypeStruct(s, d) for s, d in shapes],
        compiler_params=pltpu.CompilerParams(vmem_limit_bytes=VMEM),
        cost_estimate=pl.CostEstimate(flops=flops, bytes_accessed=nbytes, transcendentals=0),
        name=name,
    )(sc, *args)


def pack_kernel(sc_ref, w, rh, rw, n1g, n1b, n2g, n2b, pb, ob, qb, out):
    dd, E3 = w.shape[1], 3 * w.shape[2]
    for h in range(E3 // 192):
        cols = [w[j, :, h * 64 : (h + 1) * 64].astype(f32) for j in range(3)]
        out[0:dd, h * 192 : (h + 1) * 192] = jnp.concatenate(cols, 1).astype(bf16)
    out[dd:, :] = jnp.zeros((32, E3), bf16)
    L = rh.shape[1]
    t, l = iota((L, 128), 0), iota((L, 128), 1)
    back = (t == L - 1 - l).astype(f32).astype(bf16)
    same = (t == l).astype(f32).astype(bf16)
    out[dd : dd + 16, 0:128] = dot(rh[...], back, 1, 0).astype(bf16)
    out[dd : dd + 16, 128:256] = dot(rw[...], back, 1, 0).astype(bf16)
    out[dd : dd + 16, 256:384] = dot(rw[...], same, 1, 0).astype(bf16)
    rows = [v[...].astype(f32).reshape(1, dd) for v in (n1g, n1b, n2g, n2b, pb, ob)]
    rows = jnp.concatenate(rows + [jnp.zeros((10, dd), f32)], 0)
    out[dd + 16 :, 0:dd] = rows.astype(bf16)
    q = [qb[h].astype(f32) for h in range(qb.shape[0])]
    q = jnp.concatenate(q + [jnp.zeros((16 - 2 * len(q), 16), f32)], 0)
    out[dd + 16 :, 256:272] = q.astype(bf16)


def front_kernel(sc_ref, x_ref, s0, s1, s2, s3, tab_ref, v_ref, q_ref, *rest, H):
    kvs, (wt_ref, xh_ref, wn, all4, bias) = rest[:H], rest[H:]
    dd = s0.shape[0] - 32

    @pl.when(pl.program_id(0) == 0)
    def _():
        for r, s in enumerate((s0, s1, s2, s3)):
            all4[sc_ref[2] ^ r] = s[dd:, :]
            wn[rows_of(sc_ref, r, dd), :] = s[0:dd, :]
        wt_ref[...] = wn[...].T
        for j in range(4):
            tab_ref[j * 16 : (j + 1) * 16, :] = all4[j, 0:16, 0:384]
        low = [all4[j, 16:32, :].astype(f32) for j in range(4)]
        v_ref[...] = jnp.concatenate([z[0:8, 0:dd] for z in low], 1)
        q = jnp.concatenate([z[:, 256:272] for z in low] + [jnp.zeros((16, 64), f32)], 1)
        q = q.T[0:64]
        for h in range(H):
            bias[h * 192 : h * 192 + 64, :] = q[:, 2 * h : 2 * h + 1]
            bias[h * 192 + 64 : h * 192 + 128, :] = jnp.zeros((64, 1), f32)
            bias[h * 192 + 128 : (h + 1) * 192, :] = q[:, 2 * h + 1 : 2 * h + 2]

    xh, _ = norm_parts(x_ref[...].astype(f32))
    xh_ref[...] = xh.astype(bf16)
    h1 = (xh * v_ref[0:1, :] + v_ref[1:2, :]).astype(bf16)
    y = dot(wt_ref[...], h1, 1, 1) + bias[...]
    y = y.astype(bf16)
    for h in range(H):
        q_ref[h] = y[h * 192 : h * 192 + 64]
        kvs[h][...] = y[h * 192 + 64 : (h + 1) * 192]


def front(sc, x, ss, H):
    T, D = x.shape
    E3 = H * 192
    bt = min(512, T)
    rows = pl.BlockSpec((bt, D), lambda i, s: (i, 0))
    return call(
        functools.partial(front_kernel, H=H), sc, (T // bt,),
        [rows] + [whole_spec(ss[0].shape)] * 4, [x, *ss],
        [whole_spec((64, 384)), whole_spec((8, D))]
        + [pl.BlockSpec((H, 64, bt), lambda i, s: (0, 0, i))]
        + [pl.BlockSpec((128, bt), lambda i, s: (0, i))] * H
        + [whole_spec((E3, D)), rows],
        [((64, 384), bf16), ((8, D), f32), ((H, 64, T), bf16)]
        + [((128, T), bf16)] * H
        + [((E3, D), bf16), ((T, D), bf16)],
        [pltpu.VMEM((D, E3), bf16), pltpu.VMEM((4, 32, E3), bf16), pltpu.VMEM((E3, 1), f32)],
        "front", 2 * T * D * E3, 6 * T * D,
    )


def piece_specs(w):
    _, dd, cols = w[0].shape
    return [pl.BlockSpec((None, dd, cols), lambda k, s: (s[1] ^ k, 0, 0))] * 4


def assemble(sc_ref, whole, parts):
    for r, p in enumerate(parts):
        whole[rows_of(sc_ref, r, p.shape[0]), :] = p[...]


def mlp1_kernel(sc_ref, x_ref, g_ref, v_ref, *rest, nt, fb):
    no = 2 * nt
    os, ps, rest = rest[:no], rest[no : no + 4], rest[no + 4 :]
    p1, p2, rest = rest[:4], rest[4:8], rest[8:]
    a_ref, du_ref, h2_ref, da_ref, y1_ref, dy_ref, sm_ref, db_ref, *rest = rest
    dos, (dh, wp, wts, b4, bias, wi, wo) = rest[:nt], rest[nt:]
    D, ft = wi.shape
    dd = D // 4
    k = pl.program_id(0)

    @pl.when(k == 0)
    def _():
        y = x_ref[...].astype(f32) + v_ref[4:5, :]
        na = os[0].shape[0]
        for kk in range(nt):
            for r in range(4):
                wp[rows_of(sc_ref, r, dd), :] = ps[r][kk, 0:dd]
            wt = wp[...].T
            wts[kk] = wt
            y = y + dot(os[kk][...], wt[:na], 0, 0)
            y = y + dot(os[nt + kk][...], wt[na:], 0, 0)
        y1_ref[...] = y
        xh, _ = norm_parts(y)
        h2_ref[...] = (xh * v_ref[2:3, :] + v_ref[3:4, :]).astype(bf16)
        dh[...] = jnp.zeros_like(dh)

    assemble(sc_ref, wi, p1)
    assemble(sc_ref, wo, p2)
    for r in range(4):
        b4[sc_ref[2] ^ r] = ps[r][k, dd:, :].astype(f32)
    rows = jnp.concatenate([b4[j, :, 0:16] for j in range(4)], 1)
    for i in range(ft // 64):
        bias[:, i * 64 : (i + 1) * 64] = rows[i : i + 1]
    for j in range(ft // fb):
        sl = slice(j * fb, (j + 1) * fb)
        u = jnp.dot(h2_ref[...], wi[:, sl], preferred_element_type=f32) + bias[:, sl]
        ga = jnp.dot(g_ref[...], wo[:, sl], preferred_element_type=f32)
        cdf = 0.5 + 0.5 * lax.erf(u * 0.7071067811865476)
        a_ref[:, sl] = (u * cdf).astype(bf16)
        slope = cdf + u * (jnp.exp(-0.5 * u * u) * 0.3989422804014327)
        du = (slope * ga).astype(bf16)
        du_ref[:, sl] = du
        db_ref[:, sl] = jnp.sum(du.astype(f32), axis=0, keepdims=True)
        dh[...] += dot(du, wi[:, sl], 1, 1)

    @pl.when(k == pl.num_programs(0) - 1)
    def _():
        g = g_ref[...].astype(f32)
        xh, r = norm_parts(y1_ref[...])
        d = dh[...]
        dy = g + norm_back(d, v_ref[2:3, :], xh, r)
        dy_ref[...] = dy
        da = dy.astype(bf16)
        da_ref[...] = da
        for kk in range(nt):
            dos[kk][...] = dot(wts[kk], da, 1, 1).astype(bf16)
        sums = [jnp.sum(z, axis=0, keepdims=True) for z in (d * xh, d, da.astype(f32), g)]
        sm_ref[...] = jnp.concatenate(sums + [jnp.zeros((4, D), f32)], 0)


def mlp1(sc, x, g, vecs, os, ps, p1, p2):
    D = x.shape[1]
    nt, _, kt = ps[0].shape
    ft = p1[0].shape[2]
    N = os[0].shape[1]
    mine = pl.BlockSpec((N, D), lambda k, s: (s[1], 0))
    act = pl.BlockSpec((None, N, ft), lambda k, s: (k, 0, 0))
    row = pl.BlockSpec((None, 1, ft), lambda k, s: (s[1] ^ k, 0, 0))
    full = whole_spec((N, D))
    return call(
        functools.partial(mlp1_kernel, nt=nt, fb=256), sc, (nt,),
        [mine, mine, whole_spec(vecs.shape)]
        + [whole_spec(o.shape) for o in os]
        + [whole_spec(p.shape) for p in ps]
        + piece_specs(p1)
        + piece_specs(p2),
        [x, g, vecs, *os, *ps, *p1, *p2],
        [act, act, full, full, full, full, whole_spec((8, D)), row] + [whole_spec((kt, N))] * nt,
        [((nt, N, ft), bf16)] * 2
        + [((N, D), bf16)] * 2
        + [((N, D), f32)] * 2
        + [((8, D), f32), ((nt, 1, ft), f32)]
        + [((kt, N), bf16)] * nt,
        [
            pltpu.VMEM((N, D), f32),
            pltpu.VMEM((D, kt), bf16),
            pltpu.VMEM((nt, kt, D), bf16),
            pltpu.VMEM((4, 16, kt), f32),
            pltpu.VMEM((1, ft), f32),
            pltpu.VMEM((D, ft), bf16),
            pltpu.VMEM((D, ft), bf16),
        ],
        "mlp_grad", 6 * N * D * ft * nt, 24 * 2**20,
    )


def mlp2_kernel(sc_ref, g_ref, v_ref, h2_ref, da_ref, y_ref, a_ref, du_ref, *rest, nt):
    no = 2 * nt
    os, p2, rest = rest[:no], rest[no : no + 4], rest[no + 4 :]
    gws, (out_ref, hT, gT, dT, oa, acc, acn, wo) = rest[:4], rest[4:]
    ft = a_ref.shape[1]
    D = h2_ref.shape[1]
    dd = D // 4
    k = pl.program_id(0)

    @pl.when(k == 0)
    def _():
        for src, dst in ((h2_ref, hT), (g_ref, gT), (da_ref, dT)):
            acn[...] = src[...].astype(f32).T
            for r in range(4):
                dst[r * dd : (r + 1) * dd, :] = acn[rows_of(sc_ref, r, dd), :].astype(bf16)
        na = os[0].shape[0]
        for kk in range(nt):
            oa[kk, :na] = os[kk][...]
            oa[kk, na:] = os[nt + kk][...]
        acc[...] = jnp.zeros_like(acc)

    a = a_ref[...]
    assemble(sc_ref, wo, p2)
    acc[...] += dot(a, wo[...], 1, 1)

    def store(value, lo, hi):
        value = value.astype(bf16)
        for r in range(4):
            gws[r][:, lo:hi] = value[r * dd : (r + 1) * dd]

    store(jnp.dot(hT[...], du_ref[...], preferred_element_type=f32), 0, ft)
    store(jnp.dot(gT[...], a, preferred_element_type=f32), ft, 2 * ft)
    store(dot(dT[...], oa[k], 1, 1), 2 * ft, gws[0].shape[1])

    @pl.when(k == pl.num_programs(0) - 1)
    def _():
        out_ref[...] = (y_ref[...] + (acc[...] + v_ref[5:6, :])).astype(bf16)


def mlp2(sc, g, vecs, h2, da, y1, a, du, os, p2):
    N, D = h2.shape
    nt, _, ft = a.shape
    dd = D // 4
    kt = os[0].shape[0] + os[nt].shape[0]
    cols = 2 * ft + kt
    full = whole_spec((N, D))
    act = pl.BlockSpec((None, N, ft), lambda k, s: (k, 0, 0))
    gw = pl.BlockSpec((None, dd, cols), lambda k, s: (s[1] ^ k, 0, 0))
    return call(
        functools.partial(mlp2_kernel, nt=nt), sc, (nt,),
        [pl.BlockSpec((N, D), lambda k, s: (s[1], 0)), whole_spec(vecs.shape), full, full, full]
        + [act, act]
        + [whole_spec(o.shape) for o in os]
        + piece_specs(p2),
        [g, vecs, h2, da, y1, a, du, *os, *p2],
        [gw] * 4 + [full],
        [((nt, dd, cols), bf16)] * 4 + [((N, D), bf16)],
        [pltpu.VMEM((D, N), bf16)] * 3
        + [
            pltpu.VMEM((nt, kt, N), bf16),
            pltpu.VMEM((N, D), f32),
            pltpu.VMEM((D, N), f32),
            pltpu.VMEM((D, ft), bf16),
        ],
        "mlp_weights", 7 * N * D * ft * nt, 24 * 2**20,
    )


def gqkv_kernel(sc_ref, x_ref, v_ref, wt_ref, *rest, nt, H):
    dx, (keep_ref, send_ref, b_ref, n_ref, g) = rest[: H * nt], rest[H * nt :]
    dd = keep_ref.shape[1]
    lane = iota((192, 128), 1)
    gain, shift = v_ref[0:1, :], v_ref[1:2, :]
    dg, db = jnp.zeros_like(gain), jnp.zeros_like(gain)
    for h in range(H):
        t = jnp.zeros((192, x_ref.shape[2]), f32)
        b = jnp.zeros((192, 1), f32)
        for k in range(nt):
            d = dx[h * nt + k][...]
            t = t + jnp.dot(d, x_ref[sc_ref[1] ^ k], preferred_element_type=f32)
            b = b + jnp.sum(d.astype(f32), axis=1, keepdims=True)
        w = wt_ref[h * 192 : (h + 1) * 192, :].astype(f32)
        dg = dg + jnp.sum(w * t, axis=0, keepdims=True)
        db = db + jnp.sum(w * b, axis=0, keepdims=True)
        g[:, h * 192 : (h + 1) * 192] = (t * gain + shift * b).T.astype(bf16)
        b_ref[h] = jnp.where(lane == 0, b, 0.0)
    n_ref[...] = jnp.concatenate([dg, db, jnp.zeros((6, dg.shape[1]), f32)], 0)
    for r in range(4):
        dst = send_ref if r & 1 else keep_ref
        dst[r // 2] = g[rows_of(sc_ref, r, dd), :]


def gqkv(sc, xh, vecs, wT, dx, nt):
    T, D = xh.shape
    H = len(dx) // nt
    N = T // nt
    dd = D // 4
    part = (2, dd, H * 192)
    return call(
        functools.partial(gqkv_kernel, nt=nt, H=H), sc, (1,),
        [whole_spec((nt, N, D)), whole_spec(vecs.shape), whole_spec(wT.shape)]
        + [whole_spec((192, N))] * len(dx),
        [xh.reshape(nt, N, D), vecs, wT, *dx],
        [whole_spec(part), whole_spec(part), whole_spec((H, 192, 128)), whole_spec((8, D))],
        [(part, bf16), (part, bf16), ((H, 192, 128), f32), ((8, D), f32)],
        [pltpu.VMEM((D, H * 192), bf16)],
        "qkv_weights", 2 * T * D * 192 * H, 8 * 2**20,
    )


def dh1_kernel(sc_ref, x_ref, dy_ref, v_ref, *rest, nt, H):
    dx, (p3, p3b, gi_ref, da, w3) = rest[: H * nt], rest[H * nt :]
    hd = p3.shape[2]
    D = x_ref.shape[1]
    E3 = H * 192
    for k in range(nt):
        for h in range(H):
            da[(k * H + h) * 192 : (k * H + h + 1) * 192, :] = dx[h * nt + k][...]
    t = jnp.zeros((D, da.shape[1]), f32)
    for k in range(nt):
        for j in range(4):
            w3[2 * j * hd : (2 * j + 1) * hd, :] = p3[j, sc_ref[1] ^ k]
            w3[(2 * j + 1) * hd : (2 * j + 2) * hd, :] = p3b[j, sc_ref[1] ^ k]
        t = t + jnp.dot(w3[...], da[k * E3 : (k + 1) * E3, :], preferred_element_type=f32)
    xh, r = norm_parts(x_ref[...].astype(f32))
    gi_ref[...] = (dy_ref[...] + norm_back(t.T, v_ref[0:1, :], xh, r)).astype(bf16)


def dh1(sc, x, dy1, vecs, dx, p3, p3b):
    N, D = dy1.shape
    nt = p3.shape[1]
    H = len(dx) // nt
    return call(
        functools.partial(dh1_kernel, nt=nt, H=H), sc, (1,),
        [pl.BlockSpec((N, D), lambda k, s: (s[1], 0)), whole_spec((N, D)), whole_spec(vecs.shape)]
        + [whole_spec((192, N))] * len(dx)
        + [whole_spec(p3.shape)] * 2,
        [x, dy1, vecs, *dx, p3, p3b],
        [whole_spec((N, D))],
        [((N, D), bf16)],
        [pltpu.VMEM((nt * H * 192, N), bf16), pltpu.VMEM((D, H * 192), bf16)],
        "norm1_grad", 2 * N * D * D * 3, 8 * 2**20,
    )[0]


def copy_kernel(sc_ref, a, b):
    b[...] = a[...].astype(b.dtype)


def copied(sc, v, dtype):
    rows = pl.BlockSpec((v.shape[0] // 4, v.shape[1]), lambda i, s: (i, 0))
    return call(
        copy_kernel, sc, (4,), [rows], [v], [rows], [(v.shape, dtype)], [], "copied", 0, 2**22
    )[0]


def shift(value, axis, steps):
    n = lax.axis_size(axis)
    return lax.ppermute(value, axis, [(s, (s + steps) % n) for s in range(n)])


def flip(value, axis, bit):
    n = lax.axis_size(axis)
    return lax.ppermute(value, axis, [(s, s ^ bit) for s in range(n)])


def after(value, *others):
    return lax.optimization_barrier((value, *others))[0]


def gather_weights(shard):
    nd, nt = lax.axis_size("dp"), lax.axis_size("tensor")
    return lax.all_gather(shard, ("dp", "tensor")).reshape((nd, nt) + shard.shape)


def spread(parts):
    return [parts[0]] + [flip(p, "tensor", k) for k, p in enumerate(parts) if k]


def total_ctx(value):
    v = value.astype(bf16)
    if lax.axis_size("ctx") == 2:
        return v.astype(f32) + flip(v, "ctx", 1).astype(f32)
    return lax.psum(v.astype(f32), "ctx")


def per_device(
    block_input,
    cotangent,
    norm1_gain,
    norm1_bias,
    qkv_weight,
    qkv_bias,
    rel_pos_h,
    rel_pos_w,
    proj_weight,
    proj_bias,
    norm2_gain,
    norm2_bias,
    mlp_in_weight,
    mlp_in_bias,
    mlp_out_weight,
    mlp_out_bias,
):
    nt, nc = lax.axis_size("tensor"), lax.axis_size("ctx")
    me, pos, dp = lax.axis_index("tensor"), lax.axis_index("ctx"), lax.axis_index("dp")
    T, D = block_input.shape[1:]
    R = T // GW
    dd = D // 4
    N = T // nt
    H = qkv_bias.shape[1]
    E = H * HD
    L = rel_pos_h.shape[0]
    ft = mlp_in_weight.shape[1]
    x2 = block_input.reshape(T, D)
    g2 = cotangent.reshape(T, D)

    def scalars(k):
        off = (((pos - k) % nc) - pos) * R
        return jnp.stack([off, me, dp]).astype(jnp.int32)

    sc = scalars(0)
    bar = lax.optimization_barrier

    smalls = [qkv_weight.transpose(1, 0, 2), rel_pos_h.T, rel_pos_w.T]
    smalls += [norm1_gain, norm1_bias, norm2_gain, norm2_bias, proj_bias, mlp_out_bias]
    smalls += [qkv_bias.transpose(1, 0, 2)]
    small = call(
        pack_kernel, sc, (1,), [whole_spec(v.shape) for v in smalls], smalls,
        [whole_spec((dd + 32, 3 * E))], [((dd + 32, 3 * E), bf16)], [], "pack", 0, 2**16,
    )[0]
    p1 = lax.all_gather(mlp_in_weight, "tensor", axis=0)
    p2 = lax.all_gather(mlp_out_weight.T, "tensor", axis=0)
    brow = jnp.pad(mlp_in_bias, ((0, 16 - mlp_in_bias.shape[0]), (0, E - 16)))
    own = jnp.concatenate([proj_weight.T, brow], 0)
    near = flip(own, "tensor", 1)
    small = [small] + [flip(small, "dp", r) for r in (1, 2, 3)]
    near, small = bar((near, small))
    own = jnp.stack([own, near])
    two = flip(own, "tensor", 2)

    tab, vecs, qT, *rest = front(sc, x2, small, H)
    kvs, (wT, xh1) = rest[:H], rest[H:]
    kv_far = [[shift(kv, "ctx", k) for kv in kvs] for k in range(1, nc)]

    state = attn_fwd(sc, 0, qT, kvs, tab, None, False, R, nt)
    state, two, p1 = bar((state, two, p1))
    p1x = flip(p1, "dp", 2)
    own = jnp.concatenate([own, two])
    far = flip(own, "dp", 2)
    for k in range(1, nc - 1):
        state = attn_fwd(scalars(k), 0, qT, kv_far[k - 1], tab, state, False, R, nt)
    os = []
    for h0, h1 in ((0, H - 1), (H - 1, H)):
        *state, o0, o1, o2, o3 = attn_fwd(
            scalars(nc - 1), h0, qT, kv_far[-1][h0:h1], tab, state, True, R, nt
        )
        if h0 == 0:
            state, far, p2, o0, o1, o2, o3, kv_far[-1][-1] = bar(
                (state, far, p2, o0, o1, o2, o3, kv_far[-1][-1])
            )
            p2x = flip(p2, "dp", 2)
            ps = [own, flip(own, "dp", 1), far, flip(far, "dp", 1)]
        else:
            o0, ps, p1, p1x, os = bar((o0, ps, p1, p1x, os))
            p1 = (p1, flip(p1, "dp", 1), p1x, flip(p1x, "dp", 1))
        os += spread([o0, o1, o2, o3])
    o32, lse = state
    os, p2x = bar((os, p2x))
    p2 = (p2, flip(p2, "dp", 1), p2x, flip(p2x, "dp", 1))
    w0 = after(small[0], *os)[:dd]
    p3a = gather_weights(w0[: dd // 2])
    a, du, h2, da, y1, dy1, sm2, dbin, *dos = mlp1(sc, x2, g2, vecs, os, ps, p1, p2)
    dos = spread(dos)
    *gws, out = mlp2(sc, g2, vecs, h2, da, y1, a, du, os, p2)

    add = lambda *v: sum(z.astype(f32) for z in v).astype(bf16)
    out, dos, p3a = bar((out, dos, p3a))
    core = [flip(gws[1], "dp", 1), flip(gws[3], "dp", 1)]
    halves = nc == 2
    part = lambda v, i: lax.dynamic_index_in_dim(
        v.reshape(v.shape[:-2] + (2, dd // 2, v.shape[-1])), i, v.ndim - 2, keepdims=False
    )
    dtab = None
    dqs, backs = [], []
    for h0, h1 in ((0, 1), (1, H)):
        back, dq = None, None
        for k in range(1, nc):
            dq, dkv, dtab = attn_bwd(
                scalars(k), h0, qT, kv_far[k - 1][h0:h1], tab, dos, o32, lse, dq, dtab, None, R
            )
            dq = (dq, 0)
            dkv = shift(dkv, "ctx", -k)
            back = dkv if back is None else add(back, dkv)
        dqs += [(dq[0], i) for i in range(h1 - h0)]
        backs += [(back, i) for i in range(h1 - h0)]
        if h0 == 0:
            dtab, core = bar((dtab, core))
            pair = [add(gws[0], core[0]), add(gws[2], core[1])]
            if halves:
                xa = flip(pair[1][: nt // 2], "dp", 2)
                low = jnp.concatenate([z[nt // 2 :] for z in pair])
                yb = flip(part(low, 1 - pos), "ctx", 1)
            else:
                xa = flip(pair[1], "dp", 2)
    block_out = lax.all_gather(out.reshape(1, N, D), "tensor", axis=1, tiled=True)
    if halves:
        dtab, xa, yb = bar((dtab, xa, yb))
        va = add(pair[0][: nt // 2], xa)
        vb = add(part(low, pos), yb)
        ya = flip(part(va, 1 - pos), "ctx", 1)
        xb = flip(vb[nt // 2 :], "dp", 2)
    else:
        dtab, xa = bar((dtab, xa))
        v = add(pair[0], xa)
    dx, dxr = [], []
    for h in range(H):
        *d, dtab = attn_bwd(
            sc, h, qT, kvs[h : h + 1], tab, dos, o32, lse, dqs[h], dtab, backs[h], R
        )
        dx += d
        if h == 0 and halves:
            dtab, xb = bar((dtab, xb))
        if h == 0:
            p3b = gather_weights(after(w0, block_out, dtab)[dd // 2 :])
        if h == 1:
            if halves:
                dtab, ya = bar((dtab, ya))
                v = jnp.concatenate([add(part(va, pos), ya), add(vb[: nt // 2], xb)])
            dtab, dxr, v, block_out = bar((dtab, dxr, v, block_out))
        if h == 2:
            dtab, dxr, xh1 = bar((dtab, dxr, xh1))
        dxr = dxr + spread(d)
    v = after(v, dtab)
    gsum = lax.psum_scatter(v, "tensor", scatter_dimension=0)

    keepq, sendq, bq, sm1 = gqkv(sc, xh1, vecs, wT, dx, nt)

    tid = jnp.arange(nt)
    bq = bq[:, :, 0].reshape(H, 3, HD)
    bq = jnp.stack([bq[:, 0], bq[:, 2]]).reshape(1, 2 * E)
    bq = jnp.where(tid[:, None] == me, bq, 0.0)
    flat = jnp.concatenate(
        [z.reshape(-1, 256) for z in (sm2[:4], sm1[:2], dbin, bq)] + [dtab]
    )
    flat, sendq, dxr[-3] = bar((flat, sendq, dxr[-3]))
    flats = [flat] + [flip(flat, "tensor", k) for k in range(1, nt)]

    gin = dh1(sc, x2, dy1, vecs, dxr, p3a, p3b)
    gin, sendq, flats = bar((gin, sendq, flats))
    gall = lax.all_gather(gin, "tensor", axis=0, tiled=True)
    while len(flats) > 1:
        flats = [flats[i] + flats[i + 1] for i in range(0, len(flats), 2)]
    flat = flats[0] + flip(flats[0], "dp", 1)
    flat = flat + flip(flat, "dp", 2)
    flat = flat + flip(flat, "ctx", 1) if nc == 2 else lax.psum(flat, "ctx")

    coreq = flip(sendq, "dp", 1)
    if halves:
        gsum = gsum.astype(bf16)
        other = flip(gsum, "ctx", 1)
        gmine = jnp.concatenate(
            [jnp.where(pos == 0, gsum, other), jnp.where(pos == 0, other, gsum)], 0
        ).astype(f32)
    else:
        gmine = total_ctx(gsum)
    g_in = gmine[:, :ft]
    g_out = gmine[:, ft : 2 * ft].T
    g_proj = gmine[:, 2 * ft :].T
    farq = flip(add(keepq[1], coreq[1]), "dp", 2)
    gq = total_ctx(add(keepq[0], coreq[0], farq))
    g_qkv = gq.reshape(dd, H, 3, HD).transpose(0, 2, 1, 3).reshape(dd, 3, E)

    vec = flat[: 6 * D // 256].reshape(6, 4, dd)
    vec = lax.dynamic_index_in_dim(vec, dp, 1, keepdims=False)
    at = 6 * D // 256
    gb = flat[at : at + nt * ft // 256].reshape(nt, ft // 64, 4, 16)
    gb = lax.dynamic_index_in_dim(gb, me, 0, keepdims=False)
    gb = lax.dynamic_index_in_dim(gb, dp, 1, keepdims=False)
    at += nt * ft // 256
    gbq = flat[at : at + nt * 2 * E // 256].reshape(nt, 2, H, 4, 16)
    gbq = lax.dynamic_index_in_dim(gbq, me, 0, keepdims=False)
    gbq = lax.dynamic_index_in_dim(gbq, dp, 2, keepdims=False)
    at += nt * 2 * E // 256
    gtab = lax.dynamic_index_in_dim(flat[at:].reshape(4, 16, 2, 128), dp, 0, keepdims=False)
    gtab_h, gtab_w = gtab[:, 0, :L][:, ::-1].T, gtab[:, 1, :L].T
    block_out = copied(sc, after(block_out, gin).reshape(T, D), bf16)
    gall, vec, block_out, g_qkv, gbq, gtab_h, gtab_w, gb, g_in, g_out, g_proj = bar(
        (gall, vec, block_out, g_qkv, gbq, gtab_h, gtab_w, gb, g_in, g_out, g_proj)
    )
    grad_input = gall.astype(f32).reshape(1, T, D)
    return (
        block_out.reshape(1, T, D),
        grad_input,
        vec[4],
        vec[5],
        g_qkv,
        gbq,
        gtab_h,
        gtab_w,
        g_proj,
        vec[2],
        vec[0],
        vec[1],
        g_in,
        gb,
        g_out,
        vec[3],
    )


def solution(mesh):
    placed = (
        P("dp", "ctx", None),
        P("dp", "ctx", None),
        P("dp"),
        P("dp"),
        P("dp", None, "tensor"),
        P(None, "tensor", "dp"),
        P(None, "dp"),
        P(None, "dp"),
        P("tensor", "dp"),
        P("dp"),
        P("dp"),
        P("dp"),
        P("dp", "tensor"),
        P("tensor", "dp"),
        P("tensor", "dp"),
        P("dp"),
    )
    return jax.shard_map(
        per_device,
        mesh=mesh,
        in_specs=placed,
        out_specs=(placed[0], placed[0]) + placed[2:],
        check_vma=False,
    )
```
